32 devices in a mesh: groups: 2 (over y), row: 4 (over z), col: 4 (over x, core).
Axes of the slice: x: 2, y: 2, z: 4, core: 2. Of those that a mesh axis runs over, the one named last changes fastest.
Arguments:
- act_train: bfloat16 [1024, 8192], P('groups', 'row'), parts along dimension 0, may hold values from -6 to 6
- act_query: bfloat16 [256, 8192], P('groups', 'row'), parts along dimension 0, may hold values from -6 to 6
- grad_train: bfloat16 [1024, 28672], P('groups', 'col'), parts along dimension 0, may hold values from -6 to 6
- grad_query: bfloat16 [256, 28672], P('groups', 'col'), parts along dimension 0, may hold values from -6 to 6
- basis_in: bfloat16 [16384, 8192], P(('groups', 'row'), 'col'), parts along dimension 0, may hold values from -0.0625 to 0.0625
- basis_out: bfloat16 [57344, 4096], P(('groups', 'col'), 'row'), parts along dimension 0, may hold values from -0.03125 to 0.03125
- correction: float32 [8192, 8192], P(('groups', 'row'), 'col'), parts along dimension 0, may hold values from 0.1 to 2
Outputs:
- scores: float32 [16, 512], P('groups', 'row'), parts along dimension 0
The draws below stay inside these ranges and needn't reach their ends.
There are 2 independent parts, one for each index of `groups`. The reference program is written for one: setup_inputs(seed, part) draws one part's arguments, and reference() takes and returns one part's arrays. A program takes and returns all parts, laid end to end along the dimension named above; each array names one. Nothing has to cross between parts.
All inputs are finite; a program needn't handle non-finite values.
Results may differ from the reference program's by a relative error of at most 0.0054.
Values may be sent and summed in bfloat16 or wider, within the bound.
No kernel may reach another device: no remote copies, remote signals or barrier semaphores. Data moves between devices by JAX's collectives and lax.ppermute only.
A program may use at most 192 MiB of HBM per device.

```python
import math
import jax
import jax.numpy as jnp
from jax import lax

I = 8192
OFULL = 28672
O = 4096
NQ = 8
LQ = 16
TRAIN_TOK = 512
QROWS = 128


def level_of(key, dims, cuts, least, high):
    level, own = 1.0, jax.random.fold_in(key, 6)
    for dim, shards_of in cuts:
        heights = jnp.exp(jax.random.uniform(jax.random.fold_in(own, dim), (shards_of,), jnp.float32, least / len(cuts), high / len(cuts)))
        level = level * jnp.repeat(heights, dims[dim] // shards_of).reshape([-1 if axis == dim else 1 for axis in range(len(dims))])
    return level


def centred(key, extent, spread, most, split=(), dtype=jnp.bfloat16):
    drawn = jax.random.normal(key, extent, jnp.float32) * spread
    if len(split) > 0:
        drawn = level_of(key, extent, split, -0.22, 0.18) * drawn
    return jnp.clip(drawn, min=-most, max=most).astype(dtype)


def setup_inputs(seed: int = 0, part: int = 0) -> dict:
    keys = jax.random.split(jax.random.key(seed), 8)
    own_keys = jax.random.split(jax.random.fold_in(keys[7], part), 8)
    act_train = centred(own_keys[0], (TRAIN_TOK, I), 1.0, 6.0, ((1, 4),))
    act_query = centred(own_keys[1], (QROWS, I), 1.0, 6.0, ((1, 4),))
    grad_train = centred(own_keys[2], (TRAIN_TOK, OFULL), 1.0, 6.0, ((1, 4),))
    grad_query = centred(own_keys[3], (QROWS, OFULL), 1.0, 6.0, ((1, 4),))
    basis_in = centred(own_keys[4], (I, I), I ** -0.5, 0.0625, ((0, 4), (1, 4)))
    basis_out = centred(own_keys[5], (OFULL, O), OFULL ** -0.5, 0.03125, ((0, 4), (1, 4)))
    correction = jnp.clip(jnp.exp(math.log(2.0) - 2.9957323 * jax.random.uniform(own_keys[6], (O, I), jnp.float32) ** level_of(own_keys[6], (O, I), ((0, 4), (1, 4)), -0.2, 0.2)), 0.1, 2.0)
    return {"act_train": act_train, "act_query": act_query, "grad_train": grad_train, "grad_query": grad_query, "basis_in": basis_in, "basis_out": basis_out, "correction": correction}


def reference(act_train, act_query, grad_train, grad_query, basis_in, basis_out, correction):
    rot_at = jnp.dot(act_train, basis_in, preferred_element_type=jnp.float32).astype(jnp.bfloat16)
    rot_aq = jnp.dot(act_query, basis_in, preferred_element_type=jnp.float32).astype(jnp.bfloat16)
    rot_gt = jnp.dot(grad_train, basis_out, preferred_element_type=jnp.float32).astype(jnp.bfloat16)
    rot_gq = jnp.dot(grad_query, basis_out, preferred_element_type=jnp.float32).astype(jnp.bfloat16)
    norm_scale = (O * I * LQ) ** -0.5
    query_out = rot_gq.reshape(NQ, LQ, O)
    query_in = rot_aq.reshape(NQ, LQ, I)
    grad_wide = rot_gt.astype(jnp.float32)

    def one_query(members):
        g_part, a_part = members
        products = jnp.dot(g_part.T, a_part, preferred_element_type=jnp.float32)
        divided = (products / correction).astype(jnp.bfloat16)
        mapped = jnp.dot(rot_at, divided.T, preferred_element_type=jnp.float32)
        return jnp.sum(mapped * grad_wide, axis=1) * norm_scale

    return lax.map(one_query, (query_out, query_in))
```

```python
import jax
import jax.numpy as jnp
from jax import lax
from jax.sharding import PartitionSpec as P

I = 8192
O = 4096
NQ = 8
LQ = 16
CHUNKS = 4
F32 = jnp.float32
BF16 = jnp.bfloat16


def line_sum(partial, axis):
    n = lax.axis_size(axis)
    half = n // 2
    me = lax.axis_index(axis)
    if n % 2:
        return lax.psum(partial, axis).astype(BF16)
    acc = partial
    for s in range(half - 1):
        pairs = [(s, s + 1), (n - 1 - s, n - 2 - s)]
        acc = acc + lax.ppermute(acc.astype(BF16), axis, pairs).astype(F32)
    got = lax.ppermute(acc.astype(BF16), axis, [(half - 1, half), (half, half - 1)])
    total = (acc + got.astype(F32)).astype(BF16)
    for s in range(half - 2, -1, -1):
        pairs = [(s + 1, s), (n - 2 - s, n - 1 - s)]
        got = lax.ppermute(total, axis, pairs)
        total = jnp.where((me == s) | (me == n - 1 - s), got, total)
    return total


def cube_sum(partial, axis):
    n = lax.axis_size(axis)
    if n & (n - 1) or n < 2:
        return lax.psum(partial, axis).astype(BF16)
    me = lax.axis_index(axis)
    odd = me % 2 == 1
    rows = partial.shape[0] // 2
    low, high = partial[:rows], partial[rows:]
    flip = [(d, d ^ 1) for d in range(n)]
    acc = jnp.where(odd, high, low) + lax.ppermute(jnp.where(odd, low, high), axis, flip)
    bit = 2
    while bit < n:
        acc = acc + lax.ppermute(acc, axis, [(d, d ^ bit) for d in range(n)])
        bit *= 2
    mine = acc.astype(BF16)
    other = lax.ppermute(mine, axis, flip)
    return jnp.concatenate([jnp.where(odd, other, mine), jnp.where(odd, mine, other)], axis=0)


def owned_sum(partial, axis):
    n = lax.axis_size(axis)
    me = lax.axis_index(axis)
    total = lax.dynamic_index_in_dim(partial, me, 0, keepdims=False)
    for step in range(1, n):
        block = lax.dynamic_index_in_dim(partial, (me + step) % n, 0, keepdims=False)
        total = total + lax.ppermute(block, axis, [(d, (d + step) % n) for d in range(n)])
    return total


def shared_sum(partial, axis):
    n = lax.axis_size(axis)
    total = partial
    for step in range(1, n):
        total = total + lax.ppermute(partial, axis, [(d, (d + step) % n) for d in range(n)])
    return total


def on_device(act_train, act_query, grad_train, grad_query, basis_in, basis_out, correction):
    norm_scale = (O * I * LQ) ** (-0.5)
    tokens = act_train.shape[0]
    chunk = tokens // CHUNKS
    rot_aq = line_sum(jnp.dot(act_query, basis_in, preferred_element_type=F32), "row")
    rot_at = [
        line_sum(
            jnp.dot(act_train[k * chunk : (k + 1) * chunk], basis_in, preferred_element_type=F32),
            "row",
        )
        for k in range(CHUNKS)
    ]
    rot_gq = cube_sum(jnp.dot(grad_query, basis_out, preferred_element_type=F32), "col")
    rot_gt = cube_sum(jnp.dot(grad_train, basis_out, preferred_element_type=F32), "col")
    query_out = rot_gq.reshape(NQ, -1, rot_gq.shape[1])
    query_in = rot_aq.reshape(NQ, -1, rot_aq.shape[1])
    products = jnp.einsum("qso,qsi->qoi", query_out, query_in, preferred_element_type=F32)
    divided = (products / correction[None]).astype(BF16)
    values = []
    for k in range(CHUNKS):
        mapped = jnp.einsum("ti,qoi->qto", rot_at[k], divided, preferred_element_type=F32)
        wide = rot_gt[k * chunk : (k + 1) * chunk].astype(F32)
        values.append(jnp.sum(mapped * wide[None], axis=2) * norm_scale)
    partial = jnp.concatenate(values, axis=1)
    n_row = lax.axis_size("row")
    blocks = partial.reshape(NQ, n_row, tokens // n_row).transpose(1, 0, 2)
    return shared_sum(owned_sum(blocks, "row"), "col")


def solution(mesh):
    in_specs = (
        P("groups", "row"),
        P("groups", "row"),
        P("groups", "col"),
        P("groups", "col"),
        P(("groups", "row"), "col"),
        P(("groups", "col"), "row"),
        P(("groups", "row"), "col"),
    )
    out_specs = P("groups", "row")
    return jax.shard_map(
        on_device, mesh=mesh, in_specs=in_specs, out_specs=out_specs, check_vma=False
    )
```

```python
import functools

import jax
import jax.numpy as jnp
from jax import lax
from jax.experimental import pallas as pl
from jax.experimental.pallas import tpu as pltpu
from jax.sharding import PartitionSpec as P

I = 8192
O = 4096
NQ = 8
LQ = 16
LANES = 128
CHUNKS = 8
F32 = jnp.float32
BF16 = jnp.bfloat16
MIB = 1 << 20


def largest_divisor(size, choices):
    for choice in choices:
        if size % choice == 0:
            return choice
    return size


def in_kernel(train_ref, query_ref, basis_ref, out_ref):
    tokens = train_ref.shape[0]
    rows = jnp.concatenate([train_ref[...], query_ref[...]], axis=0)
    out_ref[...] = jnp.dot(rows, basis_ref[...], preferred_element_type=F32)


def in_part(act_train, act_query, basis_in, first, count, width):
    tokens, depth = act_train.shape
    queries = act_query.shape[0]
    rows = tokens + queries
    return pl.pallas_call(
        in_kernel,
        grid=(count,),
        in_specs=[
            pl.BlockSpec((tokens, depth), lambda j: (0, 0)),
            pl.BlockSpec((queries, depth), lambda j: (0, 0)),
            pl.BlockSpec((depth, width), lambda j: (0, first + j)),
        ],
        out_specs=pl.BlockSpec((rows, width), lambda j: (0, j)),
        out_shape=jax.ShapeDtypeStruct((rows, count * width), F32),
        compiler_params=pltpu.CompilerParams(vmem_limit_bytes=24 * MIB),
        cost_estimate=pl.CostEstimate(
            flops=2 * rows * depth * width * count,
            bytes_accessed=2 * rows * depth + count * width * (2 * depth + 4 * rows),
            transcendentals=0,
        ),
    )(act_train, act_query, basis_in)


def out_kernel(odd_ref, train_ref, query_ref, basis_ref, keep_ref, give_ref, acc_ref):
    step = pl.program_id(0)
    half = keep_ref.shape[0]
    rows = jnp.concatenate([train_ref[...], query_ref[...]], axis=0)
    part = jnp.dot(rows, basis_ref[...], preferred_element_type=F32)

    @pl.when(step == 0)
    def _():
        acc_ref[...] = part

    @pl.when(step > 0)
    def _():
        acc_ref[...] += part

    @pl.when(step == pl.num_programs(0) - 1)
    def _():
        odd = odd_ref[0]
        keep_ref[...] = acc_ref[pl.ds(pl.multiple_of(odd * half, 8), half), :]
        give_ref[...] = acc_ref[pl.ds(pl.multiple_of((1 - odd) * half, 8), half), :]


def out_part(odd, grad_train, grad_query, basis_out):
    tokens, depth = grad_train.shape
    queries = grad_query.shape[0]
    width = basis_out.shape[1]
    rows = tokens + queries
    block = largest_divisor(depth, (1024, 896, 512, 256, 128))
    half = jax.ShapeDtypeStruct((rows // 2, width), F32)
    return pl.pallas_call(
        out_kernel,
        grid_spec=pltpu.PrefetchScalarGridSpec(
            num_scalar_prefetch=1,
            grid=(depth // block,),
            in_specs=[
                pl.BlockSpec((tokens, block), lambda j, odd: (0, j)),
                pl.BlockSpec((queries, block), lambda j, odd: (0, j)),
                pl.BlockSpec((block, width), lambda j, odd: (j, 0)),
            ],
            out_specs=[
                pl.BlockSpec((rows // 2, width), lambda j, odd: (0, 0)),
                pl.BlockSpec((rows // 2, width), lambda j, odd: (0, 0)),
            ],
            scratch_shapes=[pltpu.VMEM((rows, width), F32)],
        ),
        out_shape=[half, half],
        compiler_params=pltpu.CompilerParams(vmem_limit_bytes=32 * MIB),
        cost_estimate=pl.CostEstimate(
            flops=2 * rows * depth * width,
            bytes_accessed=2 * depth * (rows + width) + 4 * rows * width,
            transcendentals=0,
        ),
    )(odd.reshape(1).astype(jnp.int32), grad_train, grad_query, basis_out)


def score_kernel(gt_ref, gq_ref, corr_ref, tot_ref, out_ref, quot_ref, inv_ref, wide_ref):
    tokens = gt_ref.shape[0]
    queries = gq_ref.shape[1]
    width = tot_ref.shape[1]
    inv_ref[...] = 1.0 / corr_ref[...]
    wide_ref[...] = tot_ref[:tokens, :].astype(F32)
    owner = lax.broadcasted_iota(jnp.int32, (queries, width), 0) // LQ
    lane = lax.broadcasted_iota(jnp.int32, (tokens, LANES), 1)

    def quotient(q):
        own = jnp.where(owner == q, tot_ref[tokens:, :].astype(F32), 0.0).astype(BF16)
        products = jnp.dot(gq_ref[...], own, preferred_element_type=F32)
        quot_ref[q % 2] = (products * inv_ref[...]).astype(BF16)

    quotient(0)
    result = jnp.zeros((tokens, LANES), F32)
    for q in range(NQ):
        if q + 1 < NQ:
            quotient(q + 1)
        mapped = jnp.dot(gt_ref[...], quot_ref[q % 2], preferred_element_type=F32)
        scaled = mapped * wide_ref[...]
        folded = scaled[:, :LANES]
        for part in range(1, width // LANES):
            folded = folded + scaled[:, part * LANES : (part + 1) * LANES]
        result = jnp.where(lane == q, jnp.sum(folded, axis=1, keepdims=True), result)
    out_ref[...] = result


def score_part(rot_gt, rot_gq_t, correction, total, k):
    tokens, outs = rot_gt.shape
    rows, width = total.shape
    queries = rot_gq_t.shape[1]
    return pl.pallas_call(
        score_kernel,
        grid=(1,),
        in_specs=[
            pl.BlockSpec((tokens, outs), lambda j: (0, 0)),
            pl.BlockSpec((outs, queries), lambda j: (0, 0)),
            pl.BlockSpec((outs, width), lambda j: (0, k)),
            pl.BlockSpec((rows, width), lambda j: (0, 0)),
        ],
        out_specs=pl.BlockSpec((tokens, LANES), lambda j: (0, 0)),
        out_shape=jax.ShapeDtypeStruct((tokens, LANES), F32),
        scratch_shapes=[
            pltpu.VMEM((2, outs, width), BF16),
            pltpu.VMEM((outs, width), F32),
            pltpu.VMEM((tokens, width), F32),
        ],
        compiler_params=pltpu.CompilerParams(vmem_limit_bytes=24 * MIB),
        cost_estimate=pl.CostEstimate(
            flops=2 * NQ * outs * width * (tokens + queries),
            bytes_accessed=2 * tokens * outs + 4 * outs * width + 2 * rows * width,
            transcendentals=0,
        ),
    )(rot_gt, rot_gq_t, correction, total)


def line_sum(partial, axis):
    n = lax.axis_size(axis)
    half = n // 2
    me = lax.axis_index(axis)
    if n % 2:
        return lax.psum(partial, axis).astype(BF16)
    acc = partial
    for s in range(half - 1):
        pairs = [(s, s + 1), (n - 1 - s, n - 2 - s)]
        acc = acc + lax.ppermute(acc.astype(BF16), axis, pairs).astype(F32)
    got = lax.ppermute(acc.astype(BF16), axis, [(half - 1, half), (half, half - 1)])
    total = (acc + got.astype(F32)).astype(BF16)
    for s in range(half - 2, -1, -1):
        pairs = [(s + 1, s), (n - 2 - s, n - 1 - s)]
        got = lax.ppermute(total, axis, pairs)
        total = jnp.where((me == s) | (me == n - 1 - s), got, total)
    return total


def line_sums(parts, axis):
    if lax.axis_size(axis) != 4:
        return [line_sum(part, axis) for part in parts]
    me = lax.axis_index(axis)
    end = (me == 0) | (me == 3)
    outer = [(0, 1), (1, 0), (2, 3), (3, 2)]
    inner = [(0, 0), (1, 2), (2, 1), (3, 3)]
    count = len(parts)
    lag = 3
    sent, got = {}, {}

    def swap(j, payload):
        sent[j] = payload
        got[j] = lax.ppermute(payload, axis, outer)

    for j in range(min(lag, count)):
        swap(j, parts[j].astype(BF16))
    for k in range(count):
        acc = parts[k] + got[k].astype(F32)
        other = lax.ppermute(acc.astype(BF16), axis, inner)
        total = acc + other.astype(F32)
        if k + lag < count:
            total = jnp.where(end, parts[k + lag], total)
        swap(k + lag, total.astype(BF16))
    return [jnp.where(end, got[k + lag], sent[k + lag]) for k in range(count)]


def cube_sum(keep, give, axis):
    n = lax.axis_size(axis)
    odd = lax.axis_index(axis) % 2 == 1
    flip = [(d, d ^ 1) for d in range(n)]
    acc = keep + lax.ppermute(give, axis, flip)
    bit = 2
    while bit < n:
        got = lax.ppermute(acc.astype(BF16), axis, [(d, d ^ bit) for d in range(n)])
        acc = acc + got.astype(F32)
        bit *= 2
    mine = acc.astype(BF16)
    other = lax.ppermute(mine, axis, flip)
    return jnp.concatenate([jnp.where(odd, other, mine), jnp.where(odd, mine, other)], axis=0)


def owned_sum(partial, axis):
    n = lax.axis_size(axis)
    me = lax.axis_index(axis)
    total = lax.dynamic_index_in_dim(partial, me, 0, keepdims=False)
    for step in range(1, n):
        block = lax.dynamic_index_in_dim(partial, (me + step) % n, 0, keepdims=False)
        total = total + lax.ppermute(block, axis, [(d, (d + step) % n) for d in range(n)])
    return total


def shared_sum(partial, axis):
    n = lax.axis_size(axis)
    total = partial
    for step in range(1, n):
        total = total + lax.ppermute(partial, axis, [(d, (d + step) % n) for d in range(n)])
    return total


def on_device(act_train, act_query, grad_train, grad_query, basis_in, basis_out, correction):
    norm_scale = (O * I * LQ) ** (-0.5)
    tokens = act_train.shape[0]
    width = basis_in.shape[1] // CHUNKS
    first = in_part(act_train, act_query, basis_in, 0, 1, width)
    rest = in_part(act_train, act_query, basis_in, 1, CHUNKS - 1, width)
    parts = [first] + [rest[:, k * width : (k + 1) * width] for k in range(CHUNKS - 1)]
    keep, give = out_part(lax.axis_index("col") % 2, grad_train, grad_query, basis_out)
    outs = cube_sum(keep, give, "col")
    rot_gt = outs[:tokens]
    rot_gq_t = outs[tokens:].T
    totals = line_sums(parts, "row")
    partial = None
    for k in range(CHUNKS):
        value = score_part(rot_gt, rot_gq_t, correction, totals[k], k)
        partial = value if partial is None else partial + value
    n_row = lax.axis_size("row")
    scaled = partial[:, :NQ].T * norm_scale
    blocks = scaled.reshape(NQ, n_row, tokens // n_row).transpose(1, 0, 2)
    return shared_sum(owned_sum(blocks, "row"), "col")


def solution(mesh):
    in_specs = (
        P("groups", "row"),
        P("groups", "row"),
        P("groups", "col"),
        P("groups", "col"),
        P(("groups", "row"), "col"),
        P(("groups", "col"), "row"),
        P(("groups", "row"), "col"),
    )
    out_specs = P("groups", "row")
    return jax.shard_map(
        on_device, mesh=mesh, in_specs=in_specs, out_specs=out_specs, check_vma=False
    )
```

```python
import functools

import jax
import jax.numpy as jnp
from jax import lax
from jax.experimental import pallas as pl
from jax.experimental.pallas import tpu as pltpu
from jax.sharding import PartitionSpec as P

I = 8192
O = 4096
NQ = 8
LQ = 16
LANES = 128
CHUNKS = 8
LAG = 3
F32 = jnp.float32
BF16 = jnp.bfloat16
MIB = 1 << 20

VMEM_SPEC = pl.BlockSpec(memory_space=pltpu.VMEM)
SMEM_SPEC = pl.BlockSpec(memory_space=pltpu.SMEM)
ANY_SPEC = pl.BlockSpec(memory_space=pl.ANY)


def shape_of(rows, width, dtype):
    return jax.ShapeDtypeStruct((rows, width), dtype)


def chunk_list(size):
    tiles = size // LANES
    count = min(CHUNKS, tiles)
    chunks, first = [], 0
    for k in range(count):
        width = LANES * (tiles // count + (1 if k < tiles % count else 0))
        chunks.append((first, width))
        first += width
    return chunks


def largest_divisor(size, choices):
    for choice in choices:
        if size % choice == 0:
            return choice
    return size


def cost(flops, bytes_accessed):
    return pl.CostEstimate(flops=flops, bytes_accessed=bytes_accessed, transcendentals=0)


def in_hbm(x):
    return pltpu.with_memory_space_constraint(x, pltpu.HBM)


def in_kernel(chunks, narrow, train_ref, query_ref, basis_ref, prev_ref, *refs):
    wide_refs = refs[: len(chunks)]
    narrow_refs = refs[len(chunks) : len(chunks) + narrow]
    slots, sems = refs[len(chunks) + narrow :]

    def fetch(j):
        first, width = chunks[j]
        return pltpu.make_async_copy(
            basis_ref.at[:, pl.ds(first, width)], slots.at[j % 2, :, pl.ds(0, width)], sems.at[j % 2]
        )

    fetch(0).start()
    rows = jnp.concatenate([train_ref[...], query_ref[...]], axis=0)
    for j, (first, width) in enumerate(chunks):
        if j + 1 < len(chunks):
            fetch(j + 1).start()
        fetch(j).wait()
        part = jnp.dot(rows, slots[j % 2, :, :width], preferred_element_type=F32)
        wide_refs[j][...] = part
        if j < narrow:
            narrow_refs[j][...] = part.astype(BF16)


def in_part(act_train, act_query, basis_in, prev, chunks, narrow):
    tokens, depth = act_train.shape
    rows = tokens + act_query.shape[0]
    most = max(width for _, width in chunks)
    total = sum(width for _, width in chunks)
    out = pl.pallas_call(
        functools.partial(in_kernel, chunks, narrow),
        in_specs=[VMEM_SPEC, VMEM_SPEC, ANY_SPEC, ANY_SPEC],
        out_specs=[VMEM_SPEC] * (len(chunks) + narrow),
        out_shape=[shape_of(rows, width, F32) for _, width in chunks]
        + [shape_of(rows, width, BF16) for _, width in chunks[:narrow]],
        scratch_shapes=[pltpu.VMEM((2, depth, most), BF16), pltpu.SemaphoreType.DMA((2,))],
        compiler_params=pltpu.CompilerParams(vmem_limit_bytes=24 * MIB),
        cost_estimate=cost(2 * rows * depth * total, 2 * depth * total),
    )(act_train, act_query, in_hbm(basis_in), prev)
    return list(out[: len(chunks)]), list(out[len(chunks) :])


def out_kernel(train_ref, query_ref, basis_ref, flags_ref, prev_ref, keep_ref, give_ref, acc_ref):
    step = pl.program_id(0)
    half = keep_ref.shape[0]
    rows = jnp.concatenate([train_ref[...], query_ref[...]], axis=0)

    @pl.when(step == 0)
    def _():
        acc_ref[...] = jnp.dot(rows, basis_ref[...], preferred_element_type=F32)

    @pl.when(step > 0)
    def _():
        acc_ref[...] += jnp.dot(rows, basis_ref[...], preferred_element_type=F32)

    @pl.when(step == pl.num_programs(0) - 1)
    def _():
        odd = flags_ref[1]
        keep_ref[...] = acc_ref[pl.ds(pl.multiple_of(odd * half, 16), half), :]
        give_ref[...] = acc_ref[pl.ds(pl.multiple_of((1 - odd) * half, 16), half), :]


def out_part(flags, grad_train, grad_query, basis_out, prev):
    tokens, depth = grad_train.shape
    queries = grad_query.shape[0]
    width = basis_out.shape[1]
    rows = tokens + queries
    block = largest_divisor(depth, (1792, 1024, 512, 256, 128))
    return pl.pallas_call(
        out_kernel,
        grid=(depth // block,),
        in_specs=[
            pl.BlockSpec((tokens, block), lambda j: (0, j)),
            pl.BlockSpec((queries, block), lambda j: (0, j)),
            pl.BlockSpec((block, width), lambda j: (j, 0)),
            SMEM_SPEC,
            ANY_SPEC,
        ],
        out_specs=[
            pl.BlockSpec((rows // 2, width), lambda j: (0, 0)),
            pl.BlockSpec((rows // 2, width), lambda j: (0, 0)),
        ],
        out_shape=[shape_of(rows // 2, width, F32)] * 2,
        scratch_shapes=[pltpu.VMEM((rows, width), F32)],
        compiler_params=pltpu.CompilerParams(vmem_limit_bytes=36 * MIB),
        cost_estimate=cost(2 * rows * depth * width, 2 * depth * (rows + width)),
    )(in_hbm(grad_train), in_hbm(grad_query), in_hbm(basis_out), flags, prev)


def add_kernel(keep_ref, got_ref, prev_ref, wide_ref, narrow_ref):
    total = keep_ref[...] + got_ref[...].astype(F32)
    wide_ref[...] = total
    narrow_ref[...] = total.astype(BF16)


def add_part(keep, got, prev):
    rows, width = keep.shape
    return pl.pallas_call(
        add_kernel,
        in_specs=[VMEM_SPEC, VMEM_SPEC, ANY_SPEC],
        out_specs=[VMEM_SPEC, VMEM_SPEC],
        out_shape=[shape_of(rows, width, F32), shape_of(rows, width, BF16)],
        compiler_params=pltpu.CompilerParams(vmem_limit_bytes=12 * MIB),
        cost_estimate=cost(rows * width, 14 * rows * width),
    )(keep, got, prev)


def join_kernel(tokens, mine_ref, other_ref, flags_ref, prev_ref, gt_ref, gq_ref):
    odd = flags_ref[1]
    mine, other = mine_ref[...].astype(F32), other_ref[...].astype(F32)
    low = jnp.where(odd == 1, other, mine).astype(BF16)
    high = jnp.where(odd == 1, mine, other).astype(BF16)
    rows = jnp.concatenate([low, high], axis=0)
    gt_ref[...] = rows[:tokens]
    gq_ref[...] = rows[tokens:].astype(F32).T.astype(BF16)


def join_part(flags, mine, other, prev, tokens):
    half, width = mine.shape
    queries = 2 * half - tokens
    return pl.pallas_call(
        functools.partial(join_kernel, tokens),
        in_specs=[VMEM_SPEC, VMEM_SPEC, SMEM_SPEC, ANY_SPEC],
        out_specs=[VMEM_SPEC, VMEM_SPEC],
        out_shape=[shape_of(tokens, width, BF16), shape_of(width, queries, BF16)],
        compiler_params=pltpu.CompilerParams(vmem_limit_bytes=16 * MIB),
        cost_estimate=cost(4 * half * width, 8 * half * width),
    )(mine, other, flags, prev)


def slot_kernel(has_acc, has_pay, has_part, width, flags_ref, *refs):
    refs = list(refs)
    if has_acc:
        part_ref, got_x_ref = refs.pop(0), refs.pop(0)
    if has_pay:
        old_ref, got_y_ref = refs.pop(0), refs.pop(0)
        if has_part:
            next_ref = refs.pop(0)
    refs.pop(0)
    if has_acc:
        wide_ref, narrow_ref = refs.pop(0), refs.pop(0)
        acc = part_ref[...] + got_x_ref[:, : part_ref.shape[1]].astype(F32)
        wide_ref[...] = acc
        narrow_ref[...] = acc.astype(BF16)
    if has_pay:
        pay_ref = refs.pop(0)
        end = flags_ref[0] == 1
        total = old_ref[...] + got_y_ref[...].astype(F32)
        if not has_part:
            pay_ref[...] = total.astype(BF16)
        else:
            own, theirs = next_ref.shape[1], old_ref.shape[1]
            both = min(own, theirs)
            pay_ref[:, :both] = jnp.where(end, next_ref[:, :both], total[:, :both]).astype(BF16)
            if own > both:
                pay_ref[:, both:] = next_ref[:, both:].astype(BF16)
            elif theirs > both:
                pay_ref[:, both:] = total[:, both:].astype(BF16)


def slot_part(flags, part, got_x, old, got_y, following, prev):
    has_acc, has_pay, has_part = part is not None, old is not None, following is not None
    args = [flags]
    out_shape = []
    rows = (part if has_acc else old).shape[0]
    width = 0
    if has_acc:
        args += [part, got_x]
        out_shape += [shape_of(*part.shape, F32), shape_of(*part.shape, BF16)]
    if has_pay:
        args += [old, got_y]
        width = old.shape[1]
        if has_part:
            args.append(following)
            width = max(width, following.shape[1])
        out_shape.append(shape_of(rows, width, BF16))
    specs = [SMEM_SPEC] + [VMEM_SPEC] * (len(args) - 1) + [ANY_SPEC]
    args.append(prev)
    out = pl.pallas_call(
        functools.partial(slot_kernel, has_acc, has_pay, has_part, width),
        in_specs=specs,
        out_specs=[VMEM_SPEC] * len(out_shape),
        out_shape=out_shape,
        compiler_params=pltpu.CompilerParams(vmem_limit_bytes=12 * MIB),
        cost_estimate=cost(rows * 512, rows * 512 * 8),
    )(*args)
    out = list(out)
    acc = (out.pop(0), out.pop(0)) if has_acc else (None, None)
    return acc[0], acc[1], out.pop(0) if has_pay else None


def score_kernel(
    first, flags_ref, gt_ref, gq_ref, corr_ref, sent_ref, got_ref, prev_ref,
    out_ref, quot_ref, inv_ref, wide_ref, own_ref, sem
):
    tokens = gt_ref.shape[0]
    queries = gq_ref.shape[1]
    width = inv_ref.shape[1]
    fetch = pltpu.make_async_copy(corr_ref.at[:, pl.ds(first, width)], inv_ref, sem)
    fetch.start()
    end = flags_ref[0] == 1
    total = jnp.where(end, got_ref[:, :width].astype(F32), sent_ref[:, :width].astype(F32))
    wide_ref[...] = total[:tokens]
    own_ref[...] = total[tokens:]
    owner = lax.broadcasted_iota(jnp.int32, (queries, width), 0) // LQ
    lane = lax.broadcasted_iota(jnp.int32, (tokens, LANES), 1)
    fetch.wait()
    inv_ref[...] = 1.0 / inv_ref[...]

    def quotient(q):
        own = jnp.where(owner == q, own_ref[...], 0.0).astype(BF16)
        products = jnp.dot(gq_ref[...], own, preferred_element_type=F32)
        quot_ref[q % 2] = (products * inv_ref[...]).astype(BF16)

    quotient(0)
    result = jnp.zeros((tokens, LANES), F32)
    for q in range(NQ):
        if q + 1 < NQ:
            quotient(q + 1)
        mapped = jnp.dot(gt_ref[...], quot_ref[q % 2], preferred_element_type=F32)
        scaled = mapped * wide_ref[...]
        folded = scaled[:, :LANES]
        for part in range(1, width // LANES):
            folded = folded + scaled[:, part * LANES : (part + 1) * LANES]
        result = jnp.where(lane == q, jnp.sum(folded, axis=1, keepdims=True), result)
    out_ref[...] = result


def score_part(flags, rot_gt, rot_gq_t, correction, sent, got, chunk, prev):
    tokens, outs = rot_gt.shape
    first, width = chunk
    queries = rot_gq_t.shape[1]
    return pl.pallas_call(
        functools.partial(score_kernel, first),
        in_specs=[SMEM_SPEC, VMEM_SPEC, VMEM_SPEC, ANY_SPEC, VMEM_SPEC, VMEM_SPEC, ANY_SPEC],
        out_specs=VMEM_SPEC,
        out_shape=shape_of(tokens, LANES, F32),
        scratch_shapes=[
            pltpu.VMEM((2, outs, width), BF16),
            pltpu.VMEM((outs, width), F32),
            pltpu.VMEM((tokens, width), F32),
            pltpu.VMEM((queries, width), F32),
            pltpu.SemaphoreType.DMA,
        ],
        compiler_params=pltpu.CompilerParams(vmem_limit_bytes=24 * MIB),
        cost_estimate=cost(2 * NQ * outs * width * (tokens + queries), 4 * outs * width),
    )(flags, rot_gt, rot_gq_t, in_hbm(correction), sent, got, prev)


def line_sum(partial, axis):
    n = lax.axis_size(axis)
    half = n // 2
    me = lax.axis_index(axis)
    if n % 2:
        return lax.psum(partial, axis).astype(BF16)
    acc = partial
    for s in range(half - 1):
        pairs = [(s, s + 1), (n - 1 - s, n - 2 - s)]
        acc = acc + lax.ppermute(acc.astype(BF16), axis, pairs).astype(F32)
    got = lax.ppermute(acc.astype(BF16), axis, [(half - 1, half), (half, half - 1)])
    total = (acc + got.astype(F32)).astype(BF16)
    for s in range(half - 2, -1, -1):
        pairs = [(s + 1, s), (n - 2 - s, n - 1 - s)]
        got = lax.ppermute(total, axis, pairs)
        total = jnp.where((me == s) | (me == n - 1 - s), got, total)
    return total


def owned_sum(partial, axis):
    n = lax.axis_size(axis)
    me = lax.axis_index(axis)
    total = lax.dynamic_index_in_dim(partial, me, 0, keepdims=False)
    for step in range(1, n):
        block = lax.dynamic_index_in_dim(partial, (me + step) % n, 0, keepdims=False)
        total = total + lax.ppermute(block, axis, [(d, (d + step) % n) for d in range(n)])
    return total


def shared_sum(partial, axis):
    n = lax.axis_size(axis)
    total = partial
    for step in range(1, n):
        total = total + lax.ppermute(partial, axis, [(d, (d + step) % n) for d in range(n)])
    return total


def on_device(act_train, act_query, grad_train, grad_query, basis_in, basis_out, correction):
    norm_scale = (O * I * LQ) ** (-0.5)
    tokens = act_train.shape[0]
    n_row, n_col = lax.axis_size("row"), lax.axis_size("col")
    me = lax.axis_index("row")
    end = (me == 0) | (me == n_row - 1)
    odd = lax.axis_index("col") % 2
    flags = jnp.stack([end.astype(jnp.int32), odd.astype(jnp.int32)])
    chunks = chunk_list(basis_in.shape[1])
    count = len(chunks)
    merged = n_row == 4
    outer = [(0, 1), (1, 0), (2, 3), (3, 2)]
    inner = [(1, 2), (2, 1)]
    flip = [(d, d ^ 1) for d in range(n_col)]
    sent, got, acc, got_y = {}, {}, {}, {}

    def swap(j, payload):
        sent[j] = payload
        got[j] = lax.ppermute(payload, "row", outer)

    early = 2
    parts, narrow = in_part(act_train, act_query, basis_in, flags, chunks[:early], early)
    if merged:
        for j in range(early):
            swap(j, narrow[j])
    keep, give = out_part(flags, grad_train, grad_query, basis_out, parts[-1])
    keep_sum = lax.ppermute(give, "col", flip)
    prev = keep

    def slot(j, prev):
        part = parts[j] if j < count else None
        got_x = got[j] if j < count else None
        old = acc.get(j - 1)
        following = parts[j + LAG - 1] if j >= 1 and j + LAG - 1 < count else None
        acc[j], narrow_acc, pay = slot_part(flags, part, got_x, old, got_y.get(j - 1), following, prev)
        if narrow_acc is not None:
            got_y[j] = lax.ppermute(narrow_acc, "row", inner)
        if pay is not None:
            swap(j + LAG - 1, pay)
        return acc[j] if acc[j] is not None else pay

    if merged:
        prev = slot(0, prev)
    more, narrow = in_part(act_train, act_query, basis_in, prev, chunks[early:], 1)
    parts += more
    prev = more[-1]
    if merged:
        swap(early, narrow[0])
    wide, thin = add_part(keep, keep_sum, prev)
    bit = 2
    if merged:
        prev = slot(1, thin)
        prev = slot(2, prev)
    while bit < n_col:
        other = lax.ppermute(thin, "col", [(d, d ^ bit) for d in range(n_col)])
        wide, thin = add_part(wide, other, prev)
        prev = thin
        bit *= 2
    other = lax.ppermute(thin, "col", flip)
    rot_gt, rot_gq_t = join_part(flags, thin, other, prev, tokens)
    prev = rot_gt
    values = []
    for k in range(count):
        if merged:
            j = k + LAG
            if j <= count:
                prev = slot(j, prev)
            pair = sent[j], got[j]
        else:
            total = line_sum(parts[k], "row")
            pair = total, total
        prev = score_part(flags, rot_gt, rot_gq_t, correction, *pair, chunks[k], prev)
        values.append(prev)
    partial = functools.reduce(jnp.add, values)
    scaled = partial[:, :NQ].T * norm_scale
    blocks = scaled.reshape(NQ, n_row, tokens // n_row).transpose(1, 0, 2)
    return shared_sum(owned_sum(blocks, "row"), "col")


def solution(mesh):
    in_specs = (
        P("groups", "row"),
        P("groups", "row"),
        P("groups", "col"),
        P("groups", "col"),
        P(("groups", "row"), "col"),
        P(("groups", "col"), "row"),
        P(("groups", "row"), "col"),
    )
    out_specs = P("groups", "row")
    return jax.shard_map(
        on_device, mesh=mesh, in_specs=in_specs, out_specs=out_specs, check_vma=False
    )
```

```python
import functools

import jax
import jax.numpy as jnp
from jax import lax
from jax.experimental import pallas as pl
from jax.experimental.pallas import tpu as pltpu
from jax.sharding import PartitionSpec as P

I = 8192
O = 4096
NQ = 8
LQ = 16
LANES = 128
CHUNKS = 5
F32 = jnp.float32
BF16 = jnp.bfloat16
MIB = 1 << 20

VMEM_SPEC = pl.BlockSpec(memory_space=pltpu.VMEM)
SMEM_SPEC = pl.BlockSpec(memory_space=pltpu.SMEM)
ANY_SPEC = pl.BlockSpec(memory_space=pl.ANY)


def shape_of(rows, width, dtype):
    return jax.ShapeDtypeStruct((rows, width), dtype)


def chunk_list(size):
    tiles = size // LANES
    count = min(CHUNKS, tiles)
    chunks, first = [], 0
    for k in range(count):
        width = LANES * (tiles // count + (1 if k < tiles % count else 0))
        chunks.append((first, width))
        first += width
    return chunks


def largest_divisor(size, choices):
    for choice in choices:
        if size % choice == 0:
            return choice
    return size


def cost(flops, bytes_accessed):
    return pl.CostEstimate(flops=flops, bytes_accessed=bytes_accessed, transcendentals=0)


def in_hbm(x):
    return pltpu.with_memory_space_constraint(x, pltpu.HBM)


def halves_dot(rows, basis):
    half = rows.shape[0] // 2
    return [jnp.dot(part, basis, preferred_element_type=F32) for part in (rows[:half], rows[half:])]


def in_chunk(rows, basis, wide_ref, narrow_ref):
    half = rows.shape[0] // 2
    for h, part in enumerate(halves_dot(rows, basis)):
        wide_ref[h * half : (h + 1) * half, :] = part
        narrow_ref[h * half : (h + 1) * half, :] = part.astype(BF16)


def first_kernel(chunks, groups, train_ref, query_ref, basis_ref, *refs):
    count = len(chunks)
    rows_ref, slot_ref, sems = refs[2 * count :]
    tokens = train_ref.shape[0]
    total = slot_ref.shape[1]
    depth = basis_ref.shape[0] // groups
    copies = [
        pltpu.make_async_copy(
            basis_ref.at[pl.ds(g * depth, depth), pl.ds(0, total)],
            slot_ref.at[pl.ds(g * depth, depth), :],
            sems.at[g],
        )
        for g in range(groups)
    ]
    copies.append(pltpu.make_async_copy(train_ref, rows_ref.at[pl.ds(0, tokens), :], sems.at[groups]))
    copies.append(
        pltpu.make_async_copy(
            query_ref, rows_ref.at[pl.ds(tokens, query_ref.shape[0]), :], sems.at[groups + 1]
        )
    )
    for copy in copies:
        copy.start()
    for copy in copies:
        copy.wait()
    for j, (first, width) in enumerate(chunks):
        in_chunk(rows_ref[...], slot_ref[:, first : first + width], refs[j], refs[count + j])


def rest_kernel(chunks, train_ref, query_ref, basis_ref, prev_ref, *refs):
    count = len(chunks)
    rows = jnp.concatenate([train_ref[...], query_ref[...]], axis=0)
    for j, (first, width) in enumerate(chunks):
        in_chunk(rows, basis_ref[:, first : first + width], refs[j], refs[count + j])


def in_part(act_train, act_query, basis_in, prev, chunks):
    tokens, depth = act_train.shape
    rows = tokens + act_query.shape[0]
    total = sum(width for _, width in chunks)
    shapes = [shape_of(rows, width, F32) for _, width in chunks]
    shapes += [shape_of(rows, width, BF16) for _, width in chunks]
    if prev is None:
        groups = 4
        kernel = functools.partial(first_kernel, chunks, groups)
        scratch = [
            pltpu.VMEM((rows, depth), BF16),
            pltpu.VMEM((depth, total), BF16),
            pltpu.SemaphoreType.DMA((groups + 2,)),
        ]
        specs = [ANY_SPEC] * 3
        args = [in_hbm(act_train), in_hbm(act_query), in_hbm(basis_in)]
    else:
        kernel = functools.partial(rest_kernel, chunks)
        scratch = []
        specs = [VMEM_SPEC] * 3 + [ANY_SPEC]
        args = [act_train, act_query, basis_in, prev]
    out = pl.pallas_call(
        kernel,
        in_specs=specs,
        out_specs=[VMEM_SPEC] * len(shapes),
        out_shape=shapes,
        scratch_shapes=scratch,
        compiler_params=pltpu.CompilerParams(vmem_limit_bytes=20 * MIB),
        cost_estimate=cost(1024, 1024),
    )(*args)
    return list(out[: len(chunks)]), list(out[len(chunks) :])


def out_kernel(train_ref, query_ref, basis_ref, flags_ref, prev_ref, keep_ref, give_ref, acc_ref):
    step = pl.program_id(0)
    half = keep_ref.shape[0]
    rows = jnp.concatenate([train_ref[...], query_ref[...]], axis=0)

    @pl.when(step == 0)
    def _():
        for h, part in enumerate(halves_dot(rows, basis_ref[...])):
            acc_ref[h * half : (h + 1) * half, :] = part

    @pl.when(step > 0)
    def _():
        for h, part in enumerate(halves_dot(rows, basis_ref[...])):
            acc_ref[h * half : (h + 1) * half, :] += part

    @pl.when(step == pl.num_programs(0) - 1)
    def _():
        odd = flags_ref[1]
        keep_ref[...] = acc_ref[pl.ds(pl.multiple_of(odd * half, 16), half), :]
        give_ref[...] = acc_ref[pl.ds(pl.multiple_of((1 - odd) * half, 16), half), :]


def out_part(flags, grad_train, grad_query, basis_out, prev):
    tokens, depth = grad_train.shape
    queries = grad_query.shape[0]
    width = basis_out.shape[1]
    rows = tokens + queries
    block = largest_divisor(depth, (1024, 896, 512, 256, 128))
    return pl.pallas_call(
        out_kernel,
        grid=(depth // block,),
        in_specs=[
            pl.BlockSpec((tokens, block), lambda j: (0, j)),
            pl.BlockSpec((queries, block), lambda j: (0, j)),
            pl.BlockSpec((block, width), lambda j: (j, 0)),
            SMEM_SPEC,
            ANY_SPEC,
        ],
        out_specs=[
            pl.BlockSpec((rows // 2, width), lambda j: (0, 0)),
            pl.BlockSpec((rows // 2, width), lambda j: (0, 0)),
        ],
        out_shape=[shape_of(rows // 2, width, F32)] * 2,
        scratch_shapes=[pltpu.VMEM((rows, width), F32)],
        compiler_params=pltpu.CompilerParams(vmem_limit_bytes=24 * MIB),
        cost_estimate=cost(1024, 1024),
    )(in_hbm(grad_train), in_hbm(grad_query), in_hbm(basis_out), flags, prev)


def add_kernel(keep_ref, got_ref, prev_ref, wide_ref, narrow_ref):
    total = keep_ref[...] + got_ref[...].astype(F32)
    wide_ref[...] = total
    narrow_ref[...] = total.astype(BF16)


def add_part(keep, got, prev):
    rows, width = keep.shape
    return pl.pallas_call(
        add_kernel,
        in_specs=[VMEM_SPEC, VMEM_SPEC, ANY_SPEC],
        out_specs=[VMEM_SPEC, VMEM_SPEC],
        out_shape=[shape_of(rows, width, F32), shape_of(rows, width, BF16)],
        compiler_params=pltpu.CompilerParams(vmem_limit_bytes=12 * MIB),
        cost_estimate=cost(1024, 1024),
    )(keep, got, prev)


def join_kernel(tokens, mine_ref, other_ref, flags_ref, prev_ref, gt_ref, gq_ref):
    odd = flags_ref[1]
    mine, other = mine_ref[...].astype(F32), other_ref[...].astype(F32)
    low = jnp.where(odd == 1, other, mine).astype(BF16)
    high = jnp.where(odd == 1, mine, other).astype(BF16)
    rows = jnp.concatenate([low, high], axis=0)
    gt_ref[...] = rows[:tokens]
    gq_ref[...] = rows[tokens:].astype(F32).T.astype(BF16)


def join_part(flags, mine, other, prev, tokens):
    half, width = mine.shape
    queries = 2 * half - tokens
    return pl.pallas_call(
        functools.partial(join_kernel, tokens),
        in_specs=[VMEM_SPEC, VMEM_SPEC, SMEM_SPEC, ANY_SPEC],
        out_specs=[VMEM_SPEC, VMEM_SPEC],
        out_shape=[shape_of(tokens, width, BF16), shape_of(width, queries, BF16)],
        compiler_params=pltpu.CompilerParams(vmem_limit_bytes=16 * MIB),
        cost_estimate=cost(1024, 1024),
    )(mine, other, flags, prev)


def meet_kernel(part_ref, got_ref, give_ref, prev_ref, wide_ref, narrow_ref, pass_ref):
    total = part_ref[...] + got_ref[...].astype(F32)
    wide_ref[...] = total
    narrow_ref[...] = total.astype(BF16)


def meet_part(part, got, give, prev):
    rows, width = part.shape
    return pl.pallas_call(
        meet_kernel,
        in_specs=[VMEM_SPEC, VMEM_SPEC, ANY_SPEC, ANY_SPEC],
        out_specs=[VMEM_SPEC, VMEM_SPEC, ANY_SPEC],
        out_shape=[
            shape_of(rows, width, F32),
            shape_of(rows, width, BF16),
            jax.ShapeDtypeStruct(give.shape, give.dtype),
        ],
        input_output_aliases={2: 2},
        compiler_params=pltpu.CompilerParams(vmem_limit_bytes=12 * MIB),
        cost_estimate=cost(1024, 1024),
    )(part, got, give, prev)


def total_kernel(acc_ref, got_ref, prev_ref, total_ref):
    total_ref[...] = (acc_ref[...] + got_ref[...].astype(F32)).astype(BF16)


def total_part(acc, got, prev):
    return pl.pallas_call(
        total_kernel,
        in_specs=[VMEM_SPEC, VMEM_SPEC, ANY_SPEC],
        out_specs=VMEM_SPEC,
        out_shape=shape_of(*acc.shape, BF16),
        compiler_params=pltpu.CompilerParams(vmem_limit_bytes=12 * MIB),
        cost_estimate=cost(1024, 1024),
    )(acc, got, prev)


def score_kernel(
    first, start, scale, flags_ref, gt_ref, gq_ref, corr_ref, sent_ref, got_ref, prev_ref,
    out_ref, quot_ref, inv_ref, wide_ref, own_ref
):
    tokens = gt_ref.shape[0]
    queries = gq_ref.shape[1]
    width = inv_ref.shape[1]
    inv_ref[...] = 1.0 / corr_ref[:, first : first + width]
    end = flags_ref[0] == 1
    total = jnp.where(end, got_ref[...].astype(F32), sent_ref[...].astype(F32))
    wide_ref[...] = total[:tokens]
    own_ref[...] = total[tokens:]
    owner = lax.broadcasted_iota(jnp.int32, (queries, width), 0) // LQ
    lane = lax.broadcasted_iota(jnp.int32, (tokens, LANES), 1)

    def quotient(q):
        own = jnp.where(owner == q, own_ref[...], 0.0).astype(BF16)
        products = jnp.dot(gq_ref[...], own, preferred_element_type=F32)
        quot_ref[q % 2] = (products * inv_ref[...]).astype(BF16)

    quotient(0)
    result = jnp.zeros((tokens, LANES), F32) if start else prev_ref[...]
    for q in range(NQ):
        if q + 1 < NQ:
            quotient(q + 1)
        mapped = jnp.dot(gt_ref[...], quot_ref[q % 2], preferred_element_type=F32)
        scaled = mapped * wide_ref[...]
        folded = scaled[:, :LANES]
        for part in range(1, width // LANES):
            folded = folded + scaled[:, part * LANES : (part + 1) * LANES]
        result = result + jnp.where(lane == q, jnp.sum(folded, axis=1, keepdims=True), 0.0)
    if scale is None:
        out_ref[...] = result
    else:
        out_ref[...] = (result * scale).T[:NQ]


def score_part(flags, rot_gt, rot_gq_t, correction, sent, got, chunk, prev, start, scale):
    tokens, outs = rot_gt.shape
    first, width = chunk
    queries = rot_gq_t.shape[1]
    return pl.pallas_call(
        functools.partial(score_kernel, first, start, scale),
        in_specs=[SMEM_SPEC] + [VMEM_SPEC] * 5 + [ANY_SPEC if start else VMEM_SPEC],
        out_specs=VMEM_SPEC,
        out_shape=shape_of(tokens, LANES, F32) if scale is None else shape_of(NQ, tokens, F32),
        scratch_shapes=[
            pltpu.VMEM((2, outs, width), BF16),
            pltpu.VMEM((outs, width), F32),
            pltpu.VMEM((tokens, width), F32),
            pltpu.VMEM((queries, width), F32),
        ],
        compiler_params=pltpu.CompilerParams(vmem_limit_bytes=16 * MIB),
        cost_estimate=cost(2 * NQ * outs * width * (tokens + queries), 4 * outs * width),
    )(flags, rot_gt, rot_gq_t, correction, sent, got, prev)


def line_sum(partial, axis):
    n = lax.axis_size(axis)
    half = n // 2
    me = lax.axis_index(axis)
    if n % 2:
        return lax.psum(partial, axis).astype(BF16)
    acc = partial
    for s in range(half - 1):
        pairs = [(s, s + 1), (n - 1 - s, n - 2 - s)]
        acc = acc + lax.ppermute(acc.astype(BF16), axis, pairs).astype(F32)
    got = lax.ppermute(acc.astype(BF16), axis, [(half - 1, half), (half, half - 1)])
    total = (acc + got.astype(F32)).astype(BF16)
    for s in range(half - 2, -1, -1):
        pairs = [(s + 1, s), (n - 2 - s, n - 1 - s)]
        got = lax.ppermute(total, axis, pairs)
        total = jnp.where((me == s) | (me == n - 1 - s), got, total)
    return total


def owned_sum(partial, axis):
    n = lax.axis_size(axis)
    me = lax.axis_index(axis)
    total = lax.dynamic_index_in_dim(partial, me, 0, keepdims=False)
    for step in range(1, n):
        block = lax.dynamic_index_in_dim(partial, (me + step) % n, 0, keepdims=False)
        total = total + lax.ppermute(block, axis, [(d, (d + step) % n) for d in range(n)])
    return total


def shared_sum(partial, axis):
    n = lax.axis_size(axis)
    total = partial
    for step in range(1, n):
        total = total + lax.ppermute(partial, axis, [(d, (d + step) % n) for d in range(n)])
    return total


def on_device(act_train, act_query, grad_train, grad_query, basis_in, basis_out, correction):
    norm_scale = (O * I * LQ) ** (-0.5)
    tokens = act_train.shape[0]
    n_row, n_col = lax.axis_size("row"), lax.axis_size("col")
    me = lax.axis_index("row")
    end = (me == 0) | (me == n_row - 1)
    odd = lax.axis_index("col") % 2
    flags = jnp.stack([end.astype(jnp.int32), odd.astype(jnp.int32)])
    chunks = chunk_list(basis_in.shape[1])
    count = len(chunks)
    line = n_row == 4
    flip = [(d, d ^ 1) for d in range(n_col)]
    inner = []
    for c in range(n_col):
        inner += [(n_col + c, 2 * n_col + c), (2 * n_col + c, n_col + c)]
        inner += [(c, c ^ 1), (3 * n_col + c, 3 * n_col + (c ^ 1))]
    got_in, acc, got_mid, total, got_out = {}, {}, {}, {}, {}

    def send_in(j):
        got_in[j] = lax.ppermute(narrow[j], "row", [(0, 1), (3, 2)])

    def meet(j, prev):
        if not line:
            return prev
        acc[j], thin = add_part(parts[j], got_in[j], prev)
        got_mid[j] = lax.ppermute(thin, ("row", "col"), inner)
        return thin

    def settle(j, prev):
        if not line:
            total[j] = got_out[j] = line_sum(parts[j], "row")
            return prev
        total[j] = total_part(acc[j], got_mid[j], prev)
        got_out[j] = lax.ppermute(total[j], "row", [(1, 0), (2, 3)])
        return total[j]

    def score(j, prev):
        return score_part(
            flags, rot_gt, rot_gq_t, correction, total[j], got_out[j], chunks[j], prev,
            j == 0, norm_scale if j == count - 1 else None,
        )

    early = 2
    parts, narrow = in_part(act_train, act_query, basis_in, None, chunks[:early])
    if line:
        for j in range(early):
            send_in(j)
    keep, give = out_part(flags, grad_train, grad_query, basis_out, parts[-1])
    prev = keep
    if line:
        acc[0], thin, give = meet_part(parts[0], got_in[0], give, keep)
        got_mid[0] = lax.ppermute(thin, ("row", "col"), inner)
        prev = thin
    given = lax.ppermute(give, "col", flip)
    more, more_narrow = in_part(act_train, act_query, basis_in, prev, chunks[early:])
    parts, narrow = parts + more, narrow + more_narrow
    if line:
        for j in range(early, count):
            send_in(j)
    wide, thin = add_part(keep, given, more[-1])
    bit = 2
    prev = thin
    while bit < n_col:
        other = lax.ppermute(thin, "col", [(d, d ^ bit) for d in range(n_col)])
        if bit == 2:
            prev = settle(0, meet(1, prev))
            prev = settle(1, meet(2, prev))
        wide, thin = add_part(wide, other, prev)
        prev = thin
        bit *= 2
    other = lax.ppermute(thin, "col", flip)
    prev = settle(2, meet(3, prev))
    rot_gt, rot_gq_t = join_part(flags, thin, other, prev, tokens)
    done = 0
    sums = rot_gt
    for j in range(4, count + 1):
        for k in range(done, j - 2):
            sums = score(k, sums)
        done = j - 2
        prev = sums
        if j < count:
            prev = meet(j, prev)
        prev = settle(j - 1, prev)
    for k in range(done, count):
        sums = score(k, sums)
    per_row = tokens // n_row
    blocks = sums.reshape(NQ, n_row, per_row).transpose(1, 0, 2)
    return shared_sum(owned_sum(blocks, "row"), "col")


def solution(mesh):
    in_specs = (
        P("groups", "row"),
        P("groups", "row"),
        P("groups", "col"),
        P("groups", "col"),
        P(("groups", "row"), "col"),
        P(("groups", "col"), "row"),
        P(("groups", "row"), "col"),
    )
    out_specs = P("groups", "row")
    return jax.shard_map(
        on_device, mesh=mesh, in_specs=in_specs, out_specs=out_specs, check_vma=False
    )
```

```python
import functools

import jax
import jax.numpy as jnp
from jax import lax
from jax.experimental import pallas as pl
from jax.experimental.pallas import tpu as pltpu
from jax.sharding import PartitionSpec as P

I = 8192
O = 4096
NQ = 8
LQ = 16
LANES = 128
CHUNKS = 8
LAG = 3
F32 = jnp.float32
BF16 = jnp.bfloat16
MIB = 1 << 20

VMEM_SPEC = pl.BlockSpec(memory_space=pltpu.VMEM)
SMEM_SPEC = pl.BlockSpec(memory_space=pltpu.SMEM)
ANY_SPEC = pl.BlockSpec(memory_space=pl.ANY)


def shape_of(rows, width, dtype):
    return jax.ShapeDtypeStruct((rows, width), dtype)


def chunk_list(size):
    tiles = size // LANES
    count = min(CHUNKS, tiles)
    chunks, first = [], 0
    for k in range(count):
        width = LANES * (tiles // count + (1 if k < tiles % count else 0))
        chunks.append((first, width))
        first += width
    return chunks


def largest_divisor(size, choices):
    for choice in choices:
        if size % choice == 0:
            return choice
    return size


def pieces_of(width, most):
    return max(p for p in range(1, most + 1) if width % (p * LANES) == 0)


def cost(flops, bytes_accessed):
    return pl.CostEstimate(flops=flops, bytes_accessed=bytes_accessed, transcendentals=0)


def in_hbm(x):
    return pltpu.with_memory_space_constraint(x, pltpu.HBM)


def halves_dot(rows, basis):
    half = rows.shape[0] // 2
    return [jnp.dot(part, basis, preferred_element_type=F32) for part in (rows[:half], rows[half:])]


def in_chunk(rows, basis, wide_ref, narrow_ref):
    half = rows.shape[0] // 2
    for h, part in enumerate(halves_dot(rows, basis)):
        wide_ref[h * half : (h + 1) * half, :] = part
        narrow_ref[h * half : (h + 1) * half, :] = part.astype(BF16)


def first_kernel(chunks, groups, train_ref, query_ref, basis_ref, *refs):
    count = len(chunks)
    rows_ref, slot_ref, sum_ref, sems = refs[2 * count :]
    tokens, queries = train_ref.shape[0], query_ref.shape[0]
    total = slot_ref.shape[1]
    depth = basis_ref.shape[0] // groups
    copies = []
    for g in range(groups):
        part = pl.ds(g * depth, depth)
        copies.append([
            pltpu.make_async_copy(
                basis_ref.at[part, pl.ds(0, total)], slot_ref.at[part, :], sems.at[g, 0]
            ),
            pltpu.make_async_copy(
                train_ref.at[:, part], rows_ref.at[pl.ds(0, tokens), part], sems.at[g, 1]
            ),
            pltpu.make_async_copy(
                query_ref.at[:, part], rows_ref.at[pl.ds(tokens, queries), part], sems.at[g, 2]
            ),
        ])
    for group in copies:
        for copy in group:
            copy.start()
    for g, group in enumerate(copies):
        for copy in group:
            copy.wait()
        part = slice(g * depth, (g + 1) * depth)
        half = rows_ref.shape[0] // 2
        for h, value in enumerate(halves_dot(rows_ref[:, part], slot_ref[part, :])):
            if g == 0:
                sum_ref[h * half : (h + 1) * half, :] = value
            else:
                sum_ref[h * half : (h + 1) * half, :] += value
    for j, (first, width) in enumerate(chunks):
        value = sum_ref[:, first : first + width]
        refs[j][...] = value
        refs[count + j][...] = value.astype(BF16)


def rest_kernel(chunks, train_ref, query_ref, basis_ref, prev_ref, *refs):
    count = len(chunks)
    rows = jnp.concatenate([train_ref[...], query_ref[...]], axis=0)
    for j, (first, width) in enumerate(chunks):
        in_chunk(rows, basis_ref[:, first : first + width], refs[j], refs[count + j])


def in_part(act_train, act_query, basis_in, prev, chunks):
    tokens, depth = act_train.shape
    rows = tokens + act_query.shape[0]
    total = sum(width for _, width in chunks)
    shapes = [shape_of(rows, width, F32) for _, width in chunks]
    shapes += [shape_of(rows, width, BF16) for _, width in chunks]
    if prev is None:
        groups = next(g for g in (4, 2, 1) if depth % (g * LANES) == 0)
        kernel = functools.partial(first_kernel, chunks, groups)
        scratch = [
            pltpu.VMEM((rows, depth), BF16),
            pltpu.VMEM((depth, total), BF16),
            pltpu.VMEM((rows, total), F32),
            pltpu.SemaphoreType.DMA((groups, 3)),
        ]
        specs = [ANY_SPEC] * 3
        args = [in_hbm(act_train), in_hbm(act_query), in_hbm(basis_in)]
    else:
        kernel = functools.partial(rest_kernel, chunks)
        scratch = []
        specs = [VMEM_SPEC] * 3 + [ANY_SPEC]
        args = [act_train, act_query, basis_in, prev]
    out = pl.pallas_call(
        kernel,
        in_specs=specs,
        out_specs=[VMEM_SPEC] * len(shapes),
        out_shape=shapes,
        scratch_shapes=scratch,
        compiler_params=pltpu.CompilerParams(vmem_limit_bytes=20 * MIB),
        cost_estimate=cost(1024, 1024),
    )(*args)
    return list(out[: len(chunks)]), list(out[len(chunks) :])


def out_kernel(last, train_ref, query_ref, basis_ref, flags_ref, prev_ref, *refs):
    step = pl.program_id(0)
    rows = jnp.concatenate([train_ref[...], query_ref[...]], axis=0)
    half = rows.shape[0] // 2
    acc_ref = refs[-1]

    @pl.when(step == 0)
    def _():
        for h, part in enumerate(halves_dot(rows, basis_ref[...])):
            span = slice(h * half, (h + 1) * half)
            acc_ref[span, :] = refs[0][span, :] + part if last else part

    @pl.when(step > 0)
    def _():
        for h, part in enumerate(halves_dot(rows, basis_ref[...])):
            acc_ref[h * half : (h + 1) * half, :] += part

    if last:
        keep_ref, give_refs = refs[1], refs[2:-1]

        @pl.when(step == pl.num_programs(0) - 1)
        def _():
            odd = flags_ref[1]
            keep_ref[...] = acc_ref[pl.ds(pl.multiple_of(odd * half, 16), half), :]
            cols = give_refs[0].shape[1]
            for c, give_ref in enumerate(give_refs):
                span = slice(c * cols, (c + 1) * cols)
                give_ref[...] = acc_ref[pl.ds(pl.multiple_of((1 - odd) * half, 16), half), span]


def out_part(flags, grad_train, grad_query, basis_out, prev, acc):
    tokens, depth = grad_train.shape
    queries = grad_query.shape[0]
    width = basis_out.shape[1]
    rows = tokens + queries
    block = largest_divisor(depth, (1024, 896, 512, 256, 128))
    steps = depth // block
    last = acc is not None
    first = (steps + 1) // 2
    skip, count = (first, steps - first) if last else (0, first)
    whole = pl.BlockSpec((rows, width), lambda j: (0, 0))
    half = pl.BlockSpec((rows // 2, width), lambda j: (0, 0))
    pieces = pieces_of(width, 2)
    piece = pl.BlockSpec((rows // 2, width // pieces), lambda j: (0, 0))
    if last:
        out_shape = [shape_of(rows // 2, width, F32)]
        out_shape += [shape_of(rows // 2, width // pieces, F32)] * pieces
    else:
        out_shape = [shape_of(rows, width, F32)]
    return pl.pallas_call(
        functools.partial(out_kernel, last),
        grid=(count,),
        in_specs=[
            pl.BlockSpec((tokens, block), lambda j: (0, j + skip)),
            pl.BlockSpec((queries, block), lambda j: (0, j + skip)),
            pl.BlockSpec((block, width), lambda j: (j + skip, 0)),
            SMEM_SPEC,
            ANY_SPEC,
        ]
        + ([whole] if last else []),
        out_specs=[half] + [piece] * pieces if last else [whole],
        out_shape=out_shape,
        scratch_shapes=[pltpu.VMEM((rows, width), F32)] if last else [],
        compiler_params=pltpu.CompilerParams(vmem_limit_bytes=28 * MIB),
        cost_estimate=cost(2 * rows * block * count * width, 2 * block * count * (rows + width)),
    )(
        in_hbm(grad_train), in_hbm(grad_query), in_hbm(basis_out), flags, prev,
        *([acc] if last else []),
    )


def add_kernel(pieces, outs, handed, keep_ref, *refs):
    wide_ref, narrow_refs = refs[pieces + handed + 1], refs[pieces + handed + 2 :][:outs]
    width = keep_ref.shape[1]
    cols = width // pieces
    for c in range(pieces):
        span = slice(c * cols, (c + 1) * cols)
        wide_ref[:, span] = keep_ref[:, span] + refs[c][...].astype(F32)
    cols = width // outs
    for c in range(outs):
        narrow_refs[c][...] = wide_ref[:, c * cols : (c + 1) * cols].astype(BF16)


def add_part(keep, got, prev, outs=1, handed=()):
    rows, width = keep.shape
    got, handed = list(got), list(handed)
    out = pl.pallas_call(
        functools.partial(add_kernel, len(got), outs, len(handed)),
        in_specs=[VMEM_SPEC] * (1 + len(got)) + [ANY_SPEC] * (len(handed) + 1),
        out_specs=[VMEM_SPEC] * (1 + outs) + [ANY_SPEC] * len(handed),
        out_shape=[shape_of(rows, width, F32)]
        + [shape_of(rows, width // outs, BF16)] * outs
        + [shape_of(*x.shape, x.dtype) for x in handed],
        input_output_aliases={1 + len(got) + i: 1 + outs + i for i in range(len(handed))},
        compiler_params=pltpu.CompilerParams(vmem_limit_bytes=12 * MIB),
        cost_estimate=cost(1024, 1024),
    )(keep, *got, *handed, prev)
    return out[0], list(out[1 : 1 + outs]), list(out[1 + outs :])


def join_kernel(tokens, pieces, flags_ref, corr_ref, prev_ref, *refs):
    mine_refs, other_refs = refs[:pieces], refs[pieces : 2 * pieces]
    gt_ref, gq_ref, chunk_ref, sem = refs[2 * pieces :]
    fetch = pltpu.make_async_copy(corr_ref.at[:, pl.ds(0, chunk_ref.shape[1])], chunk_ref, sem)
    fetch.start()
    odd = flags_ref[1]
    for c, (mine_ref, other_ref) in enumerate(zip(mine_refs, other_refs)):
        mine, other = mine_ref[...].astype(F32), other_ref[...].astype(F32)
        low = jnp.where(odd == 1, other, mine)
        high = jnp.where(odd == 1, mine, other)
        rows = jnp.concatenate([low, high], axis=0)
        cols = rows.shape[1]
        gt_ref[:, c * cols : (c + 1) * cols] = rows[:tokens].astype(BF16)
        gq_ref[c * cols : (c + 1) * cols, :] = rows[tokens:].T.astype(BF16)
    fetch.wait()


def join_part(flags, mine, other, correction, prev, tokens, first):
    half = mine[0].shape[0]
    width = sum(x.shape[1] for x in mine)
    queries = 2 * half - tokens
    return pl.pallas_call(
        functools.partial(join_kernel, tokens, len(mine)),
        in_specs=[SMEM_SPEC, ANY_SPEC, ANY_SPEC] + [VMEM_SPEC] * (2 * len(mine)),
        out_specs=[VMEM_SPEC] * 3,
        out_shape=[
            shape_of(tokens, width, BF16),
            shape_of(width, queries, BF16),
            shape_of(width, first, F32),
        ],
        scratch_shapes=[pltpu.SemaphoreType.DMA],
        compiler_params=pltpu.CompilerParams(vmem_limit_bytes=16 * MIB),
        cost_estimate=cost(1024, 1024),
    )(flags, in_hbm(correction), prev, *mine, *other)


def pay_kernel(has_part, flags_ref, acc_ref, got_ref, *refs):
    total = acc_ref[...] + got_ref[...].astype(F32)
    if has_part:
        total = jnp.where(flags_ref[0] == 1, refs[0][...], total)
    refs[-1][...] = total.astype(BF16)


def pay_part(flags, acc, got, part, prev):
    has_part = part is not None
    return pl.pallas_call(
        functools.partial(pay_kernel, has_part),
        in_specs=[SMEM_SPEC, VMEM_SPEC, VMEM_SPEC] + [VMEM_SPEC] * has_part + [ANY_SPEC],
        out_specs=VMEM_SPEC,
        out_shape=shape_of(*acc.shape, BF16),
        compiler_params=pltpu.CompilerParams(vmem_limit_bytes=12 * MIB),
        cost_estimate=cost(1024, 1024),
    )(flags, acc, got, *([part] if has_part else []), prev)


def score_kernel(
    start, scale, following, flags_ref, gt_ref, gq_ref, chunk_ref, sent_ref, got_ref, corr_ref,
    prev_ref, order_ref, out_ref, *refs
):
    quot_ref, inv_ref, wide_ref, own_ref, sem = refs[-5:]
    tokens = gt_ref.shape[0]
    queries = gq_ref.shape[1]
    width = inv_ref.shape[1]
    if following is not None:
        fetch = pltpu.make_async_copy(corr_ref.at[:, pl.ds(*following)], refs[0], sem)
        fetch.start()
    inv_ref[...] = 1.0 / chunk_ref[...]
    end = flags_ref[0] == 1
    total = jnp.where(end, got_ref[...].astype(F32), sent_ref[...].astype(F32))
    wide_ref[...] = total[:tokens]
    own_ref[...] = total[tokens:]
    owner = lax.broadcasted_iota(jnp.int32, (queries, width), 0) // LQ
    lane = lax.broadcasted_iota(jnp.int32, (tokens, LANES), 1)

    def quotient(q):
        own = jnp.where(owner == q, own_ref[...], 0.0).astype(BF16)
        products = jnp.dot(gq_ref[...], own, preferred_element_type=F32)
        quot_ref[q % 2] = (products * inv_ref[...]).astype(BF16)

    quotient(0)
    result = jnp.zeros((tokens, LANES), F32) if start else prev_ref[...]
    for q in range(NQ):
        if q + 1 < NQ:
            quotient(q + 1)
        mapped = jnp.dot(gt_ref[...], quot_ref[q % 2], preferred_element_type=F32)
        scaled = mapped * wide_ref[...]
        folded = scaled[:, :LANES]
        for part in range(1, width // LANES):
            folded = folded + scaled[:, part * LANES : (part + 1) * LANES]
        result = result + jnp.where(lane == q, jnp.sum(folded, axis=1, keepdims=True), 0.0)
    if scale is None:
        out_ref[...] = result
    else:
        out_ref[...] = (result * scale).T[:NQ]
    if following is not None:
        fetch.wait()


def score_part(
    flags, rot_gt, rot_gq_t, correction, chunk, sent, got, prev, order, start, scale, following
):
    tokens, outs = rot_gt.shape
    width = chunk.shape[1]
    queries = rot_gq_t.shape[1]
    out_shape = [shape_of(tokens, LANES, F32) if scale is None else shape_of(NQ, tokens, F32)]
    if following is not None:
        out_shape.append(shape_of(outs, following[1], F32))
    out = pl.pallas_call(
        functools.partial(score_kernel, start, scale, following),
        in_specs=[SMEM_SPEC] + [VMEM_SPEC] * 5
        + [ANY_SPEC, ANY_SPEC if start else VMEM_SPEC, ANY_SPEC],
        out_specs=[VMEM_SPEC] * len(out_shape),
        out_shape=out_shape,
        scratch_shapes=[
            pltpu.VMEM((2, outs, width), BF16),
            pltpu.VMEM((outs, width), F32),
            pltpu.VMEM((tokens, width), F32),
            pltpu.VMEM((queries, width), F32),
            pltpu.SemaphoreType.DMA,
        ],
        compiler_params=pltpu.CompilerParams(vmem_limit_bytes=16 * MIB),
        cost_estimate=cost(2 * NQ * outs * width * (tokens + queries), 4 * outs * width),
    )(flags, rot_gt, rot_gq_t, chunk, sent, got, in_hbm(correction), prev, order)
    return out[0], out[1] if following is not None else None


def line_sum(partial, axis):
    n = lax.axis_size(axis)
    half = n // 2
    me = lax.axis_index(axis)
    if n % 2:
        return lax.psum(partial, axis).astype(BF16)
    acc = partial
    for s in range(half - 1):
        pairs = [(s, s + 1), (n - 1 - s, n - 2 - s)]
        acc = acc + lax.ppermute(acc.astype(BF16), axis, pairs).astype(F32)
    got = lax.ppermute(acc.astype(BF16), axis, [(half - 1, half), (half, half - 1)])
    total = (acc + got.astype(F32)).astype(BF16)
    for s in range(half - 2, -1, -1):
        pairs = [(s + 1, s), (n - 2 - s, n - 1 - s)]
        got = lax.ppermute(total, axis, pairs)
        total = jnp.where((me == s) | (me == n - 1 - s), got, total)
    return total


def owned_sum(partial, axis):
    n = lax.axis_size(axis)
    me = lax.axis_index(axis)
    total = lax.dynamic_index_in_dim(partial, me, 0, keepdims=False)
    for step in range(1, n):
        block = lax.dynamic_index_in_dim(partial, (me + step) % n, 0, keepdims=False)
        total = total + lax.ppermute(block, axis, [(d, (d + step) % n) for d in range(n)])
    return total


def shared_sum(partial, axis):
    n = lax.axis_size(axis)
    total = partial
    for step in range(1, n):
        total = total + lax.ppermute(partial, axis, [(d, (d + step) % n) for d in range(n)])
    return total


def on_device(act_train, act_query, grad_train, grad_query, basis_in, basis_out, correction):
    norm_scale = (O * I * LQ) ** (-0.5)
    tokens = act_train.shape[0]
    n_row, n_col = lax.axis_size("row"), lax.axis_size("col")
    me = lax.axis_index("row")
    end = (me == 0) | (me == n_row - 1)
    odd = lax.axis_index("col") % 2
    flags = jnp.stack([end.astype(jnp.int32), odd.astype(jnp.int32)])
    chunks = chunk_list(basis_in.shape[1])
    count = len(chunks)
    line = n_row == 4
    flip = [(d, d ^ 1) for d in range(n_col)]
    outer = [(0, 1), (1, 0), (2, 3), (3, 2)]
    inner = []
    for c in range(n_col):
        inner += [(n_col + c, 2 * n_col + c), (2 * n_col + c, n_col + c)]
        inner += [(c, c ^ 1), (3 * n_col + c, 3 * n_col + (c ^ 1))]
    sent, got, acc, got_mid = {}, {}, {}, {}

    def swap(j, payload):
        sent[j] = payload
        got[j] = lax.ppermute(payload, "row", outer)

    def meet(j, prev, handed=()):
        if not line or j >= count:
            return prev, list(handed)
        acc[j], (thin,), handed = add_part(parts[j], [got[j]], prev, 1, handed)
        got_mid[j] = lax.ppermute(thin, ("row", "col"), inner)
        return thin, handed

    def pay(j, prev):
        if not line:
            sent[j + LAG] = got[j + LAG] = line_sum(parts[j], "row")
            return prev
        part = parts[j + LAG] if j + LAG < count else None
        payload = pay_part(flags, acc[j], got_mid[j], part, prev)
        swap(j + LAG, payload)
        return payload

    parts, narrow = in_part(act_train, act_query, basis_in, None, chunks[:LAG])
    if line:
        for j in range(LAG):
            swap(j, narrow[j])
    (half_sum,) = out_part(flags, grad_train, grad_query, basis_out, parts[-1], None)
    prev, _ = meet(0, half_sum)
    keep, *give = out_part(flags, grad_train, grad_query, basis_out, prev, half_sum)
    prev, give = meet(1, keep, give)
    given = [lax.ppermute(piece, "col", flip) for piece in give]
    more, _ = in_part(act_train, act_query, basis_in, prev, chunks[LAG:])
    parts += more
    prev = pay(0, more[-1])
    prev, _ = meet(2, prev)
    prev = pay(1, prev)
    outs = pieces_of(keep.shape[1], 2)
    wide, thin, _ = add_part(keep, given, prev, outs)
    prev, bit = wide, 2
    while bit < n_col:
        other = [lax.ppermute(x, "col", [(d, d ^ bit) for d in range(n_col)]) for x in thin]
        if bit == 2:
            for j in (3, 4):
                prev, _ = meet(j, prev)
                prev = pay(j - 1, prev)
        wide, thin, _ = add_part(wide, other, prev, outs)
        prev = wide
        bit *= 2
    other = [lax.ppermute(x, "col", flip) for x in thin]
    prev, _ = meet(5, prev)
    prev = pay(4, prev)
    rot_gt, rot_gq_t, chunk = join_part(flags, thin, other, correction, prev, tokens, chunks[0][1])
    sums = rot_gt
    done = 0
    for j in range(5, count + LAG):
        for k in range(done, min(j - LAG + 1, done + 2, count)):
            sums, chunk = score_part(
                flags, rot_gt, rot_gq_t, correction, chunk, sent[k + LAG], got[k + LAG], sums, prev,
                k == 0, norm_scale if k == count - 1 else None,
                chunks[k + 1] if k + 1 < count else None,
            )
            done = k + 1
        if j < count:
            prev, _ = meet(j + 1, sums)
            prev = pay(j, prev)
    per_row = tokens // n_row
    blocks = sums.reshape(NQ, n_row, per_row).transpose(1, 0, 2)
    return shared_sum(owned_sum(blocks, "row"), "col")


def solution(mesh):
    in_specs = (
        P("groups", "row"),
        P("groups", "row"),
        P("groups", "col"),
        P("groups", "col"),
        P(("groups", "row"), "col"),
        P(("groups", "col"), "row"),
        P(("groups", "row"), "col"),
    )
    out_specs = P("groups", "row")
    return jax.shard_map(
        on_device, mesh=mesh, in_specs=in_specs, out_specs=out_specs, check_vma=False
    )
```

```python
import functools

import jax
import jax.numpy as jnp
from jax import lax
from jax.experimental import pallas as pl
from jax.experimental.pallas import tpu as pltpu
from jax.sharding import PartitionSpec as P

I = 8192
O = 4096
NQ = 8
LQ = 16
LANES = 128
CHUNKS = 8
LAG = 3
F32 = jnp.float32
BF16 = jnp.bfloat16
MIB = 1 << 20

VMEM_SPEC = pl.BlockSpec(memory_space=pltpu.VMEM)
SMEM_SPEC = pl.BlockSpec(memory_space=pltpu.SMEM)
ANY_SPEC = pl.BlockSpec(memory_space=pl.ANY)


def shape_of(rows, width, dtype):
    return jax.ShapeDtypeStruct((rows, width), dtype)


def chunk_list(size):
    tiles = size // LANES
    count = min(CHUNKS, tiles)
    chunks, first = [], 0
    for k in range(count):
        width = LANES * (tiles // count + (1 if k < tiles % count else 0))
        chunks.append((first, width))
        first += width
    return chunks


def largest_divisor(size, choices):
    for choice in choices:
        if size % choice == 0:
            return choice
    return size


def pieces_of(width, most):
    return max(p for p in range(1, most + 1) if width % (p * LANES) == 0)


def cost(flops, bytes_accessed):
    return pl.CostEstimate(flops=flops, bytes_accessed=bytes_accessed, transcendentals=0)


def in_hbm(x):
    return pltpu.with_memory_space_constraint(x, pltpu.HBM)


def halves_dot(rows, basis):
    half = rows.shape[0] // 2
    return [jnp.dot(part, basis, preferred_element_type=F32) for part in (rows[:half], rows[half:])]


def in_kernel(chunks, narrow, groups, train_ref, query_ref, basis_ref, prev_ref, *refs):
    count = len(chunks)
    rows_ref, slot_ref, sum_ref, sems = refs[count + narrow :]
    tokens, queries = train_ref.shape[0], query_ref.shape[0]
    start, total = chunks[0][0], slot_ref.shape[1]
    depth = basis_ref.shape[0] // groups
    copies = []
    for g in range(groups):
        part = pl.ds(g * depth, depth)
        copies.append([
            pltpu.make_async_copy(
                basis_ref.at[part, pl.ds(start, total)], slot_ref.at[part, :], sems.at[g, 0]
            ),
            pltpu.make_async_copy(
                train_ref.at[:, part], rows_ref.at[pl.ds(0, tokens), part], sems.at[g, 1]
            ),
            pltpu.make_async_copy(
                query_ref.at[:, part], rows_ref.at[pl.ds(tokens, queries), part], sems.at[g, 2]
            ),
        ])
    for group in copies:
        for copy in group:
            copy.start()
    for g, group in enumerate(copies):
        for copy in group:
            copy.wait()
        part = slice(g * depth, (g + 1) * depth)
        half = rows_ref.shape[0] // 2
        for h, value in enumerate(halves_dot(rows_ref[:, part], slot_ref[part, :])):
            span = slice(h * half, (h + 1) * half)
            if g == 0:
                sum_ref[span, :] = value
            else:
                sum_ref[span, :] += value
    for j, (first, width) in enumerate(chunks):
        value = sum_ref[:, first - start : first - start + width]
        refs[j][...] = value
        if j < narrow:
            refs[count + j][...] = value.astype(BF16)


def in_part(act_train, act_query, basis_in, prev, chunks, narrow):
    tokens, depth = act_train.shape
    rows = tokens + act_query.shape[0]
    total = sum(width for _, width in chunks)
    groups = next(g for g in (4, 2, 1) if depth % (g * LANES) == 0)
    shapes = [shape_of(rows, width, F32) for _, width in chunks]
    shapes += [shape_of(rows, width, BF16) for _, width in chunks[:narrow]]
    out = pl.pallas_call(
        functools.partial(in_kernel, chunks, narrow, groups),
        in_specs=[ANY_SPEC] * 4,
        out_specs=[VMEM_SPEC] * len(shapes),
        out_shape=shapes,
        scratch_shapes=[
            pltpu.VMEM((rows, depth), BF16),
            pltpu.VMEM((depth, total), BF16),
            pltpu.VMEM((rows, total), F32),
            pltpu.SemaphoreType.DMA((groups, 3)),
        ],
        compiler_params=pltpu.CompilerParams(vmem_limit_bytes=24 * MIB),
        cost_estimate=cost(2 * rows * depth * total, 2 * depth * total),
    )(in_hbm(act_train), in_hbm(act_query), in_hbm(basis_in), prev)
    return list(out[: len(chunks)]), list(out[len(chunks) :])


def out_kernel(steps, train_ref, query_ref, basis_ref, prev_ref, keep_ref, *refs):
    give_refs = refs[:-4]
    rows_ref, slot_ref, acc_ref, sems = refs[-4:]
    tokens, queries = train_ref.shape[0], query_ref.shape[0]
    slots, block = slot_ref.shape[0], slot_ref.shape[1]
    half = keep_ref.shape[0]

    def copies(step):
        slot = lax.rem(step, slots)
        part = pl.ds(pl.multiple_of(step * block, block), block)
        return [
            pltpu.make_async_copy(basis_ref.at[part, :], slot_ref.at[slot], sems.at[slot, 0]),
            pltpu.make_async_copy(
                train_ref.at[:, part], rows_ref.at[slot, pl.ds(0, tokens), :], sems.at[slot, 1]
            ),
            pltpu.make_async_copy(
                query_ref.at[:, part], rows_ref.at[slot, pl.ds(tokens, queries), :], sems.at[slot, 2]
            ),
        ]

    for step in range(min(slots - 1, steps)):
        for copy in copies(step):
            copy.start()
    acc_ref[...] = jnp.zeros_like(acc_ref)

    def body(step, carry):
        for copy in copies(step):
            copy.wait()

        @pl.when(step + slots - 1 < steps)
        def _():
            for copy in copies(step + slots - 1):
                copy.start()

        slot = lax.rem(step, slots)
        for h, part in enumerate(halves_dot(rows_ref[slot], slot_ref[slot])):
            acc_ref[h * half : (h + 1) * half, :] += part
        return carry

    lax.fori_loop(0, steps, body, 0)
    odd = lax.rem(lax.axis_index("col"), 2)
    keep_ref[...] = acc_ref[pl.ds(pl.multiple_of(odd * half, 16), half), :]
    cols = give_refs[0].shape[1]
    for c, give_ref in enumerate(give_refs):
        span = slice(c * cols, (c + 1) * cols)
        give_ref[...] = acc_ref[pl.ds(pl.multiple_of((1 - odd) * half, 16), half), span]


def out_part(grad_train, grad_query, basis_out, prev):
    tokens, depth = grad_train.shape
    width = basis_out.shape[1]
    rows = tokens + grad_query.shape[0]
    block = largest_divisor(depth, (512, 256, 128))
    slots = 4
    pieces = pieces_of(width, 2)
    out_shape = [shape_of(rows // 2, width, F32)]
    out_shape += [shape_of(rows // 2, width // pieces, F32)] * pieces
    return pl.pallas_call(
        functools.partial(out_kernel, depth // block),
        in_specs=[ANY_SPEC] * 4,
        out_specs=[VMEM_SPEC] * (1 + pieces),
        out_shape=out_shape,
        scratch_shapes=[
            pltpu.VMEM((slots, rows, block), BF16),
            pltpu.VMEM((slots, block, width), BF16),
            pltpu.VMEM((rows, width), F32),
            pltpu.SemaphoreType.DMA((slots, 3)),
        ],
        compiler_params=pltpu.CompilerParams(vmem_limit_bytes=24 * MIB),
        cost_estimate=cost(2 * rows * depth * width, 2 * depth * (rows + width)),
    )(in_hbm(grad_train), in_hbm(grad_query), in_hbm(basis_out), prev)


def add_kernel(pieces, outs, handed, keep_ref, *refs):
    wide_ref, narrow_refs = refs[pieces + handed + 1], refs[pieces + handed + 2 :][:outs]
    width = keep_ref.shape[1]
    cols = width // pieces
    for c in range(pieces):
        span = slice(c * cols, (c + 1) * cols)
        wide_ref[:, span] = keep_ref[:, span] + refs[c][...].astype(F32)
    cols = width // outs
    for c in range(outs):
        narrow_refs[c][...] = wide_ref[:, c * cols : (c + 1) * cols].astype(BF16)


def add_part(keep, got, prev, outs=1, handed=()):
    rows, width = keep.shape
    got, handed = list(got), list(handed)
    out = pl.pallas_call(
        functools.partial(add_kernel, len(got), outs, len(handed)),
        in_specs=[VMEM_SPEC] * (1 + len(got)) + [ANY_SPEC] * (len(handed) + 1),
        out_specs=[VMEM_SPEC] * (1 + outs) + [ANY_SPEC] * len(handed),
        out_shape=[shape_of(rows, width, F32)]
        + [shape_of(rows, width // outs, BF16)] * outs
        + [shape_of(*x.shape, x.dtype) for x in handed],
        input_output_aliases={1 + len(got) + i: 1 + outs + i for i in range(len(handed))},
        compiler_params=pltpu.CompilerParams(vmem_limit_bytes=12 * MIB),
        cost_estimate=cost(1024, 1024),
    )(keep, *got, *handed, prev)
    return out[0], list(out[1 : 1 + outs]), list(out[1 + outs :])


def join_kernel(tokens, pieces, corr_ref, prev_ref, *refs):
    mine_refs, other_refs = refs[:pieces], refs[pieces : 2 * pieces]
    gt_ref, gq_ref, inv_ref, sem = refs[2 * pieces :]
    fetch = pltpu.make_async_copy(corr_ref.at[:, pl.ds(0, inv_ref.shape[1])], inv_ref, sem)
    fetch.start()
    odd = lax.rem(lax.axis_index("col"), 2)
    for c, (mine_ref, other_ref) in enumerate(zip(mine_refs, other_refs)):
        mine, other = mine_ref[...].astype(F32), other_ref[...].astype(F32)
        low = jnp.where(odd == 1, other, mine)
        high = jnp.where(odd == 1, mine, other)
        rows = jnp.concatenate([low, high], axis=0)
        cols = rows.shape[1]
        gt_ref[:, c * cols : (c + 1) * cols] = rows[:tokens].astype(BF16)
        gq_ref[c * cols : (c + 1) * cols, :] = rows[tokens:].T.astype(BF16)
    fetch.wait()
    inv_ref[...] = 1.0 / inv_ref[...]


def join_part(mine, other, correction, prev, tokens, first):
    half = mine[0].shape[0]
    width = sum(x.shape[1] for x in mine)
    queries = 2 * half - tokens
    return pl.pallas_call(
        functools.partial(join_kernel, tokens, len(mine)),
        in_specs=[ANY_SPEC, ANY_SPEC] + [VMEM_SPEC] * (2 * len(mine)),
        out_specs=[VMEM_SPEC] * 3,
        out_shape=[
            shape_of(tokens, width, BF16),
            shape_of(width, queries, BF16),
            shape_of(width, first, F32),
        ],
        scratch_shapes=[pltpu.SemaphoreType.DMA],
        compiler_params=pltpu.CompilerParams(vmem_limit_bytes=12 * MIB),
        cost_estimate=cost(1024, 1024),
    )(in_hbm(correction), prev, *mine, *other)


def at_end():
    me = lax.axis_index("row")
    return (me == 0) | (me == lax.axis_size("row") - 1)


def pay_kernel(has_part, acc_ref, got_ref, *refs):
    total = acc_ref[...] + got_ref[...].astype(F32)
    if has_part:
        total = jnp.where(at_end(), refs[0][...], total)
    refs[-1][...] = total.astype(BF16)


def pay_part(acc, got, part, prev):
    has_part = part is not None
    return pl.pallas_call(
        functools.partial(pay_kernel, has_part),
        in_specs=[VMEM_SPEC, VMEM_SPEC] + [VMEM_SPEC] * has_part + [ANY_SPEC],
        out_specs=VMEM_SPEC,
        out_shape=shape_of(*acc.shape, BF16),
        compiler_params=pltpu.CompilerParams(vmem_limit_bytes=12 * MIB),
        cost_estimate=cost(1024, 1024),
    )(acc, got, *([part] if has_part else []), prev)


def score_kernel(
    start, scale, outs, following, gt_ref, gq_ref, inv_ref, sent_ref, got_ref, corr_ref, prev_ref,
    order_ref, *refs
):
    out_refs, next_refs = refs[:outs], refs[outs:-4]
    quot_ref, wide_ref, own_ref, sem = refs[-4:]
    tokens = gt_ref.shape[0]
    queries = gq_ref.shape[1]
    width = inv_ref.shape[1]
    if following is not None:
        fetch = pltpu.make_async_copy(corr_ref.at[:, pl.ds(*following)], next_refs[0], sem)
        fetch.start()
    total = jnp.where(at_end(), got_ref[...].astype(F32), sent_ref[...].astype(F32))
    wide_ref[...] = total[:tokens]
    own_ref[...] = total[tokens:]
    owner = lax.broadcasted_iota(jnp.int32, (queries, width), 0) // LQ
    lane = lax.broadcasted_iota(jnp.int32, (tokens, LANES), 1)

    def quotient(q):
        own = jnp.where(owner == q, own_ref[...], 0.0).astype(BF16)
        products = jnp.dot(gq_ref[...], own, preferred_element_type=F32)
        quot_ref[q % 2] = (products * inv_ref[...]).astype(BF16)

    quotient(0)
    result = jnp.zeros((tokens, LANES), F32) if start else prev_ref[...]
    for q in range(NQ):
        if q + 1 < NQ:
            quotient(q + 1)
        elif following is not None:
            fetch.wait()
            next_refs[0][...] = 1.0 / next_refs[0][...]
        mapped = jnp.dot(gt_ref[...], quot_ref[q % 2], preferred_element_type=F32)
        scaled = mapped * wide_ref[...]
        folded = scaled[:, :LANES]
        for part in range(1, width // LANES):
            folded = folded + scaled[:, part * LANES : (part + 1) * LANES]
        result = result + jnp.where(lane == q, jnp.sum(folded, axis=1, keepdims=True), 0.0)
    if scale is None:
        out_refs[0][...] = result
        return
    final = (result * scale).T[:NQ]
    if outs == 1:
        out_refs[0][...] = final
    else:
        split(final, lax.axis_index("row") // 2, *out_refs)


def split(values, high, keep_ref, give_ref):
    cols = values.shape[1] // 2
    low_half, high_half = values[:, :cols], values[:, cols:]
    keep_ref[...] = jnp.where(high == 1, high_half, low_half)
    give_ref[...] = jnp.where(high == 1, low_half, high_half)


def score_part(
    rot_gt, rot_gq_t, correction, inv, sent, got, prev, order, start, scale, halves, following
):
    tokens, outs = rot_gt.shape
    width = inv.shape[1]
    queries = rot_gq_t.shape[1]
    if scale is None:
        out_shape = [shape_of(tokens, LANES, F32)]
    elif halves:
        out_shape = [shape_of(NQ, tokens // 2, F32)] * 2
    else:
        out_shape = [shape_of(NQ, tokens, F32)]
    count = len(out_shape)
    if following is not None:
        out_shape.append(shape_of(outs, following[1], F32))
    out = pl.pallas_call(
        functools.partial(score_kernel, start, scale, count, following),
        in_specs=[VMEM_SPEC] * 5 + [ANY_SPEC, ANY_SPEC if start else VMEM_SPEC, ANY_SPEC],
        out_specs=[VMEM_SPEC] * len(out_shape),
        out_shape=out_shape,
        scratch_shapes=[
            pltpu.VMEM((2, outs, width), BF16),
            pltpu.VMEM((tokens, width), F32),
            pltpu.VMEM((queries, width), F32),
            pltpu.SemaphoreType.DMA,
        ],
        compiler_params=pltpu.CompilerParams(vmem_limit_bytes=16 * MIB),
        cost_estimate=cost(2 * NQ * outs * width * (tokens + queries), 4 * outs * width),
    )(rot_gt, rot_gq_t, inv, sent, got, in_hbm(correction), prev, order)
    return list(out[:count]), out[-1]


def halve_kernel(keep_ref, got_ref, *refs):
    total = keep_ref[...] + got_ref[...]
    if len(refs) == 1:
        refs[0][...] = total
    else:
        split(total, lax.rem(lax.axis_index("row"), 2), *refs)


def halve_part(keep, got, halves):
    rows, width = keep.shape
    out = [shape_of(rows, width // 2, F32)] * 2 if halves else [shape_of(rows, width, F32)]
    return pl.pallas_call(
        halve_kernel,
        in_specs=[VMEM_SPEC] * 2,
        out_specs=[VMEM_SPEC] * len(out),
        out_shape=out,
        cost_estimate=cost(1024, 1024),
    )(keep, got)


def line_sum(partial, axis):
    n = lax.axis_size(axis)
    half = n // 2
    me = lax.axis_index(axis)
    if n % 2:
        return lax.psum(partial, axis).astype(BF16)
    acc = partial
    for s in range(half - 1):
        pairs = [(s, s + 1), (n - 1 - s, n - 2 - s)]
        acc = acc + lax.ppermute(acc.astype(BF16), axis, pairs).astype(F32)
    got = lax.ppermute(acc.astype(BF16), axis, [(half - 1, half), (half, half - 1)])
    total = (acc + got.astype(F32)).astype(BF16)
    for s in range(half - 2, -1, -1):
        pairs = [(s + 1, s), (n - 2 - s, n - 1 - s)]
        got = lax.ppermute(total, axis, pairs)
        total = jnp.where((me == s) | (me == n - 1 - s), got, total)
    return total


def owned_sum(partial, axis):
    n = lax.axis_size(axis)
    me = lax.axis_index(axis)
    total = lax.dynamic_index_in_dim(partial, me, 0, keepdims=False)
    for step in range(1, n):
        block = lax.dynamic_index_in_dim(partial, (me + step) % n, 0, keepdims=False)
        total = total + lax.ppermute(block, axis, [(d, (d + step) % n) for d in range(n)])
    return total


def shared_sum(partial, axis):
    n = lax.axis_size(axis)
    total = partial
    for step in range(1, n):
        total = total + lax.ppermute(partial, axis, [(d, (d + step) % n) for d in range(n)])
    return total


def on_device(act_train, act_query, grad_train, grad_query, basis_in, basis_out, correction):
    norm_scale = (O * I * LQ) ** (-0.5)
    tokens = act_train.shape[0]
    n_row, n_col = lax.axis_size("row"), lax.axis_size("col")
    chunks = chunk_list(basis_in.shape[1])
    count = len(chunks)
    line = n_row == 4
    flip = [(d, d ^ 1) for d in range(n_col)]
    outer = [(0, 1), (1, 0), (2, 3), (3, 2)]
    inner = []
    for c in range(n_col):
        inner += [(n_col + c, 2 * n_col + c), (2 * n_col + c, n_col + c)]
        inner += [(c, c ^ 1), (3 * n_col + c, 3 * n_col + (c ^ 1))]
    sent, got, acc, got_mid = {}, {}, {}, {}

    def swap(j, payload):
        sent[j] = payload
        got[j] = lax.ppermute(payload, "row", outer)

    def meet(j, prev, handed=()):
        if not line or j >= count:
            return prev, list(handed)
        acc[j], (thin,), handed = add_part(parts[j], [got[j]], prev, 1, handed)
        got_mid[j] = lax.ppermute(thin, ("row", "col"), inner)
        return thin, handed

    def pay(j, prev):
        if not line:
            sent[j + LAG] = got[j + LAG] = line_sum(parts[j], "row")
            return prev
        part = parts[j + LAG] if j + LAG < count else None
        payload = pay_part(acc[j], got_mid[j], part, prev)
        swap(j + LAG, payload)
        return payload

    parts, narrow = in_part(act_train, act_query, basis_in, act_query, chunks[:LAG], LAG)
    if line:
        for j in range(LAG):
            swap(j, narrow[j])
    keep, *give = out_part(grad_train, grad_query, basis_out, parts[-1])
    prev, _ = meet(0, keep)
    prev, give = meet(1, prev, give)
    given = [lax.ppermute(piece, "col", flip) for piece in give]
    more, _ = in_part(act_train, act_query, basis_in, prev, chunks[LAG:], 0)
    parts += more
    prev = pay(0, more[-1])
    prev, _ = meet(2, prev)
    outs = pieces_of(keep.shape[1], 2)
    wide, thin, _ = add_part(keep, given, prev, outs)
    prev, bit = wide, 2
    while bit < n_col:
        other = [lax.ppermute(x, "col", [(d, d ^ bit) for d in range(n_col)]) for x in thin]
        if bit == 2:
            prev = pay(1, prev)
            prev, _ = meet(3, prev)
            prev = pay(2, prev)
        wide, thin, _ = add_part(wide, other, prev, outs)
        prev = wide
        bit *= 2
    other = [lax.ppermute(x, "col", flip) for x in thin]
    prev, _ = meet(4, prev)
    prev = pay(3, prev)
    rot_gt, rot_gq_t, inv = join_part(thin, other, correction, prev, tokens, chunks[0][1])
    halves = n_row == 4 and n_col & (n_col - 1) == 0 and tokens % (n_row * LANES) == 0
    sums = [rot_gt]
    done = 0
    for j in range(4, count + LAG):
        for k in range(done, min(j - LAG + 1, done + 2, count)):
            sums, inv = score_part(
                rot_gt, rot_gq_t, correction, inv, sent[k + LAG], got[k + LAG], sums[0], prev,
                k == 0, norm_scale if k == count - 1 else None, halves,
                chunks[k + 1] if k + 1 < count else None,
            )
            done = k + 1
        if j < count:
            prev, _ = meet(j + 1, sums[0])
            prev = pay(j, prev)
    if not halves:
        blocks = sums[0].reshape(NQ, n_row, tokens // n_row).transpose(1, 0, 2)
        return shared_sum(owned_sum(blocks, "row"), "col")
    keep, give = sums
    swapped = lax.ppermute(give, "row", [(d, d ^ 2) for d in range(n_row)])
    keep, give = halve_part(keep, swapped, True)
    (keep,) = halve_part(keep, lax.ppermute(give, "row", outer), False)
    bit = 1
    while bit < n_col:
        swapped = lax.ppermute(keep, "col", [(d, d ^ bit) for d in range(n_col)])
        (keep,) = halve_part(keep, swapped, False)
        bit *= 2
    return keep


def solution(mesh):
    in_specs = (
        P("groups", "row"),
        P("groups", "row"),
        P("groups", "col"),
        P("groups", "col"),
        P(("groups", "row"), "col"),
        P(("groups", "col"), "row"),
        P(("groups", "row"), "col"),
    )
    out_specs = P("groups", "row")
    return jax.shard_map(
        on_device, mesh=mesh, in_specs=in_specs, out_specs=out_specs, check_vma=False
    )
```

```python
import functools

import jax
import jax.numpy as jnp
from jax import lax
from jax.experimental import pallas as pl
from jax.experimental.pallas import tpu as pltpu
from jax.sharding import PartitionSpec as P

I = 8192
O = 4096
NQ = 8
LQ = 16
LANES = 128
CHUNKS = 8
LAG = 3
F32 = jnp.float32
BF16 = jnp.bfloat16
MIB = 1 << 20

VMEM_SPEC = pl.BlockSpec(memory_space=pltpu.VMEM)
SMEM_SPEC = pl.BlockSpec(memory_space=pltpu.SMEM)
ANY_SPEC = pl.BlockSpec(memory_space=pl.ANY)


def shape_of(rows, width, dtype):
    return jax.ShapeDtypeStruct((rows, width), dtype)


def chunk_list(size):
    tiles = size // LANES
    count = min(CHUNKS, tiles)
    chunks, first = [], 0
    for k in range(count):
        width = LANES * (tiles // count + (1 if k < tiles % count else 0))
        chunks.append((first, width))
        first += width
    return chunks


def largest_divisor(size, choices):
    for choice in choices:
        if size % choice == 0:
            return choice
    return size


def pieces_of(width, most):
    return max(p for p in range(1, most + 1) if width % (p * LANES) == 0)


def cost(flops, bytes_accessed):
    return pl.CostEstimate(flops=flops, bytes_accessed=bytes_accessed, transcendentals=0)


def in_hbm(x):
    return pltpu.with_memory_space_constraint(x, pltpu.HBM)


def halves_dot(rows, basis):
    half = rows.shape[0] // 2
    return [jnp.dot(part, basis, preferred_element_type=F32) for part in (rows[:half], rows[half:])]


def in_kernel(chunks, narrow, groups, train_ref, query_ref, basis_ref, prev_ref, *refs):
    count = len(chunks)
    rows_ref, slot_ref, sum_ref, sems = refs[count + narrow :]
    tokens, queries = train_ref.shape[0], query_ref.shape[0]
    start, total = chunks[0][0], slot_ref.shape[1]
    depth = basis_ref.shape[0] // groups
    copies = []
    for g in range(groups):
        part = pl.ds(g * depth, depth)
        copies.append([
            pltpu.make_async_copy(
                basis_ref.at[part, pl.ds(start, total)], slot_ref.at[part, :], sems.at[g, 0]
            ),
            pltpu.make_async_copy(
                train_ref.at[:, part], rows_ref.at[pl.ds(0, tokens), part], sems.at[g, 1]
            ),
            pltpu.make_async_copy(
                query_ref.at[:, part], rows_ref.at[pl.ds(tokens, queries), part], sems.at[g, 2]
            ),
        ])
    for group in copies:
        for copy in group:
            copy.start()
    for g, group in enumerate(copies):
        for copy in group:
            copy.wait()
        part = slice(g * depth, (g + 1) * depth)
        half = rows_ref.shape[0] // 2
        for h, value in enumerate(halves_dot(rows_ref[:, part], slot_ref[part, :])):
            span = slice(h * half, (h + 1) * half)
            if g == 0:
                sum_ref[span, :] = value
            else:
                sum_ref[span, :] += value
    for j, (first, width) in enumerate(chunks):
        value = sum_ref[:, first - start : first - start + width]
        refs[j][...] = value
        if j < narrow:
            refs[count + j][...] = value.astype(BF16)


def in_part(act_train, act_query, basis_in, prev, chunks, narrow):
    tokens, depth = act_train.shape
    rows = tokens + act_query.shape[0]
    total = sum(width for _, width in chunks)
    groups = next(g for g in (4, 2, 1) if depth % (g * LANES) == 0)
    shapes = [shape_of(rows, width, F32) for _, width in chunks]
    shapes += [shape_of(rows, width, BF16) for _, width in chunks[:narrow]]
    out = pl.pallas_call(
        functools.partial(in_kernel, chunks, narrow, groups),
        in_specs=[ANY_SPEC] * 4,
        out_specs=[VMEM_SPEC] * len(shapes),
        out_shape=shapes,
        scratch_shapes=[
            pltpu.VMEM((rows, depth), BF16),
            pltpu.VMEM((depth, total), BF16),
            pltpu.VMEM((rows, total), F32),
            pltpu.SemaphoreType.DMA((groups, 3)),
        ],
        compiler_params=pltpu.CompilerParams(vmem_limit_bytes=24 * MIB),
        cost_estimate=cost(2 * rows * depth * total, 2 * depth * total),
    )(in_hbm(act_train), in_hbm(act_query), in_hbm(basis_in), prev)
    return list(out[: len(chunks)]), list(out[len(chunks) :])


def out_kernel(begin, steps, last, train_ref, query_ref, basis_ref, prev_ref, *refs):
    if last:
        start_ref, keep_ref, *give_refs, rows_ref, slot_ref, acc_ref, sems = refs
    else:
        acc_ref, rows_ref, slot_ref, sems = refs
    tokens, queries = train_ref.shape[0], query_ref.shape[0]
    slots, block = slot_ref.shape[0], slot_ref.shape[1]
    half = acc_ref.shape[0] // 2

    def copies(step):
        slot = lax.rem(step, slots)
        part = pl.ds(pl.multiple_of((begin + step) * block, block), block)
        return [
            pltpu.make_async_copy(basis_ref.at[part, :], slot_ref.at[slot], sems.at[slot, 0]),
            pltpu.make_async_copy(
                train_ref.at[:, part], rows_ref.at[slot, pl.ds(0, tokens), :], sems.at[slot, 1]
            ),
            pltpu.make_async_copy(
                query_ref.at[:, part], rows_ref.at[slot, pl.ds(tokens, queries), :], sems.at[slot, 2]
            ),
        ]

    for step in range(min(slots - 1, steps)):
        for copy in copies(step):
            copy.start()
    acc_ref[...] = start_ref[...] if last else jnp.zeros_like(acc_ref)

    def body(step, carry):
        for copy in copies(step):
            copy.wait()

        @pl.when(step + slots - 1 < steps)
        def _():
            for copy in copies(step + slots - 1):
                copy.start()

        slot = lax.rem(step, slots)
        for h, part in enumerate(halves_dot(rows_ref[slot], slot_ref[slot])):
            acc_ref[h * half : (h + 1) * half, :] += part
        return carry

    lax.fori_loop(0, steps, body, 0)
    if not last:
        return
    odd = lax.rem(lax.axis_index("col"), 2)
    keep_ref[...] = acc_ref[pl.ds(pl.multiple_of(odd * half, 16), half), :]
    cols = give_refs[0].shape[1]
    for c, give_ref in enumerate(give_refs):
        span = slice(c * cols, (c + 1) * cols)
        give_ref[...] = acc_ref[pl.ds(pl.multiple_of((1 - odd) * half, 16), half), span]


def out_part(grad_train, grad_query, basis_out, prev, acc):
    tokens, depth = grad_train.shape
    width = basis_out.shape[1]
    rows = tokens + grad_query.shape[0]
    block = largest_divisor(depth, (512, 256, 128))
    steps = depth // block
    slots = 4
    last = acc is not None
    begin, count = (steps // 2, steps - steps // 2) if last else (0, steps // 2)
    pieces = pieces_of(width, 2)
    if last:
        out_shape = [shape_of(rows // 2, width, F32)]
        out_shape += [shape_of(rows // 2, width // pieces, F32)] * pieces
    else:
        out_shape = [shape_of(rows, width, F32)]
    return pl.pallas_call(
        functools.partial(out_kernel, begin, count, last),
        in_specs=[ANY_SPEC] * 4 + [VMEM_SPEC] * last,
        out_specs=[VMEM_SPEC] * len(out_shape),
        out_shape=out_shape,
        scratch_shapes=[
            pltpu.VMEM((slots, rows, block), BF16),
            pltpu.VMEM((slots, block, width), BF16),
        ]
        + [pltpu.VMEM((rows, width), F32)] * last
        + [pltpu.SemaphoreType.DMA((slots, 3))],
        compiler_params=pltpu.CompilerParams(vmem_limit_bytes=20 * MIB),
        cost_estimate=cost(2 * rows * block * count * width, 2 * block * count * (rows + width)),
    )(
        in_hbm(grad_train), in_hbm(grad_query), in_hbm(basis_out), prev, *([acc] if last else [])
    )


def add_kernel(pieces, outs, handed, keep_ref, *refs):
    wide_ref, narrow_refs = refs[pieces + handed + 1], refs[pieces + handed + 2 :][:outs]
    width = keep_ref.shape[1]
    cols = width // pieces
    for c in range(pieces):
        span = slice(c * cols, (c + 1) * cols)
        wide_ref[:, span] = keep_ref[:, span] + refs[c][...].astype(F32)
    cols = width // outs
    for c in range(outs):
        narrow_refs[c][...] = wide_ref[:, c * cols : (c + 1) * cols].astype(BF16)


def add_part(keep, got, prev, outs=1, handed=()):
    rows, width = keep.shape
    got, handed = list(got), list(handed)
    out = pl.pallas_call(
        functools.partial(add_kernel, len(got), outs, len(handed)),
        in_specs=[VMEM_SPEC] * (1 + len(got)) + [ANY_SPEC] * (len(handed) + 1),
        out_specs=[VMEM_SPEC] * (1 + outs) + [ANY_SPEC] * len(handed),
        out_shape=[shape_of(rows, width, F32)]
        + [shape_of(rows, width // outs, BF16)] * outs
        + [shape_of(*x.shape, x.dtype) for x in handed],
        input_output_aliases={1 + len(got) + i: 1 + outs + i for i in range(len(handed))},
        compiler_params=pltpu.CompilerParams(vmem_limit_bytes=12 * MIB),
        cost_estimate=cost(1024, 1024),
    )(keep, *got, *handed, prev)
    return out[0], list(out[1 : 1 + outs]), list(out[1 + outs :])


def join_kernel(tokens, pieces, prev_ref, *refs):
    mine_refs, other_refs = refs[:pieces], refs[pieces : 2 * pieces]
    gt_ref, gq_ref = refs[2 * pieces :]
    odd = lax.rem(lax.axis_index("col"), 2)
    for c, (mine_ref, other_ref) in enumerate(zip(mine_refs, other_refs)):
        mine, other = mine_ref[...].astype(F32), other_ref[...].astype(F32)
        low = jnp.where(odd == 1, other, mine)
        high = jnp.where(odd == 1, mine, other)
        rows = jnp.concatenate([low, high], axis=0)
        cols = rows.shape[1]
        gt_ref[:, c * cols : (c + 1) * cols] = rows[:tokens].astype(BF16)
        gq_ref[c * cols : (c + 1) * cols, :] = rows[tokens:].T.astype(BF16)


def join_part(mine, other, prev, tokens):
    half = mine[0].shape[0]
    width = sum(x.shape[1] for x in mine)
    queries = 2 * half - tokens
    return pl.pallas_call(
        functools.partial(join_kernel, tokens, len(mine)),
        in_specs=[ANY_SPEC] + [VMEM_SPEC] * (2 * len(mine)),
        out_specs=[VMEM_SPEC] * 2,
        out_shape=[shape_of(tokens, width, BF16), shape_of(width, queries, BF16)],
        compiler_params=pltpu.CompilerParams(vmem_limit_bytes=12 * MIB),
        cost_estimate=cost(1024, 1024),
    )(prev, *mine, *other)


def inverse_kernel(chunks, corr_ref, prev_ref, *refs):
    *inv_refs, slot_ref, sems = refs
    slots, block = slot_ref.shape[0], slot_ref.shape[1]
    steps = corr_ref.shape[0] // block

    def fetch(step):
        rows = pl.ds(step * block, block)
        return pltpu.make_async_copy(
            corr_ref.at[rows, :], slot_ref.at[step % slots], sems.at[step % slots]
        )

    for step in range(min(slots, steps)):
        fetch(step).start()
    for step in range(steps):
        fetch(step).wait()
        for (first, width), inv_ref in zip(chunks, inv_refs):
            value = slot_ref[step % slots, :, first : first + width]
            inv_ref[step * block : (step + 1) * block, :] = 1.0 / value
        if step + slots < steps:
            fetch(step + slots).start()


def inverse_part(correction, prev, chunks):
    rows, width = correction.shape
    block = largest_divisor(rows, (128, 64, 8))
    out = pl.pallas_call(
        functools.partial(inverse_kernel, chunks),
        in_specs=[ANY_SPEC, ANY_SPEC],
        out_specs=[VMEM_SPEC] * len(chunks),
        out_shape=[shape_of(rows, width, F32) for _, width in chunks],
        scratch_shapes=[pltpu.VMEM((4, block, width), F32), pltpu.SemaphoreType.DMA((4,))],
        compiler_params=pltpu.CompilerParams(vmem_limit_bytes=16 * MIB),
        cost_estimate=cost(1024, 1024),
    )(in_hbm(correction), prev)
    return list(out)


def at_end():
    me = lax.axis_index("row")
    return (me == 0) | (me == lax.axis_size("row") - 1)


def pay_kernel(has_part, acc_ref, got_ref, *refs):
    total = acc_ref[...] + got_ref[...].astype(F32)
    if has_part:
        total = jnp.where(at_end(), refs[0][...], total)
    refs[-1][...] = total.astype(BF16)


def pay_part(acc, got, part, prev, hint):
    has_part = part is not None
    return pl.pallas_call(
        functools.partial(pay_kernel, has_part),
        in_specs=[VMEM_SPEC, VMEM_SPEC] + [VMEM_SPEC] * has_part + [ANY_SPEC],
        out_specs=VMEM_SPEC,
        out_shape=shape_of(*acc.shape, BF16),
        compiler_params=pltpu.CompilerParams(vmem_limit_bytes=12 * MIB),
        cost_estimate=cost(hint, 1024),
    )(acc, got, *([part] if has_part else []), prev)


def score_kernel(
    start, scale, outs, gt_ref, gq_ref, inv_ref, sent_ref, got_ref, prev_ref, order_ref, *refs
):
    out_refs = refs[:outs]
    quot_ref, wide_ref, own_ref = refs[outs:]
    tokens = gt_ref.shape[0]
    queries = gq_ref.shape[1]
    width = inv_ref.shape[1]
    total = jnp.where(at_end(), got_ref[...].astype(F32), sent_ref[...].astype(F32))
    wide_ref[...] = total[:tokens]
    own_ref[...] = total[tokens:]
    owner = lax.broadcasted_iota(jnp.int32, (queries, width), 0) // LQ
    lane = lax.broadcasted_iota(jnp.int32, (tokens, LANES), 1)

    def quotient(q):
        own = jnp.where(owner == q, own_ref[...], 0.0).astype(BF16)
        products = jnp.dot(gq_ref[...], own, preferred_element_type=F32)
        quot_ref[q % 2] = (products * inv_ref[...]).astype(BF16)

    quotient(0)
    result = jnp.zeros((tokens, LANES), F32) if start else prev_ref[...]
    for q in range(NQ):
        if q + 1 < NQ:
            quotient(q + 1)
        mapped = jnp.dot(gt_ref[...], quot_ref[q % 2], preferred_element_type=F32)
        scaled = mapped * wide_ref[...]
        folded = scaled[:, :LANES]
        for part in range(1, width // LANES):
            folded = folded + scaled[:, part * LANES : (part + 1) * LANES]
        result = result + jnp.where(lane == q, jnp.sum(folded, axis=1, keepdims=True), 0.0)
    if scale is None:
        out_refs[0][...] = result
        return
    final = (result * scale).T[:NQ]
    if outs == 1:
        out_refs[0][...] = final
    else:
        split(final, lax.axis_index("row") // 2, *out_refs)


def split(values, high, keep_ref, give_ref):
    cols = values.shape[1] // 2
    low_half, high_half = values[:, :cols], values[:, cols:]
    keep_ref[...] = jnp.where(high == 1, high_half, low_half)
    give_ref[...] = jnp.where(high == 1, low_half, high_half)


def score_part(rot_gt, rot_gq_t, inv, sent, got, prev, order, start, scale, halves):
    tokens, outs = rot_gt.shape
    width = inv.shape[1]
    queries = rot_gq_t.shape[1]
    if scale is None:
        out_shape = [shape_of(tokens, LANES, F32)]
    elif halves:
        out_shape = [shape_of(NQ, tokens // 2, F32)] * 2
    else:
        out_shape = [shape_of(NQ, tokens, F32)]
    return pl.pallas_call(
        functools.partial(score_kernel, start, scale, len(out_shape)),
        in_specs=[VMEM_SPEC] * 5 + [ANY_SPEC if start else VMEM_SPEC, ANY_SPEC],
        out_specs=[VMEM_SPEC] * len(out_shape),
        out_shape=out_shape,
        scratch_shapes=[
            pltpu.VMEM((2, outs, width), BF16),
            pltpu.VMEM((tokens, width), F32),
            pltpu.VMEM((queries, width), F32),
        ],
        compiler_params=pltpu.CompilerParams(vmem_limit_bytes=16 * MIB),
        cost_estimate=cost(2 * NQ * outs * width * (tokens + queries), 4 * outs * width),
    )(rot_gt, rot_gq_t, inv, sent, got, prev, order)


def halve_kernel(keep_ref, got_ref, *refs):
    total = keep_ref[...] + got_ref[...]
    if len(refs) == 1:
        refs[0][...] = total
    else:
        split(total, lax.rem(lax.axis_index("row"), 2), *refs)


def halve_part(keep, got, halves):
    rows, width = keep.shape
    out = [shape_of(rows, width // 2, F32)] * 2 if halves else [shape_of(rows, width, F32)]
    return pl.pallas_call(
        halve_kernel,
        in_specs=[VMEM_SPEC] * 2,
        out_specs=[VMEM_SPEC] * len(out),
        out_shape=out,
        compiler_params=pltpu.CompilerParams(vmem_limit_bytes=4 * MIB),
        cost_estimate=cost(1024, 1024),
    )(keep, got)


def line_sum(partial, axis):
    n = lax.axis_size(axis)
    half = n // 2
    me = lax.axis_index(axis)
    if n % 2:
        return lax.psum(partial, axis).astype(BF16)
    acc = partial
    for s in range(half - 1):
        pairs = [(s, s + 1), (n - 1 - s, n - 2 - s)]
        acc = acc + lax.ppermute(acc.astype(BF16), axis, pairs).astype(F32)
    got = lax.ppermute(acc.astype(BF16), axis, [(half - 1, half), (half, half - 1)])
    total = (acc + got.astype(F32)).astype(BF16)
    for s in range(half - 2, -1, -1):
        pairs = [(s + 1, s), (n - 2 - s, n - 1 - s)]
        got = lax.ppermute(total, axis, pairs)
        total = jnp.where((me == s) | (me == n - 1 - s), got, total)
    return total


def owned_sum(partial, axis):
    n = lax.axis_size(axis)
    me = lax.axis_index(axis)
    total = lax.dynamic_index_in_dim(partial, me, 0, keepdims=False)
    for step in range(1, n):
        block = lax.dynamic_index_in_dim(partial, (me + step) % n, 0, keepdims=False)
        total = total + lax.ppermute(block, axis, [(d, (d + step) % n) for d in range(n)])
    return total


def shared_sum(partial, axis):
    n = lax.axis_size(axis)
    total = partial
    for step in range(1, n):
        total = total + lax.ppermute(partial, axis, [(d, (d + step) % n) for d in range(n)])
    return total


def on_device(act_train, act_query, grad_train, grad_query, basis_in, basis_out, correction):
    norm_scale = (O * I * LQ) ** (-0.5)
    tokens = act_train.shape[0]
    n_row, n_col = lax.axis_size("row"), lax.axis_size("col")
    chunks = chunk_list(basis_in.shape[1])
    count = len(chunks)
    line = n_row == 4
    flip = [(d, d ^ 1) for d in range(n_col)]
    outer = [(0, 1), (1, 0), (2, 3), (3, 2)]
    inner = []
    for c in range(n_col):
        inner += [(n_col + c, 2 * n_col + c), (2 * n_col + c, n_col + c)]
        inner += [(c, c ^ 1), (3 * n_col + c, 3 * n_col + (c ^ 1))]
    sent, got, acc, got_mid = {}, {}, {}, {}

    def swap(j, payload):
        sent[j] = payload
        got[j] = lax.ppermute(payload, "row", outer)

    def meet(j, prev, handed=()):
        if not line or j >= count:
            return prev, list(handed)
        acc[j], (thin,), handed = add_part(parts[j], [got[j]], prev, 1, handed)
        got_mid[j] = lax.ppermute(thin, ("row", "col"), inner)
        return thin, handed

    def pay(j, prev, hint=1024):
        if not line:
            sent[j + LAG] = got[j + LAG] = line_sum(parts[j], "row")
            return prev
        part = parts[j + LAG] if j + LAG < count else None
        payload = pay_part(acc[j], got_mid[j], part, prev, hint)
        swap(j + LAG, payload)
        return payload

    early = min(LAG + 2, count)
    parts, narrow = in_part(act_train, act_query, basis_in, act_query, chunks[:early], LAG)
    if line:
        for j in range(LAG):
            swap(j, narrow[j])
    (half_sum,) = out_part(grad_train, grad_query, basis_out, parts[-1], None)
    prev, _ = meet(0, half_sum)
    keep, *give = out_part(grad_train, grad_query, basis_out, prev, half_sum)
    prev, give = meet(1, keep, give)
    given = [lax.ppermute(piece, "col", flip) for piece in give]
    prev = pay(0, prev, 4 * 10**9)
    outs = pieces_of(keep.shape[1], 2)
    wide, thin, _ = add_part(keep, given, prev, outs)
    prev, bit = wide, 2
    while bit < n_col:
        other = [lax.ppermute(x, "col", [(d, d ^ bit) for d in range(n_col)]) for x in thin]
        if bit == 2:
            prev, _ = meet(2, prev)
            prev = pay(1, prev)
            more, _ = in_part(act_train, act_query, basis_in, prev, chunks[early:], 0)
            parts += more
            invs = inverse_part(correction, more[-1], chunks)
            prev, _ = meet(3, invs[0])
            prev = pay(2, prev)
        wide, thin, _ = add_part(wide, other, prev, outs)
        prev = wide
        bit *= 2
    other = [lax.ppermute(x, "col", flip) for x in thin]
    prev, _ = meet(4, prev)
    prev = pay(3, prev)
    rot_gt, rot_gq_t = join_part(thin, other, prev, tokens)
    halves = n_row == 4 and n_col & (n_col - 1) == 0 and tokens % (n_row * LANES) == 0
    sums = [rot_gt]
    done = 0
    for j in range(4, count + LAG):
        for k in range(done, min(j - LAG + 1, done + 2, count)):
            sums = score_part(
                rot_gt, rot_gq_t, invs[k], sent[k + LAG], got[k + LAG], sums[0], prev,
                k == 0, norm_scale if k == count - 1 else None, halves,
            )
            done = k + 1
        if j < count:
            prev, _ = meet(j + 1, sums[0])
            prev = pay(j, prev)
    if not halves:
        blocks = sums[0].reshape(NQ, n_row, tokens // n_row).transpose(1, 0, 2)
        return shared_sum(owned_sum(blocks, "row"), "col")
    keep, give = sums
    swapped = lax.ppermute(give, "row", [(d, d ^ 2) for d in range(n_row)])
    keep, give = halve_part(keep, swapped, True)
    (keep,) = halve_part(keep, lax.ppermute(give, "row", outer), False)
    bit = 1
    while bit < n_col:
        swapped = lax.ppermute(keep, "col", [(d, d ^ bit) for d in range(n_col)])
        (keep,) = halve_part(keep, swapped, False)
        bit *= 2
    return keep


def solution(mesh):
    in_specs = (
        P("groups", "row"),
        P("groups", "row"),
        P("groups", "col"),
        P("groups", "col"),
        P(("groups", "row"), "col"),
        P(("groups", "col"), "row"),
        P(("groups", "row"), "col"),
    )
    out_specs = P("groups", "row")
    return jax.shard_map(
        on_device, mesh=mesh, in_specs=in_specs, out_specs=out_specs, check_vma=False
    )
```

```python
import functools

import jax
import jax.numpy as jnp
from jax import lax
from jax.experimental import pallas as pl
from jax.experimental.pallas import tpu as pltpu
from jax.sharding import PartitionSpec as P

I = 8192
O = 4096
NQ = 8
LQ = 16
LANES = 128
CHUNKS = 8
LAG = 3
F32 = jnp.float32
BF16 = jnp.bfloat16
MIB = 1 << 20

VMEM_SPEC = pl.BlockSpec(memory_space=pltpu.VMEM)
SMEM_SPEC = pl.BlockSpec(memory_space=pltpu.SMEM)
ANY_SPEC = pl.BlockSpec(memory_space=pl.ANY)


def shape_of(rows, width, dtype):
    return jax.ShapeDtypeStruct((rows, width), dtype)


def chunk_list(size):
    tiles = size // LANES
    count = min(CHUNKS, tiles)
    chunks, first = [], 0
    for k in range(count):
        width = LANES * (tiles // count + (1 if k < tiles % count else 0))
        chunks.append((first, width))
        first += width
    return chunks


def largest_divisor(size, choices):
    for choice in choices:
        if size % choice == 0:
            return choice
    return size


def pieces_of(width, most):
    return max(p for p in range(1, most + 1) if width % (p * LANES) == 0)


def cost(flops, bytes_accessed):
    return pl.CostEstimate(flops=flops, bytes_accessed=bytes_accessed, transcendentals=0)


def in_hbm(x):
    return pltpu.with_memory_space_constraint(x, pltpu.HBM)


def halves_dot(rows, basis):
    half = rows.shape[0] // 2
    return [jnp.dot(part, basis, preferred_element_type=F32) for part in (rows[:half], rows[half:])]


def in_kernel(chunks, narrow, groups, train_ref, query_ref, basis_ref, prev_ref, *refs):
    count = len(chunks)
    rows_ref, slot_ref, sum_ref, sems = refs[count + narrow :]
    tokens, queries = train_ref.shape[0], query_ref.shape[0]
    start, total = chunks[0][0], slot_ref.shape[1]
    depth = basis_ref.shape[0] // groups
    copies = []
    for g in range(groups):
        part = pl.ds(g * depth, depth)
        copies.append([
            pltpu.make_async_copy(
                basis_ref.at[part, pl.ds(start, total)], slot_ref.at[part, :], sems.at[g, 0]
            ),
            pltpu.make_async_copy(
                train_ref.at[:, part], rows_ref.at[pl.ds(0, tokens), part], sems.at[g, 1]
            ),
            pltpu.make_async_copy(
                query_ref.at[:, part], rows_ref.at[pl.ds(tokens, queries), part], sems.at[g, 2]
            ),
        ])
    for group in copies:
        for copy in group:
            copy.start()
    for g, group in enumerate(copies):
        for copy in group:
            copy.wait()
        part = slice(g * depth, (g + 1) * depth)
        half = rows_ref.shape[0] // 2
        for h, value in enumerate(halves_dot(rows_ref[:, part], slot_ref[part, :])):
            span = slice(h * half, (h + 1) * half)
            if g == 0:
                sum_ref[span, :] = value
            else:
                sum_ref[span, :] += value
    for j, (first, width) in enumerate(chunks):
        refs[j][...] = sum_ref[:, first - start : first - start + width]
    column = 0
    for narrow_ref in refs[count : count + narrow]:
        width = narrow_ref.shape[1]
        narrow_ref[...] = sum_ref[:, column : column + width].astype(BF16)
        column += width


def in_part(act_train, act_query, basis_in, prev, chunks, narrow):
    tokens, depth = act_train.shape
    rows = tokens + act_query.shape[0]
    total = sum(width for _, width in chunks)
    groups = next(g for g in (4, 2, 1) if depth % (g * LANES) == 0)
    shapes = [shape_of(rows, width, F32) for _, width in chunks]
    shapes += [shape_of(rows, width, BF16) for width in narrow]
    out = pl.pallas_call(
        functools.partial(in_kernel, chunks, len(narrow), groups),
        in_specs=[ANY_SPEC] * 4,
        out_specs=[VMEM_SPEC] * len(shapes),
        out_shape=shapes,
        scratch_shapes=[
            pltpu.VMEM((rows, depth), BF16),
            pltpu.VMEM((depth, total), BF16),
            pltpu.VMEM((rows, total), F32),
            pltpu.SemaphoreType.DMA((groups, 3)),
        ],
        compiler_params=pltpu.CompilerParams(vmem_limit_bytes=24 * MIB),
        cost_estimate=cost(1024, 1024),
    )(in_hbm(act_train), in_hbm(act_query), in_hbm(basis_in), prev)
    return list(out[: len(chunks)]), list(out[len(chunks) :])


def out_kernel(begin, steps, last, train_ref, query_ref, basis_ref, prev_ref, *refs):
    if last:
        start_ref, keep_ref, *give_refs, rows_ref, slot_ref, acc_ref, sems = refs
    else:
        acc_ref, rows_ref, slot_ref, sems = refs
    tokens, queries = train_ref.shape[0], query_ref.shape[0]
    slots, block = slot_ref.shape[0], slot_ref.shape[1]
    half = acc_ref.shape[0] // 2

    def copies(step):
        slot = lax.rem(step, slots)
        part = pl.ds(pl.multiple_of((begin + step) * block, block), block)
        return [
            pltpu.make_async_copy(basis_ref.at[part, :], slot_ref.at[slot], sems.at[slot, 0]),
            pltpu.make_async_copy(
                train_ref.at[:, part], rows_ref.at[slot, pl.ds(0, tokens), :], sems.at[slot, 1]
            ),
            pltpu.make_async_copy(
                query_ref.at[:, part], rows_ref.at[slot, pl.ds(tokens, queries), :], sems.at[slot, 2]
            ),
        ]

    for step in range(min(slots - 1, steps)):
        for copy in copies(step):
            copy.start()
    acc_ref[...] = start_ref[...] if last else jnp.zeros_like(acc_ref)

    def body(step, carry):
        for copy in copies(step):
            copy.wait()

        @pl.when(step + slots - 1 < steps)
        def _():
            for copy in copies(step + slots - 1):
                copy.start()

        slot = lax.rem(step, slots)
        for h, part in enumerate(halves_dot(rows_ref[slot], slot_ref[slot])):
            acc_ref[h * half : (h + 1) * half, :] += part
        return carry

    lax.fori_loop(0, steps, body, 0)
    if not last:
        return
    odd = lax.rem(lax.axis_index("col"), 2)
    keep_ref[...] = acc_ref[pl.ds(pl.multiple_of(odd * half, 16), half), :]
    cols = give_refs[0].shape[1]
    for c, give_ref in enumerate(give_refs):
        span = slice(c * cols, (c + 1) * cols)
        give_ref[...] = acc_ref[pl.ds(pl.multiple_of((1 - odd) * half, 16), half), span]


def out_part(grad_train, grad_query, basis_out, prev, acc):
    tokens, depth = grad_train.shape
    width = basis_out.shape[1]
    rows = tokens + grad_query.shape[0]
    block = largest_divisor(depth, (512, 256, 128))
    steps = depth // block
    slots = 4
    last = acc is not None
    begin, count = (steps // 2, steps - steps // 2) if last else (0, steps // 2)
    pieces = pieces_of(width, 2)
    if last:
        out_shape = [shape_of(rows // 2, width, F32)]
        out_shape += [shape_of(rows // 2, width // pieces, F32)] * pieces
    else:
        out_shape = [shape_of(rows, width, F32)]
    return pl.pallas_call(
        functools.partial(out_kernel, begin, count, last),
        in_specs=[ANY_SPEC] * 4 + [VMEM_SPEC] * last,
        out_specs=[VMEM_SPEC] * len(out_shape),
        out_shape=out_shape,
        scratch_shapes=[
            pltpu.VMEM((slots, rows, block), BF16),
            pltpu.VMEM((slots, block, width), BF16),
        ]
        + [pltpu.VMEM((rows, width), F32)] * last
        + [pltpu.SemaphoreType.DMA((slots, 3))],
        compiler_params=pltpu.CompilerParams(vmem_limit_bytes=20 * MIB),
        cost_estimate=cost(2 * rows * block * count * width, 2 * block * count * (rows + width)),
    )(
        in_hbm(grad_train), in_hbm(grad_query), in_hbm(basis_out), prev, *([acc] if last else [])
    )


def add_kernel(pieces, outs, skip, keep_ref, *refs):
    wide_ref, narrow_refs = refs[pieces + 1], refs[pieces + 2 :]
    width = keep_ref.shape[1]
    cols = width // pieces
    for c in range(pieces):
        span = slice(c * cols, (c + 1) * cols)
        wide_ref[:, span] = keep_ref[:, span] + refs[c][:, skip : skip + cols].astype(F32)
    cols = width // outs
    for c in range(outs):
        narrow_refs[c][...] = wide_ref[:, c * cols : (c + 1) * cols].astype(BF16)


def add_part(keep, got, prev, outs=1, skip=0):
    rows, width = keep.shape
    out = pl.pallas_call(
        functools.partial(add_kernel, len(got), outs, skip),
        in_specs=[VMEM_SPEC] * (1 + len(got)) + [ANY_SPEC],
        out_specs=[VMEM_SPEC] * (1 + outs),
        out_shape=[shape_of(rows, width, F32)] + [shape_of(rows, width // outs, BF16)] * outs,
        compiler_params=pltpu.CompilerParams(vmem_limit_bytes=12 * MIB),
        cost_estimate=cost(1024, 1024),
    )(keep, *got, prev)
    return out[0], list(out[1:])


def join_kernel(tokens, pieces, prev_ref, *refs):
    mine_refs, other_refs = refs[:pieces], refs[pieces : 2 * pieces]
    gt_ref, gq_ref = refs[2 * pieces :]
    odd = lax.rem(lax.axis_index("col"), 2)
    for c, (mine_ref, other_ref) in enumerate(zip(mine_refs, other_refs)):
        mine, other = mine_ref[...].astype(F32), other_ref[...].astype(F32)
        low = jnp.where(odd == 1, other, mine)
        high = jnp.where(odd == 1, mine, other)
        rows = jnp.concatenate([low, high], axis=0)
        cols = rows.shape[1]
        gt_ref[:, c * cols : (c + 1) * cols] = rows[:tokens].astype(BF16)
        gq_ref[c * cols : (c + 1) * cols, :] = rows[tokens:].T.astype(BF16)


def join_part(mine, other, prev, tokens):
    half = mine[0].shape[0]
    width = sum(x.shape[1] for x in mine)
    queries = 2 * half - tokens
    return pl.pallas_call(
        functools.partial(join_kernel, tokens, len(mine)),
        in_specs=[ANY_SPEC] + [VMEM_SPEC] * (2 * len(mine)),
        out_specs=[VMEM_SPEC] * 2,
        out_shape=[shape_of(tokens, width, BF16), shape_of(width, queries, BF16)],
        compiler_params=pltpu.CompilerParams(vmem_limit_bytes=12 * MIB),
        cost_estimate=cost(1024, 1024),
    )(prev, *mine, *other)


def inverse_kernel(chunks, corr_ref, prev_ref, *refs):
    *inv_refs, slot_ref, sems = refs
    slots, block = slot_ref.shape[0], slot_ref.shape[1]
    steps = corr_ref.shape[0] // block

    def fetch(step):
        rows = pl.ds(step * block, block)
        return pltpu.make_async_copy(
            corr_ref.at[rows, :], slot_ref.at[step % slots], sems.at[step % slots]
        )

    for step in range(min(slots, steps)):
        fetch(step).start()
    for step in range(steps):
        fetch(step).wait()
        for (first, width), inv_ref in zip(chunks, inv_refs):
            value = slot_ref[step % slots, :, first : first + width]
            inv_ref[step * block : (step + 1) * block, :] = 1.0 / value
        if step + slots < steps:
            fetch(step + slots).start()


def inverse_part(correction, prev, chunks):
    rows, width = correction.shape
    block = largest_divisor(rows, (128, 64, 8))
    out = pl.pallas_call(
        functools.partial(inverse_kernel, chunks),
        in_specs=[ANY_SPEC, ANY_SPEC],
        out_specs=[VMEM_SPEC] * len(chunks),
        out_shape=[shape_of(rows, width, F32) for _, width in chunks],
        scratch_shapes=[pltpu.VMEM((4, block, width), F32), pltpu.SemaphoreType.DMA((4,))],
        compiler_params=pltpu.CompilerParams(vmem_limit_bytes=16 * MIB),
        cost_estimate=cost(1024, 1024),
    )(in_hbm(correction), prev)
    return list(out)


def at_end():
    me = lax.axis_index("row")
    return (me == 0) | (me == lax.axis_size("row") - 1)


def pay_kernel(has_part, acc_ref, got_ref, *refs):
    total = acc_ref[...] + got_ref[...].astype(F32)
    if has_part:
        total = jnp.where(at_end(), refs[0][...], total)
    refs[-1][...] = total.astype(BF16)


def pay_part(hint, acc, got, part, prev):
    has_part = part is not None
    return pl.pallas_call(
        functools.partial(pay_kernel, has_part),
        in_specs=[VMEM_SPEC, VMEM_SPEC] + [VMEM_SPEC] * has_part + [ANY_SPEC],
        out_specs=VMEM_SPEC,
        out_shape=shape_of(*acc.shape, BF16),
        compiler_params=pltpu.CompilerParams(vmem_limit_bytes=12 * MIB),
        cost_estimate=cost(hint, 1024),
    )(acc, got, *([part] if has_part else []), prev)


def after_kernel(first_ref, second_ref, out_ref):
    out_ref[...] = jnp.zeros_like(out_ref)


def after_part(first, second):
    return pl.pallas_call(
        after_kernel,
        in_specs=[ANY_SPEC] * 2,
        out_specs=VMEM_SPEC,
        out_shape=shape_of(8, LANES, F32),
        compiler_params=pltpu.CompilerParams(vmem_limit_bytes=4 * MIB),
        cost_estimate=cost(10**9, 1024),
    )(first, second)


def score_kernel(
    start, scale, outs, gt_ref, gq_ref, inv_ref, sent_ref, got_ref, prev_ref, order_ref, *refs
):
    out_refs = refs[:outs]
    quot_ref, wide_ref, own_ref = refs[outs:]
    tokens = gt_ref.shape[0]
    queries = gq_ref.shape[1]
    width = inv_ref.shape[1]
    total = jnp.where(at_end(), got_ref[...].astype(F32), sent_ref[...].astype(F32))
    wide_ref[...] = total[:tokens]
    own_ref[...] = total[tokens:]
    owner = lax.broadcasted_iota(jnp.int32, (queries, width), 0) // LQ
    lane = lax.broadcasted_iota(jnp.int32, (tokens, LANES), 1)

    def quotient(q):
        own = jnp.where(owner == q, own_ref[...], 0.0).astype(BF16)
        products = jnp.dot(gq_ref[...], own, preferred_element_type=F32)
        quot_ref[q % 2] = (products * inv_ref[...]).astype(BF16)

    quotient(0)
    result = jnp.zeros((tokens, LANES), F32) if start else prev_ref[...]
    for q in range(NQ):
        if q + 1 < NQ:
            quotient(q + 1)
        mapped = jnp.dot(gt_ref[...], quot_ref[q % 2], preferred_element_type=F32)
        scaled = mapped * wide_ref[...]
        folded = scaled[:, :LANES]
        for part in range(1, width // LANES):
            folded = folded + scaled[:, part * LANES : (part + 1) * LANES]
        result = result + jnp.where(lane == q, jnp.sum(folded, axis=1, keepdims=True), 0.0)
    if scale is None:
        out_refs[0][...] = result
        return
    final = (result * scale).T[:NQ]
    if outs == 1:
        out_refs[0][...] = final
    else:
        split(final, lax.axis_index("row") // 2, *out_refs)


def split(values, high, keep_ref, give_ref):
    cols = values.shape[1] // 2
    low_half, high_half = values[:, :cols], values[:, cols:]
    keep_ref[...] = jnp.where(high == 1, high_half, low_half)
    give_ref[...] = jnp.where(high == 1, low_half, high_half)


def score_part(rot_gt, rot_gq_t, inv, sent, got, prev, order, start, scale, halves):
    tokens, outs = rot_gt.shape
    width = inv.shape[1]
    queries = rot_gq_t.shape[1]
    if scale is None:
        out_shape = [shape_of(tokens, LANES, F32)]
    elif halves:
        out_shape = [shape_of(NQ, tokens // 2, F32)] * 2
    else:
        out_shape = [shape_of(NQ, tokens, F32)]
    return pl.pallas_call(
        functools.partial(score_kernel, start, scale, len(out_shape)),
        in_specs=[VMEM_SPEC] * 5 + [ANY_SPEC if start else VMEM_SPEC, ANY_SPEC],
        out_specs=[VMEM_SPEC] * len(out_shape),
        out_shape=out_shape,
        scratch_shapes=[
            pltpu.VMEM((2, outs, width), BF16),
            pltpu.VMEM((tokens, width), F32),
            pltpu.VMEM((queries, width), F32),
        ],
        compiler_params=pltpu.CompilerParams(vmem_limit_bytes=16 * MIB),
        cost_estimate=cost(1024, 1024),
    )(rot_gt, rot_gq_t, inv, sent, got, prev, order)


def halve_kernel(keep_ref, got_ref, *refs):
    total = keep_ref[...] + got_ref[...]
    if len(refs) == 1:
        refs[0][...] = total
    else:
        split(total, lax.rem(lax.axis_index("row"), 2), *refs)


def halve_part(keep, got, halves):
    rows, width = keep.shape
    out = [shape_of(rows, width // 2, F32)] * 2 if halves else [shape_of(rows, width, F32)]
    return pl.pallas_call(
        halve_kernel,
        in_specs=[VMEM_SPEC] * 2,
        out_specs=[VMEM_SPEC] * len(out),
        out_shape=out,
        compiler_params=pltpu.CompilerParams(vmem_limit_bytes=4 * MIB),
        cost_estimate=cost(1024, 1024),
    )(keep, got)


def line_sum(partial, axis):
    n = lax.axis_size(axis)
    half = n // 2
    me = lax.axis_index(axis)
    if n % 2:
        return lax.psum(partial, axis).astype(BF16)
    acc = partial
    for s in range(half - 1):
        pairs = [(s, s + 1), (n - 1 - s, n - 2 - s)]
        acc = acc + lax.ppermute(acc.astype(BF16), axis, pairs).astype(F32)
    got = lax.ppermute(acc.astype(BF16), axis, [(half - 1, half), (half, half - 1)])
    total = (acc + got.astype(F32)).astype(BF16)
    for s in range(half - 2, -1, -1):
        pairs = [(s + 1, s), (n - 2 - s, n - 1 - s)]
        got = lax.ppermute(total, axis, pairs)
        total = jnp.where((me == s) | (me == n - 1 - s), got, total)
    return total


def owned_sum(partial, axis):
    n = lax.axis_size(axis)
    me = lax.axis_index(axis)
    total = lax.dynamic_index_in_dim(partial, me, 0, keepdims=False)
    for step in range(1, n):
        block = lax.dynamic_index_in_dim(partial, (me + step) % n, 0, keepdims=False)
        total = total + lax.ppermute(block, axis, [(d, (d + step) % n) for d in range(n)])
    return total


def shared_sum(partial, axis):
    n = lax.axis_size(axis)
    total = partial
    for step in range(1, n):
        total = total + lax.ppermute(partial, axis, [(d, (d + step) % n) for d in range(n)])
    return total


def on_device(act_train, act_query, grad_train, grad_query, basis_in, basis_out, correction):
    norm_scale = (O * I * LQ) ** (-0.5)
    tokens = act_train.shape[0]
    n_row, n_col = lax.axis_size("row"), lax.axis_size("col")
    chunks = chunk_list(basis_in.shape[1])
    count = len(chunks)
    line = n_row == 4
    flip = [(d, d ^ 1) for d in range(n_col)]
    outer = [(0, 1), (1, 0), (2, 3), (3, 2)]
    inner = []
    for c in range(n_col):
        inner += [(n_col + c, 2 * n_col + c), (2 * n_col + c, n_col + c)]
        inner += [(c, c ^ 1), (3 * n_col + c, 3 * n_col + (c ^ 1))]
    sent, got, acc, got_mid, skip = {}, {}, {}, {}, {}

    def swap(j, payload):
        sent[j] = payload
        got[j] = lax.ppermute(payload, "row", outer)

    def meet(j, prev):
        if not line or j >= count:
            return prev
        acc[j], (thin,) = add_part(parts[j], [got[j]], prev, 1, skip.get(j, 0))
        got_mid[j] = lax.ppermute(thin, ("row", "col"), inner)
        return thin

    def pay(j, prev):
        if not line:
            sent[j + LAG] = got[j + LAG] = line_sum(parts[j], "row")
            return prev
        part = parts[j + LAG] if j + LAG < count else None
        payload = pay_part(4 * 10**9 if j == 0 else 1024, acc[j], got_mid[j], part, prev)
        swap(j + LAG, payload)
        return payload

    def score(k, sums, prev):
        return score_part(
            rot_gt, rot_gq_t, invs[k], sent[k + LAG], got[k + LAG], sums[0], prev,
            k == 0, norm_scale if k == count - 1 else None, halves,
        )

    early = min(LAG + 2, count)
    widths = [width for _, width in chunks]
    parts, narrow = in_part(
        act_train, act_query, basis_in, act_query, chunks[:early], [widths[0], sum(widths[1:LAG])]
    )
    if line:
        swap(0, narrow[0])
        swap(1, narrow[1])
        for j in range(2, LAG):
            got[j] = got[1]
            skip[j] = sum(widths[1:j])
    (half_sum,) = out_part(grad_train, grad_query, basis_out, parts[-1], None)
    prev = meet(0, half_sum)
    keep, *give = out_part(grad_train, grad_query, basis_out, prev, half_sum)
    given = [lax.ppermute(piece, "col", flip) for piece in give]
    prev = pay(0, meet(1, keep))
    outs = pieces_of(keep.shape[1], 2)
    wide, thin = add_part(keep, given, prev, outs)
    prev, bit = wide, 2
    while bit < n_col:
        other = [lax.ppermute(x, "col", [(d, d ^ bit) for d in range(n_col)]) for x in thin]
        if bit == 2:
            prev = meet(2, prev)
            more, _ = in_part(act_train, act_query, basis_in, prev, chunks[early:], [])
            parts += more
            prev = meet(3, pay(1, more[-1]))
            invs = inverse_part(correction, prev, chunks)
            prev = invs[0]
        wide, thin = add_part(wide, other, prev, outs)
        prev = wide
        bit *= 2
    other = [lax.ppermute(x, "col", flip) for x in thin]
    prev = pay(3, meet(4, pay(2, prev)))
    rot_gt, rot_gq_t = join_part(thin, other, prev, tokens)
    halves = n_row == 4 and n_col & (n_col - 1) == 0 and tokens % (n_row * LANES) == 0
    sums = [rot_gt]
    for j in range(5, count + 1):
        sums = score(j - 5, sums, prev)
        prev = meet(j, sums[0])
        if line and j == count:
            prev = after_part(prev, got[count])
        prev = pay(j - 1, prev)
    for k in range(count - 4, count):
        sums = score(k, sums, prev)
    if not halves:
        blocks = sums[0].reshape(NQ, n_row, tokens // n_row).transpose(1, 0, 2)
        return shared_sum(owned_sum(blocks, "row"), "col")
    keep, give = sums
    swapped = lax.ppermute(give, "row", [(d, d ^ 2) for d in range(n_row)])
    keep, give = halve_part(keep, swapped, True)
    (keep,) = halve_part(keep, lax.ppermute(give, "row", outer), False)
    bit = 1
    while bit < n_col:
        swapped = lax.ppermute(keep, "col", [(d, d ^ bit) for d in range(n_col)])
        (keep,) = halve_part(keep, swapped, False)
        bit *= 2
    return keep


def solution(mesh):
    in_specs = (
        P("groups", "row"),
        P("groups", "row"),
        P("groups", "col"),
        P("groups", "col"),
        P(("groups", "row"), "col"),
        P(("groups", "col"), "row"),
        P(("groups", "row"), "col"),
    )
    out_specs = P("groups", "row")
    return jax.shard_map(
        on_device, mesh=mesh, in_specs=in_specs, out_specs=out_specs, check_vma=False
    )
```

```python
import functools

import jax
import jax.numpy as jnp
from jax import lax
from jax.experimental import pallas as pl
from jax.experimental.pallas import tpu as pltpu
from jax.sharding import PartitionSpec as P

I = 8192
O = 4096
NQ = 8
LQ = 16
LANES = 128
CHUNKS = 8
LAG = 3
F32 = jnp.float32
BF16 = jnp.bfloat16
MIB = 1 << 20

VMEM_SPEC = pl.BlockSpec(memory_space=pltpu.VMEM)
SMEM_SPEC = pl.BlockSpec(memory_space=pltpu.SMEM)
ANY_SPEC = pl.BlockSpec(memory_space=pl.ANY)


def shape_of(rows, width, dtype):
    return jax.ShapeDtypeStruct((rows, width), dtype)


def chunk_list(size):
    tiles = size // LANES
    count = min(CHUNKS, tiles)
    chunks, first = [], 0
    for k in range(count):
        width = LANES * (tiles // count + (1 if k < tiles % count else 0))
        chunks.append((first, width))
        first += width
    return chunks


def largest_divisor(size, choices):
    for choice in choices:
        if size % choice == 0:
            return choice
    return size


def pieces_of(width, most):
    return max(p for p in range(1, most + 1) if width % (p * LANES) == 0)


def cost(flops, bytes_accessed):
    return pl.CostEstimate(flops=flops, bytes_accessed=bytes_accessed, transcendentals=0)


def in_hbm(x):
    return pltpu.with_memory_space_constraint(x, pltpu.HBM)


def halves_dot(rows, basis):
    half = rows.shape[0] // 2
    return [jnp.dot(part, basis, preferred_element_type=F32) for part in (rows[:half], rows[half:])]


def in_kernel(chunks, narrow, groups, train_ref, query_ref, basis_ref, prev_ref, *refs):
    count = len(chunks)
    rows_ref, slot_ref, sum_ref, sems = refs[count + narrow :]
    tokens, queries = train_ref.shape[0], query_ref.shape[0]
    start, total = chunks[0][0], slot_ref.shape[1]
    depth = basis_ref.shape[0] // groups
    copies = []
    for g in range(groups):
        part = pl.ds(g * depth, depth)
        copies.append([
            pltpu.make_async_copy(
                basis_ref.at[part, pl.ds(start, total)], slot_ref.at[part, :], sems.at[g, 0]
            ),
            pltpu.make_async_copy(
                train_ref.at[:, part], rows_ref.at[pl.ds(0, tokens), part], sems.at[g, 1]
            ),
            pltpu.make_async_copy(
                query_ref.at[:, part], rows_ref.at[pl.ds(tokens, queries), part], sems.at[g, 2]
            ),
        ])
    for group in copies:
        for copy in group:
            copy.start()
    for g, group in enumerate(copies):
        for copy in group:
            copy.wait()
        part = slice(g * depth, (g + 1) * depth)
        half = rows_ref.shape[0] // 2
        for h, value in enumerate(halves_dot(rows_ref[:, part], slot_ref[part, :])):
            span = slice(h * half, (h + 1) * half)
            if g == 0:
                sum_ref[span, :] = value
            else:
                sum_ref[span, :] += value
    for j, (first, width) in enumerate(chunks):
        refs[j][...] = sum_ref[:, first - start : first - start + width]
    column = 0
    for narrow_ref in refs[count : count + narrow]:
        width = narrow_ref.shape[1]
        narrow_ref[...] = sum_ref[:, column : column + width].astype(BF16)
        column += width


def in_part(act_train, act_query, basis_in, prev, chunks, narrow):
    tokens, depth = act_train.shape
    rows = tokens + act_query.shape[0]
    total = sum(width for _, width in chunks)
    groups = next(g for g in (4, 2, 1) if depth % (g * LANES) == 0)
    shapes = [shape_of(rows, width, F32) for _, width in chunks]
    shapes += [shape_of(rows, width, BF16) for width in narrow]
    out = pl.pallas_call(
        functools.partial(in_kernel, chunks, len(narrow), groups),
        in_specs=[ANY_SPEC] * 4,
        out_specs=[VMEM_SPEC] * len(shapes),
        out_shape=shapes,
        scratch_shapes=[
            pltpu.VMEM((rows, depth), BF16),
            pltpu.VMEM((depth, total), BF16),
            pltpu.VMEM((rows, total), F32),
            pltpu.SemaphoreType.DMA((groups, 3)),
        ],
        compiler_params=pltpu.CompilerParams(vmem_limit_bytes=24 * MIB),
        cost_estimate=cost(1024, 1024),
    )(in_hbm(act_train), in_hbm(act_query), in_hbm(basis_in), prev)
    return list(out[: len(chunks)]), list(out[len(chunks) :])


def out_kernel(begin, steps, last, train_ref, query_ref, basis_ref, prev_ref, *refs):
    if last:
        start_ref, keep_ref, *give_refs, rows_ref, slot_ref, acc_ref, sems = refs
    else:
        acc_ref, rows_ref, slot_ref, sems = refs
    tokens, queries = train_ref.shape[0], query_ref.shape[0]
    slots, block = slot_ref.shape[0], slot_ref.shape[1]
    half, width = acc_ref.shape[0] // 2, acc_ref.shape[1]
    tile = largest_divisor(width, (256, 128))

    def copies(step):
        slot = lax.rem(step, slots)
        part = pl.ds(pl.multiple_of((begin + step) * block, block), block)
        return [
            pltpu.make_async_copy(basis_ref.at[part, :], slot_ref.at[slot], sems.at[slot, 0]),
            pltpu.make_async_copy(
                train_ref.at[:, part], rows_ref.at[slot, pl.ds(0, tokens), :], sems.at[slot, 1]
            ),
            pltpu.make_async_copy(
                query_ref.at[:, part], rows_ref.at[slot, pl.ds(tokens, queries), :], sems.at[slot, 2]
            ),
        ]

    for step in range(min(slots - 1, steps)):
        for copy in copies(step):
            copy.start()
    acc_ref[...] = start_ref[...] if last else jnp.zeros_like(acc_ref)

    def body(step, carry):
        for copy in copies(step):
            copy.wait()

        @pl.when(step + slots - 1 < steps)
        def _():
            for copy in copies(step + slots - 1):
                copy.start()

        slot = lax.rem(step, slots)
        rows = rows_ref[slot]
        for first in range(0, width, tile):
            span = slice(first, first + tile)
            acc_ref[:, span] += jnp.dot(rows, slot_ref[slot, :, span], preferred_element_type=F32)
        return carry

    lax.fori_loop(0, steps, body, 0)
    if not last:
        return
    odd = lax.rem(lax.axis_index("col"), 2)
    keep_ref[...] = acc_ref[pl.ds(pl.multiple_of(odd * half, 16), half), :]
    cols = give_refs[0].shape[1]
    for c, give_ref in enumerate(give_refs):
        span = slice(c * cols, (c + 1) * cols)
        give_ref[...] = acc_ref[pl.ds(pl.multiple_of((1 - odd) * half, 16), half), span]


def out_part(grad_train, grad_query, basis_out, prev, acc):
    tokens, depth = grad_train.shape
    width = basis_out.shape[1]
    rows = tokens + grad_query.shape[0]
    block = largest_divisor(depth, (512, 256, 128))
    steps = depth // block
    slots = 4
    last = acc is not None
    first = steps * 9 // 14
    begin, count = (first, steps - first) if last else (0, first)
    pieces = pieces_of(width, 2)
    if last:
        out_shape = [shape_of(rows // 2, width, F32)]
        out_shape += [shape_of(rows // 2, width // pieces, F32)] * pieces
    else:
        out_shape = [shape_of(rows, width, F32)]
    return pl.pallas_call(
        functools.partial(out_kernel, begin, count, last),
        in_specs=[ANY_SPEC] * 4 + [VMEM_SPEC] * last,
        out_specs=[VMEM_SPEC] * len(out_shape),
        out_shape=out_shape,
        scratch_shapes=[
            pltpu.VMEM((slots, rows, block), BF16),
            pltpu.VMEM((slots, block, width), BF16),
        ]
        + [pltpu.VMEM((rows, width), F32)] * last
        + [pltpu.SemaphoreType.DMA((slots, 3))],
        compiler_params=pltpu.CompilerParams(vmem_limit_bytes=20 * MIB),
        cost_estimate=cost(2 * rows * block * count * width if last else 1024, 1024),
    )(
        in_hbm(grad_train), in_hbm(grad_query), in_hbm(basis_out), prev, *([acc] if last else [])
    )


def add_kernel(pieces, outs, skip, keep_ref, *refs):
    wide_ref, narrow_refs = refs[pieces + 1], refs[pieces + 2 :]
    width = keep_ref.shape[1]
    cols = width // pieces
    for c in range(pieces):
        span = slice(c * cols, (c + 1) * cols)
        wide_ref[:, span] = keep_ref[:, span] + refs[c][:, skip : skip + cols].astype(F32)
    cols = width // outs
    for c in range(outs):
        narrow_refs[c][...] = wide_ref[:, c * cols : (c + 1) * cols].astype(BF16)


def add_part(keep, got, prev, outs=1, skip=0):
    rows, width = keep.shape
    out = pl.pallas_call(
        functools.partial(add_kernel, len(got), outs, skip),
        in_specs=[VMEM_SPEC] * (1 + len(got)) + [ANY_SPEC],
        out_specs=[VMEM_SPEC] * (1 + outs),
        out_shape=[shape_of(rows, width, F32)] + [shape_of(rows, width // outs, BF16)] * outs,
        compiler_params=pltpu.CompilerParams(vmem_limit_bytes=12 * MIB),
        cost_estimate=cost(1024, 1024),
    )(keep, *got, prev)
    return out[0], list(out[1:])


def join_kernel(tokens, pieces, prev_ref, *refs):
    mine_refs, other_refs = refs[:pieces], refs[pieces : 2 * pieces]
    gt_ref, gq_ref = refs[2 * pieces :]
    odd = lax.rem(lax.axis_index("col"), 2)
    for c, (mine_ref, other_ref) in enumerate(zip(mine_refs, other_refs)):
        mine, other = mine_ref[...].astype(F32), other_ref[...].astype(F32)
        low = jnp.where(odd == 1, other, mine)
        high = jnp.where(odd == 1, mine, other)
        rows = jnp.concatenate([low, high], axis=0)
        cols = rows.shape[1]
        gt_ref[:, c * cols : (c + 1) * cols] = rows[:tokens].astype(BF16)
        gq_ref[c * cols : (c + 1) * cols, :] = rows[tokens:].T.astype(BF16)


def join_part(mine, other, prev, tokens):
    half = mine[0].shape[0]
    width = sum(x.shape[1] for x in mine)
    queries = 2 * half - tokens
    return pl.pallas_call(
        functools.partial(join_kernel, tokens, len(mine)),
        in_specs=[ANY_SPEC] + [VMEM_SPEC] * (2 * len(mine)),
        out_specs=[VMEM_SPEC] * 2,
        out_shape=[shape_of(tokens, width, BF16), shape_of(width, queries, BF16)],
        compiler_params=pltpu.CompilerParams(vmem_limit_bytes=12 * MIB),
        cost_estimate=cost(1024, 1024),
    )(prev, *mine, *other)


def inverse_kernel(chunks, corr_ref, prev_ref, *refs):
    *inv_refs, slot_ref, sems = refs
    slots, block = slot_ref.shape[0], slot_ref.shape[1]
    steps = corr_ref.shape[0] // block

    def fetch(step):
        rows = pl.ds(step * block, block)
        return pltpu.make_async_copy(
            corr_ref.at[rows, :], slot_ref.at[step % slots], sems.at[step % slots]
        )

    for step in range(min(slots, steps)):
        fetch(step).start()
    for step in range(steps):
        fetch(step).wait()
        for (first, width), inv_ref in zip(chunks, inv_refs):
            value = slot_ref[step % slots, :, first : first + width]
            inv_ref[step * block : (step + 1) * block, :] = 1.0 / value
        if step + slots < steps:
            fetch(step + slots).start()


def inverse_part(correction, prev, chunks):
    rows, width = correction.shape
    block = largest_divisor(rows, (128, 64, 8))
    out = pl.pallas_call(
        functools.partial(inverse_kernel, chunks),
        in_specs=[ANY_SPEC, ANY_SPEC],
        out_specs=[VMEM_SPEC] * len(chunks),
        out_shape=[shape_of(rows, width, F32) for _, width in chunks],
        scratch_shapes=[pltpu.VMEM((4, block, width), F32), pltpu.SemaphoreType.DMA((4,))],
        compiler_params=pltpu.CompilerParams(vmem_limit_bytes=16 * MIB),
        cost_estimate=cost(1024, 1024),
    )(in_hbm(correction), prev)
    return list(out)


def at_end():
    me = lax.axis_index("row")
    return (me == 0) | (me == lax.axis_size("row") - 1)


def pay_kernel(has_part, acc_ref, got_ref, *refs):
    total = acc_ref[...] + got_ref[...].astype(F32)
    if has_part:
        total = jnp.where(at_end(), refs[0][...], total)
    refs[-1][...] = total.astype(BF16)


def pay_part(hint, acc, got, part, prev):
    has_part = part is not None
    return pl.pallas_call(
        functools.partial(pay_kernel, has_part),
        in_specs=[VMEM_SPEC, VMEM_SPEC] + [VMEM_SPEC] * has_part + [ANY_SPEC],
        out_specs=VMEM_SPEC,
        out_shape=shape_of(*acc.shape, BF16),
        compiler_params=pltpu.CompilerParams(vmem_limit_bytes=12 * MIB),
        cost_estimate=cost(hint, 1024),
    )(acc, got, *([part] if has_part else []), prev)


def after_kernel(first_ref, second_ref, out_ref):
    out_ref[...] = jnp.zeros_like(out_ref)


def after_part(first, second):
    return pl.pallas_call(
        after_kernel,
        in_specs=[ANY_SPEC] * 2,
        out_specs=VMEM_SPEC,
        out_shape=shape_of(8, LANES, F32),
        compiler_params=pltpu.CompilerParams(vmem_limit_bytes=4 * MIB),
        cost_estimate=cost(10**9, 1024),
    )(first, second)


def score_kernel(
    start, scale, outs, gt_ref, gq_ref, inv_ref, sent_ref, got_ref, prev_ref, order_ref, *refs
):
    out_refs = refs[:outs]
    quot_ref, wide_ref, own_ref = refs[outs:]
    tokens = gt_ref.shape[0]
    queries = gq_ref.shape[1]
    width = inv_ref.shape[1]
    total = jnp.where(at_end(), got_ref[...].astype(F32), sent_ref[...].astype(F32))
    wide_ref[...] = total[:tokens]
    own_ref[...] = total[tokens:]
    owner = lax.broadcasted_iota(jnp.int32, (queries, width), 0) // LQ
    lane = lax.broadcasted_iota(jnp.int32, (tokens, LANES), 1)

    def quotient(q):
        own = jnp.where(owner == q, own_ref[...], 0.0).astype(BF16)
        products = jnp.dot(gq_ref[...], own, preferred_element_type=F32)
        quot_ref[q % 2] = (products * inv_ref[...]).astype(BF16)

    quotient(0)
    result = jnp.zeros((tokens, LANES), F32) if start else prev_ref[...]
    for q in range(NQ):
        if q + 1 < NQ:
            quotient(q + 1)
        mapped = jnp.dot(gt_ref[...], quot_ref[q % 2], preferred_element_type=F32)
        scaled = mapped * wide_ref[...]
        folded = scaled[:, :LANES]
        for part in range(1, width // LANES):
            folded = folded + scaled[:, part * LANES : (part + 1) * LANES]
        result = result + jnp.where(lane == q, jnp.sum(folded, axis=1, keepdims=True), 0.0)
    if scale is None:
        out_refs[0][...] = result
        return
    final = (result * scale).T[:NQ]
    if outs == 1:
        out_refs[0][...] = final
    else:
        split(final, lax.axis_index("row") // 2, *out_refs)


def split(values, high, keep_ref, give_ref):
    cols = values.shape[1] // 2
    low_half, high_half = values[:, :cols], values[:, cols:]
    keep_ref[...] = jnp.where(high == 1, high_half, low_half)
    give_ref[...] = jnp.where(high == 1, low_half, high_half)


def score_part(rot_gt, rot_gq_t, inv, sent, got, prev, order, start, scale, halves):
    tokens, outs = rot_gt.shape
    width = inv.shape[1]
    queries = rot_gq_t.shape[1]
    if scale is None:
        out_shape = [shape_of(tokens, LANES, F32)]
    elif halves:
        out_shape = [shape_of(NQ, tokens // 2, F32)] * 2
    else:
        out_shape = [shape_of(NQ, tokens, F32)]
    return pl.pallas_call(
        functools.partial(score_kernel, start, scale, len(out_shape)),
        in_specs=[VMEM_SPEC] * 5 + [ANY_SPEC if start else VMEM_SPEC, ANY_SPEC],
        out_specs=[VMEM_SPEC] * len(out_shape),
        out_shape=out_shape,
        scratch_shapes=[
            pltpu.VMEM((2, outs, width), BF16),
            pltpu.VMEM((tokens, width), F32),
            pltpu.VMEM((queries, width), F32),
        ],
        compiler_params=pltpu.CompilerParams(vmem_limit_bytes=16 * MIB),
        cost_estimate=cost(1024, 1024),
    )(rot_gt, rot_gq_t, inv, sent, got, prev, order)


def halve_kernel(keep_ref, got_ref, *refs):
    total = keep_ref[...] + got_ref[...]
    if len(refs) == 1:
        refs[0][...] = total
    else:
        split(total, lax.rem(lax.axis_index("row"), 2), *refs)


def halve_part(keep, got, halves):
    rows, width = keep.shape
    out = [shape_of(rows, width // 2, F32)] * 2 if halves else [shape_of(rows, width, F32)]
    return pl.pallas_call(
        halve_kernel,
        in_specs=[VMEM_SPEC] * 2,
        out_specs=[VMEM_SPEC] * len(out),
        out_shape=out,
        compiler_params=pltpu.CompilerParams(vmem_limit_bytes=4 * MIB),
        cost_estimate=cost(1024, 1024),
    )(keep, got)


def line_sum(partial, axis):
    n = lax.axis_size(axis)
    half = n // 2
    me = lax.axis_index(axis)
    if n % 2:
        return lax.psum(partial, axis).astype(BF16)
    acc = partial
    for s in range(half - 1):
        pairs = [(s, s + 1), (n - 1 - s, n - 2 - s)]
        acc = acc + lax.ppermute(acc.astype(BF16), axis, pairs).astype(F32)
    got = lax.ppermute(acc.astype(BF16), axis, [(half - 1, half), (half, half - 1)])
    total = (acc + got.astype(F32)).astype(BF16)
    for s in range(half - 2, -1, -1):
        pairs = [(s + 1, s), (n - 2 - s, n - 1 - s)]
        got = lax.ppermute(total, axis, pairs)
        total = jnp.where((me == s) | (me == n - 1 - s), got, total)
    return total


def owned_sum(partial, axis):
    n = lax.axis_size(axis)
    me = lax.axis_index(axis)
    total = lax.dynamic_index_in_dim(partial, me, 0, keepdims=False)
    for step in range(1, n):
        block = lax.dynamic_index_in_dim(partial, (me + step) % n, 0, keepdims=False)
        total = total + lax.ppermute(block, axis, [(d, (d + step) % n) for d in range(n)])
    return total


def shared_sum(partial, axis):
    n = lax.axis_size(axis)
    total = partial
    for step in range(1, n):
        total = total + lax.ppermute(partial, axis, [(d, (d + step) % n) for d in range(n)])
    return total


def on_device(act_train, act_query, grad_train, grad_query, basis_in, basis_out, correction):
    norm_scale = (O * I * LQ) ** (-0.5)
    tokens = act_train.shape[0]
    n_row, n_col = lax.axis_size("row"), lax.axis_size("col")
    chunks = chunk_list(basis_in.shape[1])
    count = len(chunks)
    line = n_row == 4
    flip = [(d, d ^ 1) for d in range(n_col)]
    outer = [(0, 1), (1, 0), (2, 3), (3, 2)]
    inner = []
    for c in range(n_col):
        inner += [(n_col + c, 2 * n_col + c), (2 * n_col + c, n_col + c)]
        inner += [(c, c ^ 1), (3 * n_col + c, 3 * n_col + (c ^ 1))]
    sent, got, acc, got_mid, skip = {}, {}, {}, {}, {}

    def swap(j, payload):
        sent[j] = payload
        got[j] = lax.ppermute(payload, "row", outer)

    def meet(j, prev):
        if not line or j >= count:
            return prev
        acc[j], (thin,) = add_part(parts[j], [got[j]], prev, 1, skip.get(j, 0))
        got_mid[j] = lax.ppermute(thin, ("row", "col"), inner)
        return thin

    def pay(j, prev):
        if not line:
            sent[j + LAG] = got[j + LAG] = line_sum(parts[j], "row")
            return prev
        part = parts[j + LAG] if j + LAG < count else None
        payload = pay_part(4 * 10**9 if j == 0 else 1024, acc[j], got_mid[j], part, prev)
        swap(j + LAG, payload)
        return payload

    def score(k, sums, prev):
        return score_part(
            rot_gt, rot_gq_t, invs[k], sent[k + LAG], got[k + LAG], sums[0], prev,
            k == 0, norm_scale if k == count - 1 else None, halves,
        )

    early = min(LAG + 2, count)
    widths = [width for _, width in chunks]
    parts, narrow = in_part(
        act_train, act_query, basis_in, act_query, chunks[:2], [widths[0] + widths[1]]
    )
    if line:
        swap(0, narrow[0])
        got[1], skip[1] = got[0], widths[0]
    more, narrow = in_part(
        act_train, act_query, basis_in, parts[-1], chunks[2:early], [widths[2]]
    )
    parts += more
    if line:
        swap(2, narrow[0])
    (half_sum,) = out_part(grad_train, grad_query, basis_out, parts[-1], None)
    prev = meet(1, meet(0, half_sum))
    keep, *give = out_part(grad_train, grad_query, basis_out, prev, half_sum)
    given = [lax.ppermute(piece, "col", flip) for piece in give]
    prev = keep
    if line:
        prev = after_part(prev, got[2])
    prev = meet(2, pay(0, prev))
    outs = pieces_of(keep.shape[1], 2)
    wide, thin = add_part(keep, given, prev, outs)
    prev, bit = wide, 2
    while bit < n_col:
        other = [lax.ppermute(x, "col", [(d, d ^ bit) for d in range(n_col)]) for x in thin]
        if bit == 2:
            more, _ = in_part(act_train, act_query, basis_in, prev, chunks[early:], [])
            parts += more
            prev = meet(3, pay(1, more[-1]))
            invs = inverse_part(correction, prev, chunks)
            prev = pay(2, invs[0])
        wide, thin = add_part(wide, other, prev, outs)
        prev = wide
        bit *= 2
    other = [lax.ppermute(x, "col", flip) for x in thin]
    prev = meet(5, pay(3, meet(4, prev)))
    rot_gt, rot_gq_t = join_part(thin, other, prev, tokens)
    prev = rot_gt
    halves = n_row == 4 and n_col & (n_col - 1) == 0 and tokens % (n_row * LANES) == 0
    sums = score(0, [rot_gt], prev)
    done = 1
    for j in range(6, count + 1):
        prev = meet(j, pay(j - 2, sums[0]))
        sums = score(done, sums, prev)
        done += 1
    sums = score(done, sums, prev)
    done += 1
    if line:
        prev = after_part(sums[0], got[count])
    prev = pay(count - 1, prev)
    for k in range(done, count):
        sums = score(k, sums, prev)
    if not halves:
        blocks = sums[0].reshape(NQ, n_row, tokens // n_row).transpose(1, 0, 2)
        return shared_sum(owned_sum(blocks, "row"), "col")
    keep, give = sums
    swapped = lax.ppermute(give, "row", [(d, d ^ 2) for d in range(n_row)])
    keep, give = halve_part(keep, swapped, True)
    (keep,) = halve_part(keep, lax.ppermute(give, "row", outer), False)
    bit = 1
    while bit < n_col:
        swapped = lax.ppermute(keep, "col", [(d, d ^ bit) for d in range(n_col)])
        (keep,) = halve_part(keep, swapped, False)
        bit *= 2
    return keep


def solution(mesh):
    in_specs = (
        P("groups", "row"),
        P("groups", "row"),
        P("groups", "col"),
        P("groups", "col"),
        P(("groups", "row"), "col"),
        P(("groups", "col"), "row"),
        P(("groups", "row"), "col"),
    )
    out_specs = P("groups", "row")
    return jax.shard_map(
        on_device, mesh=mesh, in_specs=in_specs, out_specs=out_specs, check_vma=False
    )
```

```python
import functools

import jax
import jax.numpy as jnp
from jax import lax
from jax.experimental import pallas as pl
from jax.experimental.pallas import tpu as pltpu
from jax.sharding import PartitionSpec as P

I = 8192
O = 4096
NQ = 8
LQ = 16
LANES = 128
CHUNKS = 8
LAG = 3
F32 = jnp.float32
BF16 = jnp.bfloat16
MIB = 1 << 20

VMEM_SPEC = pl.BlockSpec(memory_space=pltpu.VMEM)
SMEM_SPEC = pl.BlockSpec(memory_space=pltpu.SMEM)
ANY_SPEC = pl.BlockSpec(memory_space=pl.ANY)


def shape_of(rows, width, dtype):
    return jax.ShapeDtypeStruct((rows, width), dtype)


def chunk_list(size):
    tiles = size // LANES
    count = min(CHUNKS, tiles)
    chunks, first = [], 0
    for k in range(count):
        width = LANES * (tiles // count + (1 if k < tiles % count else 0))
        chunks.append((first, width))
        first += width
    return chunks


def largest_divisor(size, choices):
    for choice in choices:
        if size % choice == 0:
            return choice
    return size


def pieces_of(width, most):
    return max(p for p in range(1, most + 1) if width % (p * LANES) == 0)


def cost(flops, bytes_accessed):
    return pl.CostEstimate(flops=flops, bytes_accessed=bytes_accessed, transcendentals=0)


def in_hbm(x):
    return pltpu.with_memory_space_constraint(x, pltpu.HBM)


def halves_dot(rows, basis):
    half = rows.shape[0] // 2
    return [jnp.dot(part, basis, preferred_element_type=F32) for part in (rows[:half], rows[half:])]


def in_kernel(chunks, narrow, groups, train_ref, query_ref, basis_ref, prev_ref, *refs):
    count = len(chunks)
    rows_ref, slot_ref, sum_ref, sems = refs[count + narrow :]
    tokens, queries = train_ref.shape[0], query_ref.shape[0]
    start, total = chunks[0][0], slot_ref.shape[1]
    depth = basis_ref.shape[0] // groups
    copies = []
    for g in range(groups):
        part = pl.ds(g * depth, depth)
        copies.append([
            pltpu.make_async_copy(
                basis_ref.at[part, pl.ds(start, total)], slot_ref.at[part, :], sems.at[g, 0]
            ),
            pltpu.make_async_copy(
                train_ref.at[:, part], rows_ref.at[pl.ds(0, tokens), part], sems.at[g, 1]
            ),
            pltpu.make_async_copy(
                query_ref.at[:, part], rows_ref.at[pl.ds(tokens, queries), part], sems.at[g, 2]
            ),
        ])
    for group in copies:
        for copy in group:
            copy.start()
    for g, group in enumerate(copies):
        for copy in group:
            copy.wait()
        part = slice(g * depth, (g + 1) * depth)
        half = rows_ref.shape[0] // 2
        for h, value in enumerate(halves_dot(rows_ref[:, part], slot_ref[part, :])):
            span = slice(h * half, (h + 1) * half)
            if g == 0:
                sum_ref[span, :] = value
            else:
                sum_ref[span, :] += value
    for j, (first, width) in enumerate(chunks):
        refs[j][...] = sum_ref[:, first - start : first - start + width]
    column = 0
    for narrow_ref in refs[count : count + narrow]:
        width = narrow_ref.shape[1]
        narrow_ref[...] = sum_ref[:, column : column + width].astype(BF16)
        column += width


def in_part(act_train, act_query, basis_in, prev, chunks, narrow):
    tokens, depth = act_train.shape
    rows = tokens + act_query.shape[0]
    total = sum(width for _, width in chunks)
    groups = next(g for g in (4, 2, 1) if depth % (g * LANES) == 0)
    shapes = [shape_of(rows, width, F32) for _, width in chunks]
    shapes += [shape_of(rows, width, BF16) for width in narrow]
    out = pl.pallas_call(
        functools.partial(in_kernel, chunks, len(narrow), groups),
        in_specs=[ANY_SPEC] * 4,
        out_specs=[VMEM_SPEC] * len(shapes),
        out_shape=shapes,
        scratch_shapes=[
            pltpu.VMEM((rows, depth), BF16),
            pltpu.VMEM((depth, total), BF16),
            pltpu.VMEM((rows, total), F32),
            pltpu.SemaphoreType.DMA((groups, 3)),
        ],
        compiler_params=pltpu.CompilerParams(vmem_limit_bytes=24 * MIB),
        cost_estimate=cost(1024, 1024),
    )(in_hbm(act_train), in_hbm(act_query), in_hbm(basis_in), prev)
    return list(out[: len(chunks)]), list(out[len(chunks) :])


def out_kernel(begin, steps, last, train_ref, query_ref, basis_ref, prev_ref, *refs):
    if last:
        start_ref, keep_ref, *give_refs, rows_ref, slot_ref, acc_ref, sems = refs
    else:
        acc_ref, rows_ref, slot_ref, sems = refs
    tokens, queries = train_ref.shape[0], query_ref.shape[0]
    slots, block = slot_ref.shape[0], slot_ref.shape[1]
    half, width = acc_ref.shape[0] // 2, acc_ref.shape[1]
    tile = largest_divisor(width, (256, 128))

    def copies(step):
        slot = lax.rem(step, slots)
        part = pl.ds(pl.multiple_of((begin + step) * block, block), block)
        return [
            pltpu.make_async_copy(basis_ref.at[part, :], slot_ref.at[slot], sems.at[slot, 0]),
            pltpu.make_async_copy(
                train_ref.at[:, part], rows_ref.at[slot, pl.ds(0, tokens), :], sems.at[slot, 1]
            ),
            pltpu.make_async_copy(
                query_ref.at[:, part], rows_ref.at[slot, pl.ds(tokens, queries), :], sems.at[slot, 2]
            ),
        ]

    for step in range(min(slots - 1, steps)):
        for copy in copies(step):
            copy.start()
    acc_ref[...] = start_ref[...] if last else jnp.zeros_like(acc_ref)

    def body(step, carry):
        for copy in copies(step):
            copy.wait()

        @pl.when(step + slots - 1 < steps)
        def _():
            for copy in copies(step + slots - 1):
                copy.start()

        slot = lax.rem(step, slots)
        rows = rows_ref[slot]
        for first in range(0, width, tile):
            span = slice(first, first + tile)
            acc_ref[:, span] += jnp.dot(rows, slot_ref[slot, :, span], preferred_element_type=F32)
        return carry

    lax.fori_loop(0, steps, body, 0)
    if not last:
        return
    odd = lax.rem(lax.axis_index("col"), 2)
    keep_ref[...] = acc_ref[pl.ds(pl.multiple_of(odd * half, 16), half), :]
    cols = give_refs[0].shape[1]
    for c, give_ref in enumerate(give_refs):
        span = slice(c * cols, (c + 1) * cols)
        give_ref[...] = acc_ref[pl.ds(pl.multiple_of((1 - odd) * half, 16), half), span]


def out_part(grad_train, grad_query, basis_out, prev, acc):
    tokens, depth = grad_train.shape
    width = basis_out.shape[1]
    rows = tokens + grad_query.shape[0]
    block = largest_divisor(depth, (512, 256, 128))
    steps = depth // block
    slots = min(6, steps)
    last = acc is not None
    first = steps * 2 // 7
    begin, count = (first, steps - first) if last else (0, first)
    pieces = pieces_of(width, 2)
    if last:
        out_shape = [shape_of(rows // 2, width, F32)]
        out_shape += [shape_of(rows // 2, width // pieces, F32)] * pieces
    else:
        out_shape = [shape_of(rows, width, F32)]
    return pl.pallas_call(
        functools.partial(out_kernel, begin, count, last),
        in_specs=[ANY_SPEC] * 4 + [VMEM_SPEC] * last,
        out_specs=[VMEM_SPEC] * len(out_shape),
        out_shape=out_shape,
        scratch_shapes=[
            pltpu.VMEM((slots, rows, block), BF16),
            pltpu.VMEM((slots, block, width), BF16),
        ]
        + [pltpu.VMEM((rows, width), F32)] * last
        + [pltpu.SemaphoreType.DMA((slots, 3))],
        compiler_params=pltpu.CompilerParams(vmem_limit_bytes=22 * MIB),
        cost_estimate=cost(2 * rows * block * count * width if last else 1024, 1024),
    )(
        in_hbm(grad_train), in_hbm(grad_query), in_hbm(basis_out), prev, *([acc] if last else [])
    )


def add_kernel(pieces, outs, cast, keep_ref, *refs):
    wide_ref, narrow_refs = refs[pieces + cast + 1], refs[pieces + cast + 2 :]
    width = keep_ref.shape[1]
    cols = width // pieces
    for c in range(pieces):
        span = slice(c * cols, (c + 1) * cols)
        wide_ref[:, span] = keep_ref[:, span] + refs[c][...].astype(F32)
    cols = width // outs
    for c in range(outs):
        narrow_refs[c][...] = wide_ref[:, c * cols : (c + 1) * cols].astype(BF16)
    if cast:
        narrow_refs[outs][...] = refs[pieces][...].astype(BF16)


def add_part(keep, got, prev, outs=1, cast=()):
    rows, width = keep.shape
    out = pl.pallas_call(
        functools.partial(add_kernel, len(got), outs, len(cast)),
        in_specs=[VMEM_SPEC] * (1 + len(got) + len(cast)) + [ANY_SPEC],
        out_specs=[VMEM_SPEC] * (1 + outs + len(cast)),
        out_shape=[shape_of(rows, width, F32)]
        + [shape_of(rows, width // outs, BF16)] * outs
        + [shape_of(*x.shape, BF16) for x in cast],
        compiler_params=pltpu.CompilerParams(vmem_limit_bytes=12 * MIB),
        cost_estimate=cost(1024, 1024),
    )(keep, *got, *cast, prev)
    return out[0], list(out[1:])


def join_kernel(tokens, pieces, prev_ref, *refs):
    mine_refs, other_refs = refs[:pieces], refs[pieces : 2 * pieces]
    gt_ref, gq_ref = refs[2 * pieces :]
    odd = lax.rem(lax.axis_index("col"), 2)
    for c, (mine_ref, other_ref) in enumerate(zip(mine_refs, other_refs)):
        mine, other = mine_ref[...].astype(F32), other_ref[...].astype(F32)
        low = jnp.where(odd == 1, other, mine)
        high = jnp.where(odd == 1, mine, other)
        rows = jnp.concatenate([low, high], axis=0)
        cols = rows.shape[1]
        gt_ref[:, c * cols : (c + 1) * cols] = rows[:tokens].astype(BF16)
        gq_ref[c * cols : (c + 1) * cols, :] = rows[tokens:].T.astype(BF16)


def join_part(mine, other, prev, tokens):
    half = mine[0].shape[0]
    width = sum(x.shape[1] for x in mine)
    queries = 2 * half - tokens
    return pl.pallas_call(
        functools.partial(join_kernel, tokens, len(mine)),
        in_specs=[ANY_SPEC] + [VMEM_SPEC] * (2 * len(mine)),
        out_specs=[VMEM_SPEC] * 2,
        out_shape=[shape_of(tokens, width, BF16), shape_of(width, queries, BF16)],
        compiler_params=pltpu.CompilerParams(vmem_limit_bytes=12 * MIB),
        cost_estimate=cost(1024, 1024),
    )(prev, *mine, *other)


def inverse_kernel(chunks, corr_ref, prev_ref, *refs):
    *inv_refs, slot_ref, sems = refs
    slots, block = slot_ref.shape[0], slot_ref.shape[1]
    steps = corr_ref.shape[0] // block

    def fetch(step):
        rows = pl.ds(step * block, block)
        return pltpu.make_async_copy(
            corr_ref.at[rows, :], slot_ref.at[step % slots], sems.at[step % slots]
        )

    for step in range(min(slots, steps)):
        fetch(step).start()
    for step in range(steps):
        fetch(step).wait()
        for (first, width), inv_ref in zip(chunks, inv_refs):
            value = slot_ref[step % slots, :, first : first + width]
            inv_ref[step * block : (step + 1) * block, :] = 1.0 / value
        if step + slots < steps:
            fetch(step + slots).start()


def inverse_part(correction, prev, chunks):
    rows, width = correction.shape
    block = largest_divisor(rows, (128, 64, 8))
    out = pl.pallas_call(
        functools.partial(inverse_kernel, chunks),
        in_specs=[ANY_SPEC, ANY_SPEC],
        out_specs=[VMEM_SPEC] * len(chunks),
        out_shape=[shape_of(rows, width, F32) for _, width in chunks],
        scratch_shapes=[pltpu.VMEM((4, block, width), F32), pltpu.SemaphoreType.DMA((4,))],
        compiler_params=pltpu.CompilerParams(vmem_limit_bytes=16 * MIB),
        cost_estimate=cost(1024, 1024),
    )(in_hbm(correction), prev)
    return list(out)


def at_end():
    me = lax.axis_index("row")
    return (me == 0) | (me == lax.axis_size("row") - 1)


def pay_kernel(has_part, acc_ref, got_ref, *refs):
    total = acc_ref[...] + got_ref[...].astype(F32)
    if has_part:
        total = jnp.where(at_end(), refs[0][...], total)
    refs[-1][...] = total.astype(BF16)


def pay_part(hint, acc, got, part, prev):
    has_part = part is not None
    return pl.pallas_call(
        functools.partial(pay_kernel, has_part),
        in_specs=[VMEM_SPEC, VMEM_SPEC] + [VMEM_SPEC] * has_part + [ANY_SPEC],
        out_specs=VMEM_SPEC,
        out_shape=shape_of(*acc.shape, BF16),
        compiler_params=pltpu.CompilerParams(vmem_limit_bytes=12 * MIB),
        cost_estimate=cost(hint, 1024),
    )(acc, got, *([part] if has_part else []), prev)


def after_kernel(first_ref, second_ref, out_ref):
    out_ref[...] = jnp.zeros_like(out_ref)


def after_part(first, second):
    return pl.pallas_call(
        after_kernel,
        in_specs=[ANY_SPEC] * 2,
        out_specs=VMEM_SPEC,
        out_shape=shape_of(8, LANES, F32),
        compiler_params=pltpu.CompilerParams(vmem_limit_bytes=4 * MIB),
        cost_estimate=cost(10**9, 1024),
    )(first, second)


def score_kernel(
    start, scale, outs, gt_ref, gq_ref, inv_ref, sent_ref, got_ref, prev_ref, order_ref, *refs
):
    out_refs = refs[:outs]
    quot_ref, wide_ref, own_ref = refs[outs:]
    tokens = gt_ref.shape[0]
    queries = gq_ref.shape[1]
    width = inv_ref.shape[1]
    total = jnp.where(at_end(), got_ref[...].astype(F32), sent_ref[...].astype(F32))
    wide_ref[...] = total[:tokens]
    own_ref[...] = total[tokens:]
    owner = lax.broadcasted_iota(jnp.int32, (queries, width), 0) // LQ
    lane = lax.broadcasted_iota(jnp.int32, (tokens, LANES), 1)

    def quotient(q):
        own = jnp.where(owner == q, own_ref[...], 0.0).astype(BF16)
        products = jnp.dot(gq_ref[...], own, preferred_element_type=F32)
        quot_ref[q % 2] = (products * inv_ref[...]).astype(BF16)

    quotient(0)
    result = jnp.zeros((tokens, LANES), F32) if start else prev_ref[...]
    for q in range(NQ):
        if q + 1 < NQ:
            quotient(q + 1)
        mapped = jnp.dot(gt_ref[...], quot_ref[q % 2], preferred_element_type=F32)
        scaled = mapped * wide_ref[...]
        folded = scaled[:, :LANES]
        for part in range(1, width // LANES):
            folded = folded + scaled[:, part * LANES : (part + 1) * LANES]
        result = result + jnp.where(lane == q, jnp.sum(folded, axis=1, keepdims=True), 0.0)
    if scale is None:
        out_refs[0][...] = result
        return
    final = (result * scale).T[:NQ]
    if outs == 1:
        out_refs[0][...] = final
    else:
        split(final, lax.axis_index("row") // 2, *out_refs)


def split(values, high, keep_ref, give_ref):
    cols = values.shape[1] // 2
    low_half, high_half = values[:, :cols], values[:, cols:]
    keep_ref[...] = jnp.where(high == 1, high_half, low_half)
    give_ref[...] = jnp.where(high == 1, low_half, high_half)


def score_part(rot_gt, rot_gq_t, inv, sent, got, prev, order, start, scale, halves):
    tokens, outs = rot_gt.shape
    width = inv.shape[1]
    queries = rot_gq_t.shape[1]
    if scale is None:
        out_shape = [shape_of(tokens, LANES, F32)]
    elif halves:
        out_shape = [shape_of(NQ, tokens // 2, F32)] * 2
    else:
        out_shape = [shape_of(NQ, tokens, F32)]
    return pl.pallas_call(
        functools.partial(score_kernel, start, scale, len(out_shape)),
        in_specs=[VMEM_SPEC] * 5 + [ANY_SPEC if start else VMEM_SPEC, ANY_SPEC],
        out_specs=[VMEM_SPEC] * len(out_shape),
        out_shape=out_shape,
        scratch_shapes=[
            pltpu.VMEM((2, outs, width), BF16),
            pltpu.VMEM((tokens, width), F32),
            pltpu.VMEM((queries, width), F32),
        ],
        compiler_params=pltpu.CompilerParams(vmem_limit_bytes=16 * MIB),
        cost_estimate=cost(1024, 1024),
    )(rot_gt, rot_gq_t, inv, sent, got, prev, order)


def halve_kernel(keep_ref, got_ref, *refs):
    total = keep_ref[...] + got_ref[...]
    if len(refs) == 1:
        refs[0][...] = total
    else:
        split(total, lax.rem(lax.axis_index("row"), 2), *refs)


def halve_part(keep, got, halves):
    rows, width = keep.shape
    out = [shape_of(rows, width // 2, F32)] * 2 if halves else [shape_of(rows, width, F32)]
    return pl.pallas_call(
        halve_kernel,
        in_specs=[VMEM_SPEC] * 2,
        out_specs=[VMEM_SPEC] * len(out),
        out_shape=out,
        compiler_params=pltpu.CompilerParams(vmem_limit_bytes=4 * MIB),
        cost_estimate=cost(1024, 1024),
    )(keep, got)


def line_sum(partial, axis):
    n = lax.axis_size(axis)
    half = n // 2
    me = lax.axis_index(axis)
    if n % 2:
        return lax.psum(partial, axis).astype(BF16)
    acc = partial
    for s in range(half - 1):
        pairs = [(s, s + 1), (n - 1 - s, n - 2 - s)]
        acc = acc + lax.ppermute(acc.astype(BF16), axis, pairs).astype(F32)
    got = lax.ppermute(acc.astype(BF16), axis, [(half - 1, half), (half, half - 1)])
    total = (acc + got.astype(F32)).astype(BF16)
    for s in range(half - 2, -1, -1):
        pairs = [(s + 1, s), (n - 2 - s, n - 1 - s)]
        got = lax.ppermute(total, axis, pairs)
        total = jnp.where((me == s) | (me == n - 1 - s), got, total)
    return total


def owned_sum(partial, axis):
    n = lax.axis_size(axis)
    me = lax.axis_index(axis)
    total = lax.dynamic_index_in_dim(partial, me, 0, keepdims=False)
    for step in range(1, n):
        block = lax.dynamic_index_in_dim(partial, (me + step) % n, 0, keepdims=False)
        total = total + lax.ppermute(block, axis, [(d, (d + step) % n) for d in range(n)])
    return total


def shared_sum(partial, axis):
    n = lax.axis_size(axis)
    total = partial
    for step in range(1, n):
        total = total + lax.ppermute(partial, axis, [(d, (d + step) % n) for d in range(n)])
    return total


def on_device(act_train, act_query, grad_train, grad_query, basis_in, basis_out, correction):
    norm_scale = (O * I * LQ) ** (-0.5)
    tokens = act_train.shape[0]
    n_row, n_col = lax.axis_size("row"), lax.axis_size("col")
    chunks = chunk_list(basis_in.shape[1])
    count = len(chunks)
    line = n_row == 4
    flip = [(d, d ^ 1) for d in range(n_col)]
    outer = [(0, 1), (1, 0), (2, 3), (3, 2)]
    inner = []
    for c in range(n_col):
        inner += [(n_col + c, 2 * n_col + c), (2 * n_col + c, n_col + c)]
        inner += [(c, c ^ 1), (3 * n_col + c, 3 * n_col + (c ^ 1))]
    sent, got, acc, got_mid = {}, {}, {}, {}

    def swap(j, payload):
        sent[j] = payload
        got[j] = lax.ppermute(payload, "row", outer)

    def meet(j, prev):
        if not line or j >= count:
            return prev
        cast = [parts[2]] if j == 0 else []
        acc[j], thin = add_part(parts[j], [got[j]], prev, 1, cast)
        got_mid[j] = lax.ppermute(thin[0], ("row", "col"), inner)
        if cast:
            swap(2, thin[1])
        return thin[0]

    def pay(j, prev):
        if not line:
            sent[j + LAG] = got[j + LAG] = line_sum(parts[j], "row")
            return prev
        part = parts[j + LAG] if j + LAG < count else None
        payload = pay_part(4 * 10**9 if j == 0 else 1024, acc[j], got_mid[j], part, prev)
        swap(j + LAG, payload)
        return payload

    def score(k, sums, prev):
        return score_part(
            rot_gt, rot_gq_t, invs[k], sent[k + LAG], got[k + LAG], sums[0], prev,
            k == 0, norm_scale if k == count - 1 else None, halves,
        )

    early = min(LAG + 2, count)
    widths = [width for _, width in chunks]
    parts, narrow = in_part(
        act_train, act_query, basis_in, act_query, chunks[:1], [widths[0]]
    )
    if line:
        swap(0, narrow[0])
    more, narrow = in_part(
        act_train, act_query, basis_in, parts[0], chunks[1:early], [widths[1]]
    )
    parts += more
    if line:
        swap(1, narrow[0])
    (half_sum,) = out_part(grad_train, grad_query, basis_out, parts[-1], None)
    prev = meet(0, half_sum)
    keep, *give = out_part(grad_train, grad_query, basis_out, prev, half_sum)
    given = [lax.ppermute(piece, "col", flip) for piece in give]
    prev = meet(1, keep)
    if line:
        prev = after_part(prev, got[2])
    prev = meet(2, pay(0, prev))
    outs = pieces_of(keep.shape[1], 2)
    wide, thin = add_part(keep, given, prev, outs)
    prev, bit = wide, 2
    while bit < n_col:
        other = [lax.ppermute(x, "col", [(d, d ^ bit) for d in range(n_col)]) for x in thin]
        if bit == 2:
            more, _ = in_part(act_train, act_query, basis_in, prev, chunks[early:], [])
            parts += more
            prev = meet(3, pay(1, more[-1]))
            invs = inverse_part(correction, prev, chunks)
            prev = pay(2, invs[0])
        wide, thin = add_part(wide, other, prev, outs)
        prev = wide
        bit *= 2
    other = [lax.ppermute(x, "col", flip) for x in thin]
    prev = meet(5, pay(3, meet(4, prev)))
    rot_gt, rot_gq_t = join_part(thin, other, prev, tokens)
    prev = rot_gt
    halves = n_row == 4 and n_col & (n_col - 1) == 0 and tokens % (n_row * LANES) == 0
    sums = score(0, [rot_gt], prev)
    done = 1
    for j in range(6, count + 1):
        prev = meet(j, pay(j - 2, sums[0]))
        sums = score(done, sums, prev)
        done += 1
    sums = score(done, sums, prev)
    done += 1
    if line:
        prev = after_part(sums[0], got[count])
    prev = pay(count - 1, prev)
    for k in range(done, count):
        sums = score(k, sums, prev)
    if not halves:
        blocks = sums[0].reshape(NQ, n_row, tokens // n_row).transpose(1, 0, 2)
        return shared_sum(owned_sum(blocks, "row"), "col")
    keep, give = sums
    swapped = lax.ppermute(give, "row", [(d, d ^ 2) for d in range(n_row)])
    keep, give = halve_part(keep, swapped, True)
    (keep,) = halve_part(keep, lax.ppermute(give, "row", outer), False)
    bit = 1
    while bit < n_col:
        swapped = lax.ppermute(keep, "col", [(d, d ^ bit) for d in range(n_col)])
        (keep,) = halve_part(keep, swapped, False)
        bit *= 2
    return keep


def solution(mesh):
    in_specs = (
        P("groups", "row"),
        P("groups", "row"),
        P("groups", "col"),
        P("groups", "col"),
        P(("groups", "row"), "col"),
        P(("groups", "col"), "row"),
        P(("groups", "row"), "col"),
    )
    out_specs = P("groups", "row")
    return jax.shard_map(
        on_device, mesh=mesh, in_specs=in_specs, out_specs=out_specs, check_vma=False
    )
```

```python
import functools

import jax
import jax.numpy as jnp
from jax import lax
from jax.experimental import pallas as pl
from jax.experimental.pallas import tpu as pltpu
from jax.sharding import PartitionSpec as P

I = 8192
O = 4096
NQ = 8
LQ = 16
LANES = 128
CHUNKS = 8
LAG = 3
F32 = jnp.float32
BF16 = jnp.bfloat16
MIB = 1 << 20

VMEM_SPEC = pl.BlockSpec(memory_space=pltpu.VMEM)
SMEM_SPEC = pl.BlockSpec(memory_space=pltpu.SMEM)
ANY_SPEC = pl.BlockSpec(memory_space=pl.ANY)


def shape_of(rows, width, dtype):
    return jax.ShapeDtypeStruct((rows, width), dtype)


def chunk_list(size):
    tiles = size // LANES
    count = min(CHUNKS, tiles)
    chunks, first = [], 0
    for k in range(count):
        width = LANES * (tiles // count + (1 if k < tiles % count else 0))
        chunks.append((first, width))
        first += width
    return chunks


def largest_divisor(size, choices):
    for choice in choices:
        if size % choice == 0:
            return choice
    return size


def pieces_of(width, most):
    return max(p for p in range(1, most + 1) if width % (p * LANES) == 0)


def cost(flops, bytes_accessed):
    return pl.CostEstimate(flops=flops, bytes_accessed=bytes_accessed, transcendentals=0)


def in_hbm(x):
    return pltpu.with_memory_space_constraint(x, pltpu.HBM)


def halves_dot(rows, basis):
    half = rows.shape[0] // 2
    return [jnp.dot(part, basis, preferred_element_type=F32) for part in (rows[:half], rows[half:])]


def in_kernel(chunks, narrow, groups, train_ref, query_ref, basis_ref, prev_ref, *refs):
    count = len(chunks)
    rows_ref, slot_ref, sum_ref, sems = refs[count + narrow :]
    tokens, queries = train_ref.shape[0], query_ref.shape[0]
    start, total = chunks[0][0], slot_ref.shape[1]
    depth = basis_ref.shape[0] // groups
    copies = []
    for g in range(groups):
        part = pl.ds(g * depth, depth)
        copies.append([
            pltpu.make_async_copy(
                basis_ref.at[part, pl.ds(start, total)], slot_ref.at[part, :], sems.at[g, 0]
            ),
            pltpu.make_async_copy(
                train_ref.at[:, part], rows_ref.at[pl.ds(0, tokens), part], sems.at[g, 1]
            ),
            pltpu.make_async_copy(
                query_ref.at[:, part], rows_ref.at[pl.ds(tokens, queries), part], sems.at[g, 2]
            ),
        ])
    for group in copies:
        for copy in group:
            copy.start()
    for g, group in enumerate(copies):
        for copy in group:
            copy.wait()
        part = slice(g * depth, (g + 1) * depth)
        half = rows_ref.shape[0] // 2
        for h, value in enumerate(halves_dot(rows_ref[:, part], slot_ref[part, :])):
            span = slice(h * half, (h + 1) * half)
            if g == 0:
                sum_ref[span, :] = value
            else:
                sum_ref[span, :] += value
    for j, (first, width) in enumerate(chunks):
        refs[j][...] = sum_ref[:, first - start : first - start + width]
    column = 0
    for narrow_ref in refs[count : count + narrow]:
        width = narrow_ref.shape[1]
        narrow_ref[...] = sum_ref[:, column : column + width].astype(BF16)
        column += width


def in_part(act_train, act_query, basis_in, prev, chunks, narrow):
    tokens, depth = act_train.shape
    rows = tokens + act_query.shape[0]
    total = sum(width for _, width in chunks)
    groups = next(g for g in (4, 2, 1) if depth % (g * LANES) == 0)
    shapes = [shape_of(rows, width, F32) for _, width in chunks]
    shapes += [shape_of(rows, width, BF16) for width in narrow]
    out = pl.pallas_call(
        functools.partial(in_kernel, chunks, len(narrow), groups),
        in_specs=[ANY_SPEC] * 4,
        out_specs=[VMEM_SPEC] * len(shapes),
        out_shape=shapes,
        scratch_shapes=[
            pltpu.VMEM((rows, depth), BF16),
            pltpu.VMEM((depth, total), BF16),
            pltpu.VMEM((rows, total), F32),
            pltpu.SemaphoreType.DMA((groups, 3)),
        ],
        compiler_params=pltpu.CompilerParams(vmem_limit_bytes=24 * MIB),
        cost_estimate=cost(1024, 1024),
    )(in_hbm(act_train), in_hbm(act_query), in_hbm(basis_in), prev)
    return list(out[: len(chunks)]), list(out[len(chunks) :])


def out_kernel(begin, column, groups, block, chained, last, held, *refs):
    refs = list(refs)
    if held:
        row_refs = [refs.pop(0) for _ in range(held)]
    else:
        train_ref, query_ref = refs.pop(0), refs.pop(0)
    basis_ref, _ = refs.pop(0), refs.pop(0)
    start_ref = refs.pop(0) if chained else None
    slot_ref, sems = refs[-2:]
    acc_ref = refs[-3] if last else refs[0]
    rows, width = acc_ref.shape
    half = rows // 2
    tile = largest_divisor(width, (256, 128))
    if not held:
        row_refs = [refs[2] if last else refs[1]]
        tokens, queries = train_ref.shape[0], query_ref.shape[0]
    copies = []
    for unit in range(sum(groups)):
        there = pl.ds((begin + unit) * block, block)
        here = pl.ds(unit * block, block)
        arriving = [
            pltpu.make_async_copy(
                basis_ref.at[there, pl.ds(column, width)], slot_ref.at[here, :], sems.at[unit, 0]
            )
        ]
        if not held:
            arriving += [
                pltpu.make_async_copy(
                    train_ref.at[:, there], row_refs[0].at[pl.ds(0, tokens), here], sems.at[unit, 1]
                ),
                pltpu.make_async_copy(
                    query_ref.at[:, there],
                    row_refs[0].at[pl.ds(tokens, queries), here],
                    sems.at[unit, 2],
                ),
            ]
        copies.append(arriving)
    for arriving in copies:
        for copy in arriving:
            copy.start()
    unit = 0
    for g, group in enumerate(groups):
        for arriving in copies[unit : unit + group]:
            for copy in arriving:
                copy.wait()
        first = unit * block
        depth = group * block
        unit += group
        row_ref, skip = row_refs[0], 0
        if held and first >= row_refs[0].shape[1]:
            row_ref, skip = row_refs[1], row_refs[0].shape[1]
        left = row_ref[:, first - skip : first - skip + depth]
        for c in range(0, width, tile):
            span = slice(c, c + tile)
            part = jnp.dot(
                left, slot_ref[first : first + depth, span], preferred_element_type=F32
            )
            if g > 0:
                part = part + acc_ref[:, span]
            elif chained:
                part = part + start_ref[:, span]
            acc_ref[:, span] = part
    if last:
        keep_ref, give_ref = refs[:2]
        odd = lax.rem(lax.axis_index("col"), 2)
        keep_ref[...] = acc_ref[pl.ds(pl.multiple_of(odd * half, 16), half), :]
        give_ref[...] = acc_ref[pl.ds(pl.multiple_of((1 - odd) * half, 16), half), :]


def out_part(rows, fresh, basis_out, prev, acc, begin, units, block, column, width, last):
    count = sum(units)
    total = rows[0].shape[0] + rows[1].shape[0] if fresh else rows[0].shape[0]
    if last:
        out_shape = [shape_of(total // 2, width, F32)] * 2
    else:
        out_shape = [shape_of(total, width, F32)]
    if fresh:
        out_shape.append(shape_of(total, count * block, BF16))
    chained = acc is not None
    return pl.pallas_call(
        functools.partial(
            out_kernel, begin, column, units, block, chained, last, 0 if fresh else len(rows)
        ),
        in_specs=[ANY_SPEC if fresh else VMEM_SPEC] * len(rows)
        + [ANY_SPEC] * 2
        + [VMEM_SPEC] * chained,
        out_specs=[VMEM_SPEC] * len(out_shape),
        out_shape=out_shape,
        scratch_shapes=[pltpu.VMEM((total, width), F32)] * last
        + [pltpu.VMEM((count * block, width), BF16), pltpu.SemaphoreType.DMA((count, 3))],
        compiler_params=pltpu.CompilerParams(vmem_limit_bytes=20 * MIB),
        cost_estimate=cost(1024, 1024),
    )(
        *([in_hbm(x) for x in rows] if fresh else rows),
        in_hbm(basis_out),
        prev,
        *([acc] if chained else []),
    )


def unit_groups(count):
    groups = [1] + [2] * ((count - 1) // 2)
    return groups + [1] * (count - sum(groups))


def add_kernel(pieces, outs, cast, keep_ref, *refs):
    wide_ref, narrow_refs = refs[pieces + cast + 1], refs[pieces + cast + 2 :]
    width = keep_ref.shape[1]
    cols = width // pieces
    for c in range(pieces):
        span = slice(c * cols, (c + 1) * cols)
        wide_ref[:, span] = keep_ref[:, span] + refs[c][...].astype(F32)
    cols = width // outs
    for c in range(outs):
        narrow_refs[c][...] = wide_ref[:, c * cols : (c + 1) * cols].astype(BF16)
    if cast:
        narrow_refs[outs][...] = refs[pieces][...].astype(BF16)


def add_part(keep, got, prev, outs=1, cast=(), hint=1024):
    rows, width = keep.shape
    out = pl.pallas_call(
        functools.partial(add_kernel, len(got), outs, len(cast)),
        in_specs=[VMEM_SPEC] * (1 + len(got) + len(cast)) + [ANY_SPEC],
        out_specs=[VMEM_SPEC] * (1 + outs + len(cast)),
        out_shape=[shape_of(rows, width, F32)]
        + [shape_of(rows, width // outs, BF16)] * outs
        + [shape_of(*x.shape, BF16) for x in cast],
        compiler_params=pltpu.CompilerParams(vmem_limit_bytes=12 * MIB),
        cost_estimate=cost(hint, 1024),
    )(keep, *got, *cast, prev)
    return out[0], list(out[1:])


def join_kernel(tokens, pieces, prev_ref, *refs):
    mine_refs, other_refs = refs[:pieces], refs[pieces : 2 * pieces]
    gt_ref, gq_ref = refs[2 * pieces :]
    odd = lax.rem(lax.axis_index("col"), 2)
    for c, (mine_ref, other_ref) in enumerate(zip(mine_refs, other_refs)):
        mine, other = mine_ref[...].astype(F32), other_ref[...].astype(F32)
        low = jnp.where(odd == 1, other, mine)
        high = jnp.where(odd == 1, mine, other)
        rows = jnp.concatenate([low, high], axis=0)
        cols = rows.shape[1]
        gt_ref[:, c * cols : (c + 1) * cols] = rows[:tokens].astype(BF16)
        gq_ref[c * cols : (c + 1) * cols, :] = rows[tokens:].T.astype(BF16)


def join_part(mine, other, prev, tokens):
    half = mine[0].shape[0]
    width = sum(x.shape[1] for x in mine)
    queries = 2 * half - tokens
    return pl.pallas_call(
        functools.partial(join_kernel, tokens, len(mine)),
        in_specs=[ANY_SPEC] + [VMEM_SPEC] * (2 * len(mine)),
        out_specs=[VMEM_SPEC] * 2,
        out_shape=[shape_of(tokens, width, BF16), shape_of(width, queries, BF16)],
        compiler_params=pltpu.CompilerParams(vmem_limit_bytes=12 * MIB),
        cost_estimate=cost(1024, 1024),
    )(prev, *mine, *other)


def inverse_kernel(chunks, corr_ref, prev_ref, *refs):
    *inv_refs, slot_ref, sems = refs
    slots, block = slot_ref.shape[0], slot_ref.shape[1]
    steps = corr_ref.shape[0] // block

    def fetch(step):
        rows = pl.ds(step * block, block)
        return pltpu.make_async_copy(
            corr_ref.at[rows, :], slot_ref.at[step % slots], sems.at[step % slots]
        )

    for step in range(min(slots, steps)):
        fetch(step).start()
    for step in range(steps):
        fetch(step).wait()
        for (first, width), inv_ref in zip(chunks, inv_refs):
            value = slot_ref[step % slots, :, first : first + width]
            inv_ref[step * block : (step + 1) * block, :] = 1.0 / value
        if step + slots < steps:
            fetch(step + slots).start()


def inverse_part(correction, prev, chunks):
    rows, width = correction.shape
    block = largest_divisor(rows, (128, 64, 8))
    out = pl.pallas_call(
        functools.partial(inverse_kernel, chunks),
        in_specs=[ANY_SPEC, ANY_SPEC],
        out_specs=[VMEM_SPEC] * len(chunks),
        out_shape=[shape_of(rows, width, F32) for _, width in chunks],
        scratch_shapes=[pltpu.VMEM((4, block, width), F32), pltpu.SemaphoreType.DMA((4,))],
        compiler_params=pltpu.CompilerParams(vmem_limit_bytes=16 * MIB),
        cost_estimate=cost(1024, 1024),
    )(in_hbm(correction), prev)
    return list(out)


def at_end():
    me = lax.axis_index("row")
    return (me == 0) | (me == lax.axis_size("row") - 1)


def pay_kernel(has_part, acc_ref, got_ref, *refs):
    total = acc_ref[...] + got_ref[...].astype(F32)
    if has_part:
        total = jnp.where(at_end(), refs[0][...], total)
    refs[-1][...] = total.astype(BF16)


def pay_part(hint, acc, got, part, prev):
    has_part = part is not None
    return pl.pallas_call(
        functools.partial(pay_kernel, has_part),
        in_specs=[VMEM_SPEC, VMEM_SPEC] + [VMEM_SPEC] * has_part + [ANY_SPEC],
        out_specs=VMEM_SPEC,
        out_shape=shape_of(*acc.shape, BF16),
        compiler_params=pltpu.CompilerParams(vmem_limit_bytes=12 * MIB),
        cost_estimate=cost(hint, 1024),
    )(acc, got, *([part] if has_part else []), prev)


def after_kernel(first_ref, second_ref, out_ref):
    out_ref[...] = jnp.zeros_like(out_ref)


def after_part(first, second):
    return pl.pallas_call(
        after_kernel,
        in_specs=[ANY_SPEC] * 2,
        out_specs=VMEM_SPEC,
        out_shape=shape_of(8, LANES, F32),
        compiler_params=pltpu.CompilerParams(vmem_limit_bytes=4 * MIB),
        cost_estimate=cost(10**9, 1024),
    )(first, second)


def score_kernel(
    start, scale, outs, gt_ref, gq_ref, inv_ref, sent_ref, got_ref, prev_ref, order_ref, *refs
):
    out_refs = refs[:outs]
    quot_ref, wide_ref, own_ref = refs[outs:]
    tokens = gt_ref.shape[0]
    queries = gq_ref.shape[1]
    width = inv_ref.shape[1]
    total = jnp.where(at_end(), got_ref[...].astype(F32), sent_ref[...].astype(F32))
    wide_ref[...] = total[:tokens]
    own_ref[...] = total[tokens:]
    owner = lax.broadcasted_iota(jnp.int32, (queries, width), 0) // LQ
    lane = lax.broadcasted_iota(jnp.int32, (tokens, LANES), 1)

    def quotient(q):
        own = jnp.where(owner == q, own_ref[...], 0.0).astype(BF16)
        products = jnp.dot(gq_ref[...], own, preferred_element_type=F32)
        quot_ref[q % 2] = (products * inv_ref[...]).astype(BF16)

    quotient(0)
    result = jnp.zeros((tokens, LANES), F32) if start else prev_ref[...]
    for q in range(NQ):
        if q + 1 < NQ:
            quotient(q + 1)
        mapped = jnp.dot(gt_ref[...], quot_ref[q % 2], preferred_element_type=F32)
        scaled = mapped * wide_ref[...]
        folded = scaled[:, :LANES]
        for part in range(1, width // LANES):
            folded = folded + scaled[:, part * LANES : (part + 1) * LANES]
        result = result + jnp.where(lane == q, jnp.sum(folded, axis=1, keepdims=True), 0.0)
    if scale is None:
        out_refs[0][...] = result
        return
    final = (result * scale).T[:NQ]
    if outs == 1:
        out_refs[0][...] = final
    else:
        split(final, lax.axis_index("row") // 2, *out_refs)


def split(values, high, keep_ref, give_ref):
    cols = values.shape[1] // 2
    low_half, high_half = values[:, :cols], values[:, cols:]
    keep_ref[...] = jnp.where(high == 1, high_half, low_half)
    give_ref[...] = jnp.where(high == 1, low_half, high_half)


def score_part(rot_gt, rot_gq_t, inv, sent, got, prev, order, start, scale, halves):
    tokens, outs = rot_gt.shape
    width = inv.shape[1]
    queries = rot_gq_t.shape[1]
    if scale is None:
        out_shape = [shape_of(tokens, LANES, F32)]
    elif halves:
        out_shape = [shape_of(NQ, tokens // 2, F32)] * 2
    else:
        out_shape = [shape_of(NQ, tokens, F32)]
    return pl.pallas_call(
        functools.partial(score_kernel, start, scale, len(out_shape)),
        in_specs=[VMEM_SPEC] * 5 + [ANY_SPEC if start else VMEM_SPEC, ANY_SPEC],
        out_specs=[VMEM_SPEC] * len(out_shape),
        out_shape=out_shape,
        scratch_shapes=[
            pltpu.VMEM((2, outs, width), BF16),
            pltpu.VMEM((tokens, width), F32),
            pltpu.VMEM((queries, width), F32),
        ],
        compiler_params=pltpu.CompilerParams(vmem_limit_bytes=16 * MIB),
        cost_estimate=cost(1024, 1024),
    )(rot_gt, rot_gq_t, inv, sent, got, prev, order)


def halve_kernel(keep_ref, got_ref, *refs):
    total = keep_ref[...] + got_ref[...]
    if len(refs) == 1:
        refs[0][...] = total
    else:
        split(total, lax.rem(lax.axis_index("row"), 2), *refs)


def halve_part(keep, got, halves):
    rows, width = keep.shape
    out = [shape_of(rows, width // 2, F32)] * 2 if halves else [shape_of(rows, width, F32)]
    return pl.pallas_call(
        halve_kernel,
        in_specs=[VMEM_SPEC] * 2,
        out_specs=[VMEM_SPEC] * len(out),
        out_shape=out,
        compiler_params=pltpu.CompilerParams(vmem_limit_bytes=4 * MIB),
        cost_estimate=cost(1024, 1024),
    )(keep, got)


def line_sum(partial, axis):
    n = lax.axis_size(axis)
    half = n // 2
    me = lax.axis_index(axis)
    if n % 2:
        return lax.psum(partial, axis).astype(BF16)
    acc = partial
    for s in range(half - 1):
        pairs = [(s, s + 1), (n - 1 - s, n - 2 - s)]
        acc = acc + lax.ppermute(acc.astype(BF16), axis, pairs).astype(F32)
    got = lax.ppermute(acc.astype(BF16), axis, [(half - 1, half), (half, half - 1)])
    total = (acc + got.astype(F32)).astype(BF16)
    for s in range(half - 2, -1, -1):
        pairs = [(s + 1, s), (n - 2 - s, n - 1 - s)]
        got = lax.ppermute(total, axis, pairs)
        total = jnp.where((me == s) | (me == n - 1 - s), got, total)
    return total


def owned_sum(partial, axis):
    n = lax.axis_size(axis)
    me = lax.axis_index(axis)
    total = lax.dynamic_index_in_dim(partial, me, 0, keepdims=False)
    for step in range(1, n):
        block = lax.dynamic_index_in_dim(partial, (me + step) % n, 0, keepdims=False)
        total = total + lax.ppermute(block, axis, [(d, (d + step) % n) for d in range(n)])
    return total


def shared_sum(partial, axis):
    n = lax.axis_size(axis)
    total = partial
    for step in range(1, n):
        total = total + lax.ppermute(partial, axis, [(d, (d + step) % n) for d in range(n)])
    return total


def on_device(act_train, act_query, grad_train, grad_query, basis_in, basis_out, correction):
    norm_scale = (O * I * LQ) ** (-0.5)
    tokens = act_train.shape[0]
    n_row, n_col = lax.axis_size("row"), lax.axis_size("col")
    chunks = chunk_list(basis_in.shape[1])
    count = len(chunks)
    line = n_row == 4
    flip = [(d, d ^ 1) for d in range(n_col)]
    outer = [(0, 1), (1, 0), (2, 3), (3, 2)]
    inner = []
    for c in range(n_col):
        inner += [(n_col + c, 2 * n_col + c), (2 * n_col + c, n_col + c)]
        inner += [(c, c ^ 1), (3 * n_col + c, 3 * n_col + (c ^ 1))]
    sent, got, acc, got_mid = {}, {}, {}, {}

    def swap(j, payload):
        sent[j] = payload
        got[j] = lax.ppermute(payload, "row", outer)

    def meet(j, prev):
        if not line or j >= count:
            return prev
        cast = [parts[2]] if j == 0 else []
        acc[j], thin = add_part(parts[j], [got[j]], prev, 1, cast, 4 * 10**9 if j == 3 else 1024)
        got_mid[j] = lax.ppermute(thin[0], ("row", "col"), inner)
        if cast:
            swap(2, thin[1])
        return thin[0]

    def pay(j, prev):
        if not line:
            sent[j + LAG] = got[j + LAG] = line_sum(parts[j], "row")
            return prev
        part = parts[j + LAG] if j + LAG < count else None
        payload = pay_part(4 * 10**9 if j == 0 else 1024, acc[j], got_mid[j], part, prev)
        swap(j + LAG, payload)
        return payload

    def score(k, sums, prev):
        return score_part(
            rot_gt, rot_gq_t, invs[k], sent[k + LAG], got[k + LAG], sums[0], prev,
            k == 0, norm_scale if k == count - 1 else None, halves,
        )

    early = min(LAG + 2, count)
    widths = [width for _, width in chunks]
    parts, narrow = in_part(
        act_train, act_query, basis_in, act_query, chunks[:1], [widths[0]]
    )
    if line:
        swap(0, narrow[0])
    more, narrow = in_part(
        act_train, act_query, basis_in, parts[0], chunks[1:early], [widths[1]]
    )
    parts += more
    if line:
        swap(1, narrow[0])
    block = largest_divisor(grad_train.shape[1], (512, 256, 128))
    units = grad_train.shape[1] // block
    near = units // 2
    outs = basis_out.shape[1]
    pieces = pieces_of(outs, 2)
    piece = outs // pieces
    grads = (grad_train, grad_query)
    bits = []
    while 2 << len(bits) < n_col:
        bits.append(2 << len(bits))

    def over(x, bit):
        return lax.ppermute(x, "col", [(d, d ^ bit) for d in range(n_col)])

    def settle(wide, other, prev, hint=1024):
        for bit in bits[1:] + [0]:
            wide, (thin,) = add_part(wide, [other], prev, 1, (), hint)
            other = over(thin, bit) if bit else None
        return thin

    def add_given(keep, given, prev):
        wide, (thin,) = add_part(keep, [given], prev)
        return wide, over(thin, bits[0]) if bits else thin

    part_sum, held = out_part(
        grads, True, basis_out, parts[-1], None, 0, unit_groups(near), block, 0, piece, False
    )
    prev = meet(0, part_sum)
    keep, give, more_held = out_part(
        grads, True, basis_out, prev, part_sum, near, unit_groups(units - near), block, 0, piece, True
    )
    given = over(give, 1)
    prev = meet(1, keep)
    if line:
        prev = after_part(prev, got[2])
    prev = pay(0, prev)
    wide, other = add_given(keep, given, prev)
    prev = wide
    later = pieces == 2
    if later:
        all_units = unit_groups(near) + unit_groups(units - near)
        keep2, give2 = out_part(
            (held, more_held), False, basis_out, prev, None, 0, all_units, block, piece, piece, True
        )
        given2 = over(give2, 1)
        prev = keep2
    prev = meet(3, pay(1, meet(2, prev)))
    mine = [settle(wide, other, prev, 4 * 10**9)]
    theirs = [over(mine[0], 1)]
    prev = mine[0]
    if later:
        wide, other = add_given(keep2, given2, prev)
        prev = wide
    more, _ = in_part(act_train, act_query, basis_in, prev, chunks[early:], [])
    parts += more
    prev = meet(4, pay(2, more[-1]))
    invs = inverse_part(correction, prev, chunks)
    prev = invs[0]
    if later:
        mine.append(settle(wide, other, prev))
        theirs.append(over(mine[1], 1))
        prev = mine[1]
    prev = meet(5, pay(3, prev))
    rot_gt, rot_gq_t = join_part(mine, theirs, prev, tokens)
    prev = rot_gt
    halves = n_row == 4 and n_col & (n_col - 1) == 0 and tokens % (n_row * LANES) == 0
    sums = score(0, [rot_gt], prev)
    done = 1
    for j in range(6, count + 1):
        prev = meet(j, pay(j - 2, sums[0]))
        sums = score(done, sums, prev)
        done += 1
    if line:
        prev = after_part(sums[0], got[count])
    prev = pay(count - 1, prev)
    for k in range(done, count):
        sums = score(k, sums, prev)
    if not halves:
        blocks = sums[0].reshape(NQ, n_row, tokens // n_row).transpose(1, 0, 2)
        return shared_sum(owned_sum(blocks, "row"), "col")
    keep, give = sums
    swapped = lax.ppermute(give, "row", [(d, d ^ 2) for d in range(n_row)])
    keep, give = halve_part(keep, swapped, True)
    (keep,) = halve_part(keep, lax.ppermute(give, "row", outer), False)
    bit = 1
    while bit < n_col:
        swapped = lax.ppermute(keep, "col", [(d, d ^ bit) for d in range(n_col)])
        (keep,) = halve_part(keep, swapped, False)
        bit *= 2
    return keep


def solution(mesh):
    in_specs = (
        P("groups", "row"),
        P("groups", "row"),
        P("groups", "col"),
        P("groups", "col"),
        P(("groups", "row"), "col"),
        P(("groups", "col"), "row"),
        P(("groups", "row"), "col"),
    )
    out_specs = P("groups", "row")
    return jax.shard_map(
        on_device, mesh=mesh, in_specs=in_specs, out_specs=out_specs, check_vma=False
    )
```

```python
import functools

import jax
import jax.numpy as jnp
from jax import lax
from jax.experimental import pallas as pl
from jax.experimental.pallas import tpu as pltpu
from jax.sharding import PartitionSpec as P

I = 8192
O = 4096
NQ = 8
LQ = 16
LANES = 128
CHUNKS = 8
LAG = 3
F32 = jnp.float32
BF16 = jnp.bfloat16
MIB = 1 << 20

VMEM_SPEC = pl.BlockSpec(memory_space=pltpu.VMEM)
SMEM_SPEC = pl.BlockSpec(memory_space=pltpu.SMEM)
ANY_SPEC = pl.BlockSpec(memory_space=pl.ANY)


def shape_of(rows, width, dtype):
    return jax.ShapeDtypeStruct((rows, width), dtype)


def chunk_list(size):
    tiles = size // LANES
    count = min(CHUNKS, tiles)
    chunks, first = [], 0
    for k in range(count):
        width = LANES * (tiles // count + (1 if k < tiles % count else 0))
        chunks.append((first, width))
        first += width
    return chunks


def largest_divisor(size, choices):
    for choice in choices:
        if size % choice == 0:
            return choice
    return size


def pieces_of(width, most):
    return max(p for p in range(1, most + 1) if width % (p * LANES) == 0)


def cost(flops, bytes_accessed):
    return pl.CostEstimate(flops=flops, bytes_accessed=bytes_accessed, transcendentals=0)


def in_hbm(x):
    return pltpu.with_memory_space_constraint(x, pltpu.HBM)


def halves_dot(rows, basis):
    half = rows.shape[0] // 2
    return [jnp.dot(part, basis, preferred_element_type=F32) for part in (rows[:half], rows[half:])]


def in_kernel(chunks, narrow, groups, train_ref, query_ref, basis_ref, prev_ref, *refs):
    count = len(chunks)
    rows_ref, slot_ref, sum_ref, sems = refs[count + narrow :]
    tokens, queries = train_ref.shape[0], query_ref.shape[0]
    start, total = chunks[0][0], slot_ref.shape[1]
    depth = basis_ref.shape[0] // groups
    copies = []
    for g in range(groups):
        part = pl.ds(g * depth, depth)
        copies.append([
            pltpu.make_async_copy(
                basis_ref.at[part, pl.ds(start, total)], slot_ref.at[part, :], sems.at[g, 0]
            ),
            pltpu.make_async_copy(
                train_ref.at[:, part], rows_ref.at[pl.ds(0, tokens), part], sems.at[g, 1]
            ),
            pltpu.make_async_copy(
                query_ref.at[:, part], rows_ref.at[pl.ds(tokens, queries), part], sems.at[g, 2]
            ),
        ])
    for group in copies:
        for copy in group:
            copy.start()
    for g, group in enumerate(copies):
        for copy in group:
            copy.wait()
        part = slice(g * depth, (g + 1) * depth)
        half = rows_ref.shape[0] // 2
        for h, value in enumerate(halves_dot(rows_ref[:, part], slot_ref[part, :])):
            span = slice(h * half, (h + 1) * half)
            if g == 0:
                sum_ref[span, :] = value
            else:
                sum_ref[span, :] += value
    for j, (first, width) in enumerate(chunks):
        refs[j][...] = sum_ref[:, first - start : first - start + width]
    column = 0
    for narrow_ref in refs[count : count + narrow]:
        width = narrow_ref.shape[1]
        narrow_ref[...] = sum_ref[:, column : column + width].astype(BF16)
        column += width


def in_part(act_train, act_query, basis_in, prev, chunks, narrow):
    tokens, depth = act_train.shape
    rows = tokens + act_query.shape[0]
    total = sum(width for _, width in chunks)
    groups = next(g for g in (4, 2, 1) if depth % (g * LANES) == 0)
    shapes = [shape_of(rows, width, F32) for _, width in chunks]
    shapes += [shape_of(rows, width, BF16) for width in narrow]
    out = pl.pallas_call(
        functools.partial(in_kernel, chunks, len(narrow), groups),
        in_specs=[ANY_SPEC] * 4,
        out_specs=[VMEM_SPEC] * len(shapes),
        out_shape=shapes,
        scratch_shapes=[
            pltpu.VMEM((rows, depth), BF16),
            pltpu.VMEM((depth, total), BF16),
            pltpu.VMEM((rows, total), F32),
            pltpu.SemaphoreType.DMA((groups, 3)),
        ],
        compiler_params=pltpu.CompilerParams(vmem_limit_bytes=24 * MIB),
        cost_estimate=cost(1024, 1024),
    )(in_hbm(act_train), in_hbm(act_query), in_hbm(basis_in), prev)
    return list(out[: len(chunks)]), list(out[len(chunks) :])


def out_kernel(begin, steps, last, train_ref, query_ref, basis_ref, prev_ref, *refs):
    if last:
        start_ref, keep_ref, *give_refs, rows_ref, slot_ref, acc_ref, sems = refs
    else:
        acc_ref, rows_ref, slot_ref, sems = refs
    tokens, queries = train_ref.shape[0], query_ref.shape[0]
    slots, block = slot_ref.shape[0], slot_ref.shape[1]
    half, width = acc_ref.shape[0] // 2, acc_ref.shape[1]
    tile = largest_divisor(width, (256, 128))

    def copies(step):
        slot = lax.rem(step, slots)
        part = pl.ds(pl.multiple_of((begin + step) * block, block), block)
        return [
            pltpu.make_async_copy(basis_ref.at[part, :], slot_ref.at[slot], sems.at[slot, 0]),
            pltpu.make_async_copy(
                train_ref.at[:, part], rows_ref.at[slot, pl.ds(0, tokens), :], sems.at[slot, 1]
            ),
            pltpu.make_async_copy(
                query_ref.at[:, part], rows_ref.at[slot, pl.ds(tokens, queries), :], sems.at[slot, 2]
            ),
        ]

    for step in range(min(slots - 1, steps)):
        for copy in copies(step):
            copy.start()
    acc_ref[...] = start_ref[...] if last else jnp.zeros_like(acc_ref)

    def body(step, carry):
        for copy in copies(step):
            copy.wait()

        @pl.when(step + slots - 1 < steps)
        def _():
            for copy in copies(step + slots - 1):
                copy.start()

        slot = lax.rem(step, slots)
        rows = rows_ref[slot]
        for first in range(0, width, tile):
            span = slice(first, first + tile)
            acc_ref[:, span] += jnp.dot(rows, slot_ref[slot, :, span], preferred_element_type=F32)
        return carry

    lax.fori_loop(0, steps, body, 0)
    if not last:
        return
    odd = lax.rem(lax.axis_index("col"), 2)
    keep_ref[...] = acc_ref[pl.ds(pl.multiple_of(odd * half, 16), half), :]
    cols = give_refs[0].shape[1]
    for c, give_ref in enumerate(give_refs):
        span = slice(c * cols, (c + 1) * cols)
        give_ref[...] = acc_ref[pl.ds(pl.multiple_of((1 - odd) * half, 16), half), span]


def out_part(grad_train, grad_query, basis_out, prev, acc):
    tokens, depth = grad_train.shape
    width = basis_out.shape[1]
    rows = tokens + grad_query.shape[0]
    block = largest_divisor(depth, (512, 256, 128))
    steps = depth // block
    slots = min(6, steps)
    last = acc is not None
    first = steps * 2 // 7
    begin, count = (first, steps - first) if last else (0, first)
    pieces = pieces_of(width, 2)
    if last:
        out_shape = [shape_of(rows // 2, width, F32)]
        out_shape += [shape_of(rows // 2, width // pieces, F32)] * pieces
    else:
        out_shape = [shape_of(rows, width, F32)]
    return pl.pallas_call(
        functools.partial(out_kernel, begin, count, last),
        in_specs=[ANY_SPEC] * 4 + [VMEM_SPEC] * last,
        out_specs=[VMEM_SPEC] * len(out_shape),
        out_shape=out_shape,
        scratch_shapes=[
            pltpu.VMEM((slots, rows, block), BF16),
            pltpu.VMEM((slots, block, width), BF16),
        ]
        + [pltpu.VMEM((rows, width), F32)] * last
        + [pltpu.SemaphoreType.DMA((slots, 3))],
        compiler_params=pltpu.CompilerParams(vmem_limit_bytes=22 * MIB),
        cost_estimate=cost(2 * rows * block * count * width if last else 1024, 1024),
    )(
        in_hbm(grad_train), in_hbm(grad_query), in_hbm(basis_out), prev, *([acc] if last else [])
    )


def add_kernel(pieces, outs, cast, keep_ref, *refs):
    wide_ref, narrow_refs = refs[pieces + cast + 1], refs[pieces + cast + 2 :]
    width = keep_ref.shape[1]
    cols = width // pieces
    for c in range(pieces):
        span = slice(c * cols, (c + 1) * cols)
        wide_ref[:, span] = keep_ref[:, span] + refs[c][...].astype(F32)
    cols = width // outs
    for c in range(outs):
        narrow_refs[c][...] = wide_ref[:, c * cols : (c + 1) * cols].astype(BF16)
    if cast:
        narrow_refs[outs][...] = refs[pieces][...].astype(BF16)


def add_part(keep, got, prev, outs=1, cast=()):
    rows, width = keep.shape
    out = pl.pallas_call(
        functools.partial(add_kernel, len(got), outs, len(cast)),
        in_specs=[VMEM_SPEC] * (1 + len(got) + len(cast)) + [ANY_SPEC],
        out_specs=[VMEM_SPEC] * (1 + outs + len(cast)),
        out_shape=[shape_of(rows, width, F32)]
        + [shape_of(rows, width // outs, BF16)] * outs
        + [shape_of(*x.shape, BF16) for x in cast],
        compiler_params=pltpu.CompilerParams(vmem_limit_bytes=12 * MIB),
        cost_estimate=cost(1024, 1024),
    )(keep, *got, *cast, prev)
    return out[0], list(out[1:])


def join_kernel(tokens, pieces, prev_ref, *refs):
    mine_refs, other_refs = refs[:pieces], refs[pieces : 2 * pieces]
    gt_ref, gq_ref = refs[2 * pieces :]
    odd = lax.rem(lax.axis_index("col"), 2)
    for c, (mine_ref, other_ref) in enumerate(zip(mine_refs, other_refs)):
        mine, other = mine_ref[...].astype(F32), other_ref[...].astype(F32)
        low = jnp.where(odd == 1, other, mine)
        high = jnp.where(odd == 1, mine, other)
        rows = jnp.concatenate([low, high], axis=0)
        cols = rows.shape[1]
        gt_ref[:, c * cols : (c + 1) * cols] = rows[:tokens].astype(BF16)
        gq_ref[c * cols : (c + 1) * cols, :] = rows[tokens:].T.astype(BF16)


def join_part(mine, other, prev, tokens):
    half = mine[0].shape[0]
    width = sum(x.shape[1] for x in mine)
    queries = 2 * half - tokens
    return pl.pallas_call(
        functools.partial(join_kernel, tokens, len(mine)),
        in_specs=[ANY_SPEC] + [VMEM_SPEC] * (2 * len(mine)),
        out_specs=[VMEM_SPEC] * 2,
        out_shape=[shape_of(tokens, width, BF16), shape_of(width, queries, BF16)],
        compiler_params=pltpu.CompilerParams(vmem_limit_bytes=12 * MIB),
        cost_estimate=cost(1024, 1024),
    )(prev, *mine, *other)


def inverse_kernel(chunks, corr_ref, prev_ref, *refs):
    *inv_refs, slot_ref, sems = refs
    slots, block = slot_ref.shape[0], slot_ref.shape[1]
    steps = corr_ref.shape[0] // block

    def fetch(step):
        rows = pl.ds(step * block, block)
        return pltpu.make_async_copy(
            corr_ref.at[rows, :], slot_ref.at[step % slots], sems.at[step % slots]
        )

    for step in range(min(slots, steps)):
        fetch(step).start()
    for step in range(steps):
        fetch(step).wait()
        for (first, width), inv_ref in zip(chunks, inv_refs):
            value = slot_ref[step % slots, :, first : first + width]
            inv_ref[step * block : (step + 1) * block, :] = 1.0 / value
        if step + slots < steps:
            fetch(step + slots).start()


def inverse_part(correction, prev, chunks):
    rows, width = correction.shape
    block = largest_divisor(rows, (128, 64, 8))
    out = pl.pallas_call(
        functools.partial(inverse_kernel, chunks),
        in_specs=[ANY_SPEC, ANY_SPEC],
        out_specs=[VMEM_SPEC] * len(chunks),
        out_shape=[shape_of(rows, width, F32) for _, width in chunks],
        scratch_shapes=[pltpu.VMEM((4, block, width), F32), pltpu.SemaphoreType.DMA((4,))],
        compiler_params=pltpu.CompilerParams(vmem_limit_bytes=16 * MIB),
        cost_estimate=cost(1024, 1024),
    )(in_hbm(correction), prev)
    return list(out)


def at_end():
    me = lax.axis_index("row")
    return (me == 0) | (me == lax.axis_size("row") - 1)


def pay_kernel(has_part, acc_ref, got_ref, *refs):
    total = acc_ref[...] + got_ref[...].astype(F32)
    if has_part:
        total = jnp.where(at_end(), refs[0][...], total)
    refs[-1][...] = total.astype(BF16)


def pay_part(hint, acc, got, part, prev):
    has_part = part is not None
    return pl.pallas_call(
        functools.partial(pay_kernel, has_part),
        in_specs=[VMEM_SPEC, VMEM_SPEC] + [VMEM_SPEC] * has_part + [ANY_SPEC],
        out_specs=VMEM_SPEC,
        out_shape=shape_of(*acc.shape, BF16),
        compiler_params=pltpu.CompilerParams(vmem_limit_bytes=12 * MIB),
        cost_estimate=cost(hint, 1024),
    )(acc, got, *([part] if has_part else []), prev)


def after_kernel(first_ref, second_ref, out_ref):
    out_ref[...] = jnp.zeros_like(out_ref)


def after_part(first, second):
    return pl.pallas_call(
        after_kernel,
        in_specs=[ANY_SPEC] * 2,
        out_specs=VMEM_SPEC,
        out_shape=shape_of(8, LANES, F32),
        compiler_params=pltpu.CompilerParams(vmem_limit_bytes=4 * MIB),
        cost_estimate=cost(10**9, 1024),
    )(first, second)


def score_kernel(
    start, scale, outs, gt_ref, gq_ref, inv_ref, sent_ref, got_ref, prev_ref, order_ref, *refs
):
    out_refs = refs[:outs]
    quot_ref, wide_ref, own_ref = refs[outs:]
    tokens = gt_ref.shape[0]
    queries = gq_ref.shape[1]
    width = inv_ref.shape[1]
    total = jnp.where(at_end(), got_ref[...].astype(F32), sent_ref[...].astype(F32))
    wide_ref[...] = total[:tokens]
    own_ref[...] = total[tokens:]
    owner = lax.broadcasted_iota(jnp.int32, (queries, width), 0) // LQ
    lane = lax.broadcasted_iota(jnp.int32, (tokens, LANES), 1)

    def quotient(q):
        own = jnp.where(owner == q, own_ref[...], 0.0).astype(BF16)
        products = jnp.dot(gq_ref[...], own, preferred_element_type=F32)
        quot_ref[q % 2] = (products * inv_ref[...]).astype(BF16)

    quotient(0)
    result = jnp.zeros((tokens, LANES), F32) if start else prev_ref[...]
    for q in range(NQ):
        if q + 1 < NQ:
            quotient(q + 1)
        mapped = jnp.dot(gt_ref[...], quot_ref[q % 2], preferred_element_type=F32)
        scaled = mapped * wide_ref[...]
        folded = scaled[:, :LANES]
        for part in range(1, width // LANES):
            folded = folded + scaled[:, part * LANES : (part + 1) * LANES]
        result = result + jnp.where(lane == q, jnp.sum(folded, axis=1, keepdims=True), 0.0)
    if scale is None:
        out_refs[0][...] = result
        return
    final = (result * scale).T[:NQ]
    if outs == 1:
        out_refs[0][...] = final
        return
    me = lax.axis_index("row")
    cols = final.shape[1] // outs
    for step, out_ref in enumerate(out_refs):
        block = final[:, :cols]
        for other in range(1, outs):
            own = final[:, other * cols : (other + 1) * cols]
            block = jnp.where(jnp.bitwise_xor(me, step) == other, own, block)
        out_ref[...] = block


def score_part(rot_gt, rot_gq_t, inv, sent, got, prev, order, start, scale, halves):
    tokens, outs = rot_gt.shape
    width = inv.shape[1]
    queries = rot_gq_t.shape[1]
    if scale is None:
        out_shape = [shape_of(tokens, LANES, F32)]
    elif halves:
        out_shape = [shape_of(NQ, tokens // halves, F32)] * halves
    else:
        out_shape = [shape_of(NQ, tokens, F32)]
    return pl.pallas_call(
        functools.partial(score_kernel, start, scale, len(out_shape)),
        in_specs=[VMEM_SPEC] * 5 + [ANY_SPEC if start else VMEM_SPEC, ANY_SPEC],
        out_specs=[VMEM_SPEC] * len(out_shape),
        out_shape=out_shape,
        scratch_shapes=[
            pltpu.VMEM((2, outs, width), BF16),
            pltpu.VMEM((tokens, width), F32),
            pltpu.VMEM((queries, width), F32),
        ],
        compiler_params=pltpu.CompilerParams(vmem_limit_bytes=16 * MIB),
        cost_estimate=cost(1024, 1024),
    )(rot_gt, rot_gq_t, inv, sent, got, prev, order)


def gather_kernel(*refs):
    total = refs[0][...]
    for ref in refs[1:-1]:
        total = total + ref[...]
    refs[-1][...] = total


def gather_part(arrays):
    return pl.pallas_call(
        gather_kernel,
        in_specs=[VMEM_SPEC] * len(arrays),
        out_specs=VMEM_SPEC,
        out_shape=shape_of(*arrays[0].shape, F32),
        compiler_params=pltpu.CompilerParams(vmem_limit_bytes=4 * MIB),
        cost_estimate=cost(1024, 1024),
    )(*arrays)


def line_sum(partial, axis):
    n = lax.axis_size(axis)
    half = n // 2
    me = lax.axis_index(axis)
    if n % 2:
        return lax.psum(partial, axis).astype(BF16)
    acc = partial
    for s in range(half - 1):
        pairs = [(s, s + 1), (n - 1 - s, n - 2 - s)]
        acc = acc + lax.ppermute(acc.astype(BF16), axis, pairs).astype(F32)
    got = lax.ppermute(acc.astype(BF16), axis, [(half - 1, half), (half, half - 1)])
    total = (acc + got.astype(F32)).astype(BF16)
    for s in range(half - 2, -1, -1):
        pairs = [(s + 1, s), (n - 2 - s, n - 1 - s)]
        got = lax.ppermute(total, axis, pairs)
        total = jnp.where((me == s) | (me == n - 1 - s), got, total)
    return total


def owned_sum(partial, axis):
    n = lax.axis_size(axis)
    me = lax.axis_index(axis)
    total = lax.dynamic_index_in_dim(partial, me, 0, keepdims=False)
    for step in range(1, n):
        block = lax.dynamic_index_in_dim(partial, (me + step) % n, 0, keepdims=False)
        total = total + lax.ppermute(block, axis, [(d, (d + step) % n) for d in range(n)])
    return total


def shared_sum(partial, axis):
    n = lax.axis_size(axis)
    total = partial
    for step in range(1, n):
        total = total + lax.ppermute(partial, axis, [(d, (d + step) % n) for d in range(n)])
    return total


def on_device(act_train, act_query, grad_train, grad_query, basis_in, basis_out, correction):
    norm_scale = (O * I * LQ) ** (-0.5)
    tokens = act_train.shape[0]
    n_row, n_col = lax.axis_size("row"), lax.axis_size("col")
    chunks = chunk_list(basis_in.shape[1])
    count = len(chunks)
    line = n_row == 4
    flip = [(d, d ^ 1) for d in range(n_col)]
    outer = [(0, 1), (1, 0), (2, 3), (3, 2)]
    inner = []
    for c in range(n_col):
        inner += [(n_col + c, 2 * n_col + c), (2 * n_col + c, n_col + c)]
        inner += [(c, c ^ 1), (3 * n_col + c, 3 * n_col + (c ^ 1))]
    sent, got, acc, got_mid = {}, {}, {}, {}

    def swap(j, payload):
        sent[j] = payload
        got[j] = lax.ppermute(payload, "row", outer)

    def meet(j, prev):
        if not line or j >= count:
            return prev
        cast = [parts[2]] if j == 0 else []
        acc[j], thin = add_part(parts[j], [got[j]], prev, 1, cast)
        got_mid[j] = lax.ppermute(thin[0], ("row", "col"), inner)
        if cast:
            swap(2, thin[1])
        return thin[0]

    def pay(j, prev):
        if not line:
            sent[j + LAG] = got[j + LAG] = line_sum(parts[j], "row")
            return prev
        part = parts[j + LAG] if j + LAG < count else None
        payload = pay_part(4 * 10**9 if j == 0 else 1024, acc[j], got_mid[j], part, prev)
        swap(j + LAG, payload)
        return payload

    def score(k, sums, prev):
        return score_part(
            rot_gt, rot_gq_t, invs[k], sent[k + LAG], got[k + LAG], sums[0], prev,
            k == 0, norm_scale if k == count - 1 else None, halves,
        )

    early = min(LAG + 2, count)
    widths = [width for _, width in chunks]
    parts, narrow = in_part(
        act_train, act_query, basis_in, act_query, chunks[:1], [widths[0]]
    )
    if line:
        swap(0, narrow[0])
    more, narrow = in_part(
        act_train, act_query, basis_in, parts[0], chunks[1:early], [widths[1]]
    )
    parts += more
    if line:
        swap(1, narrow[0])
    (half_sum,) = out_part(grad_train, grad_query, basis_out, parts[-1], None)
    prev = meet(0, half_sum)
    keep, *give = out_part(grad_train, grad_query, basis_out, prev, half_sum)
    given = [lax.ppermute(piece, "col", flip) for piece in give]
    prev = meet(1, keep)
    if line:
        prev = after_part(prev, got[2])
    prev = meet(2, pay(0, prev))
    outs = pieces_of(keep.shape[1], 2)
    wide, thin = add_part(keep, given, prev, outs)
    prev, bit = wide, 2
    while bit < n_col:
        other = [lax.ppermute(x, "col", [(d, d ^ bit) for d in range(n_col)]) for x in thin]
        if bit == 2:
            more, _ = in_part(act_train, act_query, basis_in, prev, chunks[early:], [])
            parts += more
            prev = meet(3, pay(1, more[-1]))
            invs = inverse_part(correction, prev, chunks)
            prev = pay(2, invs[0])
        wide, thin = add_part(wide, other, prev, outs)
        prev = wide
        bit *= 2
    other = [lax.ppermute(x, "col", flip) for x in thin]
    prev = meet(5, pay(3, meet(4, prev)))
    rot_gt, rot_gq_t = join_part(thin, other, prev, tokens)
    prev = rot_gt
    halves = n_row if n_row == 4 and n_col == 4 and tokens % (n_row * LANES) == 0 else 0
    sums = score(0, [rot_gt], prev)
    done = 1
    for j in range(6, count + 1):
        prev = meet(j, pay(j - 2, sums[0]))
        sums = score(done, sums, prev)
        done += 1
    if line:
        prev = after_part(sums[0], got[count])
    prev = pay(count - 1, prev)
    for k in range(done, count):
        sums = score(k, sums, prev)
    if not halves:
        blocks = sums[0].reshape(NQ, n_row, tokens // n_row).transpose(1, 0, 2)
        return shared_sum(owned_sum(blocks, "row"), "col")
    moved = [
        lax.ppermute(sums[step], "row", [(d, d ^ step) for d in range(n_row)])
        for step in range(1, n_row)
    ]
    owned = gather_part([sums[0]] + moved)
    moved = [
        lax.ppermute(owned, "col", [(d, d ^ step) for d in range(n_col)]) for step in range(1, n_col)
    ]
    return gather_part([owned] + moved)


def solution(mesh):
    in_specs = (
        P("groups", "row"),
        P("groups", "row"),
        P("groups", "col"),
        P("groups", "col"),
        P(("groups", "row"), "col"),
        P(("groups", "col"), "row"),
        P(("groups", "row"), "col"),
    )
    out_specs = P("groups", "row")
    return jax.shard_map(
        on_device, mesh=mesh, in_specs=in_specs, out_specs=out_specs, check_vma=False
    )
```

```python
import functools

import jax
import jax.numpy as jnp
from jax import lax
from jax.experimental import pallas as pl
from jax.experimental.pallas import tpu as pltpu
from jax.sharding import PartitionSpec as P

I = 8192
O = 4096
NQ = 8
LQ = 16
LANES = 128
CHUNKS = 8
LAG = 3
F32 = jnp.float32
BF16 = jnp.bfloat16
MIB = 1 << 20

VMEM_SPEC = pl.BlockSpec(memory_space=pltpu.VMEM)
SMEM_SPEC = pl.BlockSpec(memory_space=pltpu.SMEM)
ANY_SPEC = pl.BlockSpec(memory_space=pl.ANY)


def shape_of(rows, width, dtype):
    return jax.ShapeDtypeStruct((rows, width), dtype)


def chunk_list(size):
    tiles = size // LANES
    count = min(CHUNKS, tiles)
    chunks, first = [], 0
    for k in range(count):
        width = LANES * (tiles // count + (1 if k < tiles % count else 0))
        chunks.append((first, width))
        first += width
    return chunks


def largest_divisor(size, choices):
    for choice in choices:
        if size % choice == 0:
            return choice
    return size


def pieces_of(width, most):
    return max(p for p in range(1, most + 1) if width % (p * LANES) == 0)


def cost(flops, bytes_accessed):
    return pl.CostEstimate(flops=flops, bytes_accessed=bytes_accessed, transcendentals=0)


def in_hbm(x):
    return pltpu.with_memory_space_constraint(x, pltpu.HBM)


def halves_dot(rows, basis):
    half = rows.shape[0] // 2
    return [jnp.dot(part, basis, preferred_element_type=F32) for part in (rows[:half], rows[half:])]


def in_kernel(chunks, narrow, groups, train_ref, query_ref, basis_ref, prev_ref, *refs):
    count = len(chunks)
    rows_ref, slot_ref, sum_ref, sems = refs[count + narrow :]
    tokens, queries = train_ref.shape[0], query_ref.shape[0]
    start, total = chunks[0][0], slot_ref.shape[1]
    depth = basis_ref.shape[0] // groups
    copies = []
    for g in range(groups):
        part = pl.ds(g * depth, depth)
        copies.append([
            pltpu.make_async_copy(
                basis_ref.at[part, pl.ds(start, total)], slot_ref.at[part, :], sems.at[g, 0]
            ),
            pltpu.make_async_copy(
                train_ref.at[:, part], rows_ref.at[pl.ds(0, tokens), part], sems.at[g, 1]
            ),
            pltpu.make_async_copy(
                query_ref.at[:, part], rows_ref.at[pl.ds(tokens, queries), part], sems.at[g, 2]
            ),
        ])
    for group in copies:
        for copy in group:
            copy.start()
    for g, group in enumerate(copies):
        for copy in group:
            copy.wait()
        part = slice(g * depth, (g + 1) * depth)
        half = rows_ref.shape[0] // 2
        for h, value in enumerate(halves_dot(rows_ref[:, part], slot_ref[part, :])):
            span = slice(h * half, (h + 1) * half)
            if g == 0:
                sum_ref[span, :] = value
            else:
                sum_ref[span, :] += value
    for j, (first, width) in enumerate(chunks):
        refs[j][...] = sum_ref[:, first - start : first - start + width]
    column = 0
    for narrow_ref in refs[count : count + narrow]:
        width = narrow_ref.shape[1]
        narrow_ref[...] = sum_ref[:, column : column + width].astype(BF16)
        column += width


def in_part(act_train, act_query, basis_in, prev, chunks, narrow):
    tokens, depth = act_train.shape
    rows = tokens + act_query.shape[0]
    total = sum(width for _, width in chunks)
    groups = next(g for g in (4, 2, 1) if depth % (g * LANES) == 0)
    shapes = [shape_of(rows, width, F32) for _, width in chunks]
    shapes += [shape_of(rows, width, BF16) for width in narrow]
    out = pl.pallas_call(
        functools.partial(in_kernel, chunks, len(narrow), groups),
        in_specs=[ANY_SPEC] * 4,
        out_specs=[VMEM_SPEC] * len(shapes),
        out_shape=shapes,
        scratch_shapes=[
            pltpu.VMEM((rows, depth), BF16),
            pltpu.VMEM((depth, total), BF16),
            pltpu.VMEM((rows, total), F32),
            pltpu.SemaphoreType.DMA((groups, 3)),
        ],
        compiler_params=pltpu.CompilerParams(vmem_limit_bytes=24 * MIB),
        cost_estimate=cost(1024, 1024),
    )(in_hbm(act_train), in_hbm(act_query), in_hbm(basis_in), prev)
    return list(out[: len(chunks)]), list(out[len(chunks) :])


def out_kernel(begin, steps, last, train_ref, query_ref, basis_ref, prev_ref, *refs):
    if last:
        start_ref, keep_ref, *give_refs, rows_ref, slot_ref, acc_ref, sems = refs
    else:
        acc_ref, rows_ref, slot_ref, sems = refs
    tokens, queries = train_ref.shape[0], query_ref.shape[0]
    slots, block = slot_ref.shape[0], slot_ref.shape[1]
    half, width = acc_ref.shape[0] // 2, acc_ref.shape[1]
    tile = largest_divisor(width, (256, 128))

    def copies(step):
        slot = lax.rem(step, slots)
        part = pl.ds(pl.multiple_of((begin + step) * block, block), block)
        return [
            pltpu.make_async_copy(basis_ref.at[part, :], slot_ref.at[slot], sems.at[slot, 0]),
            pltpu.make_async_copy(
                train_ref.at[:, part], rows_ref.at[slot, pl.ds(0, tokens), :], sems.at[slot, 1]
            ),
            pltpu.make_async_copy(
                query_ref.at[:, part], rows_ref.at[slot, pl.ds(tokens, queries), :], sems.at[slot, 2]
            ),
        ]

    for step in range(min(slots - 1, steps)):
        for copy in copies(step):
            copy.start()
    acc_ref[...] = start_ref[...] if last else jnp.zeros_like(acc_ref)

    def body(step, carry):
        for copy in copies(step):
            copy.wait()

        @pl.when(step + slots - 1 < steps)
        def _():
            for copy in copies(step + slots - 1):
                copy.start()

        slot = lax.rem(step, slots)
        rows = rows_ref[slot]
        for first in range(0, width, tile):
            span = slice(first, first + tile)
            acc_ref[:, span] += jnp.dot(rows, slot_ref[slot, :, span], preferred_element_type=F32)
        return carry

    lax.fori_loop(0, steps, body, 0)
    if not last:
        return
    odd = lax.rem(lax.axis_index("col"), 2)
    keep_ref[...] = acc_ref[pl.ds(pl.multiple_of(odd * half, 16), half), :]
    cols = give_refs[0].shape[1]
    for c, give_ref in enumerate(give_refs):
        span = slice(c * cols, (c + 1) * cols)
        give_ref[...] = acc_ref[pl.ds(pl.multiple_of((1 - odd) * half, 16), half), span]


def out_part(grad_train, grad_query, basis_out, prev, acc):
    tokens, depth = grad_train.shape
    width = basis_out.shape[1]
    rows = tokens + grad_query.shape[0]
    block = largest_divisor(depth, (512, 256, 128))
    steps = depth // block
    slots = min(6, steps)
    last = acc is not None
    first = steps * 2 // 7
    begin, count = (first, steps - first) if last else (0, first)
    pieces = pieces_of(width, 2)
    if last:
        out_shape = [shape_of(rows // 2, width, F32)]
        out_shape += [shape_of(rows // 2, width // pieces, F32)] * pieces
    else:
        out_shape = [shape_of(rows, width, F32)]
    return pl.pallas_call(
        functools.partial(out_kernel, begin, count, last),
        in_specs=[ANY_SPEC] * 4 + [VMEM_SPEC] * last,
        out_specs=[VMEM_SPEC] * len(out_shape),
        out_shape=out_shape,
        scratch_shapes=[
            pltpu.VMEM((slots, rows, block), BF16),
            pltpu.VMEM((slots, block, width), BF16),
        ]
        + [pltpu.VMEM((rows, width), F32)] * last
        + [pltpu.SemaphoreType.DMA((slots, 3))],
        compiler_params=pltpu.CompilerParams(vmem_limit_bytes=22 * MIB),
        cost_estimate=cost(2 * rows * block * count * width if last else 1024, 1024),
    )(
        in_hbm(grad_train), in_hbm(grad_query), in_hbm(basis_out), prev, *([acc] if last else [])
    )


def add_kernel(pieces, outs, cast, keep_ref, *refs):
    wide_ref, narrow_refs = refs[pieces + cast + 1], refs[pieces + cast + 2 :]
    width = keep_ref.shape[1]
    cols = width // pieces
    for c in range(pieces):
        span = slice(c * cols, (c + 1) * cols)
        wide_ref[:, span] = keep_ref[:, span] + refs[c][...].astype(F32)
    cols = width // outs
    for c in range(outs):
        narrow_refs[c][...] = wide_ref[:, c * cols : (c + 1) * cols].astype(BF16)
    if cast:
        narrow_refs[outs][...] = refs[pieces][...].astype(BF16)


def add_part(keep, got, prev, outs=1, cast=()):
    rows, width = keep.shape
    out = pl.pallas_call(
        functools.partial(add_kernel, len(got), outs, len(cast)),
        in_specs=[VMEM_SPEC] * (1 + len(got) + len(cast)) + [ANY_SPEC],
        out_specs=[VMEM_SPEC] * (1 + outs + len(cast)),
        out_shape=[shape_of(rows, width, F32)]
        + [shape_of(rows, width // outs, BF16)] * outs
        + [shape_of(*x.shape, BF16) for x in cast],
        compiler_params=pltpu.CompilerParams(vmem_limit_bytes=12 * MIB),
        cost_estimate=cost(1024, 1024),
    )(keep, *got, *cast, prev)
    return out[0], list(out[1:])


def join_kernel(tokens, pieces, prev_ref, *refs):
    mine_refs, other_refs = refs[:pieces], refs[pieces : 2 * pieces]
    gt_ref, gq_ref = refs[2 * pieces :]
    odd = lax.rem(lax.axis_index("col"), 2)
    for c, (mine_ref, other_ref) in enumerate(zip(mine_refs, other_refs)):
        mine, other = mine_ref[...].astype(F32), other_ref[...].astype(F32)
        low = jnp.where(odd == 1, other, mine)
        high = jnp.where(odd == 1, mine, other)
        rows = jnp.concatenate([low, high], axis=0)
        cols = rows.shape[1]
        gt_ref[:, c * cols : (c + 1) * cols] = rows[:tokens].astype(BF16)
        gq_ref[c * cols : (c + 1) * cols, :] = rows[tokens:].T.astype(BF16)


def join_part(mine, other, prev, tokens):
    half = mine[0].shape[0]
    width = sum(x.shape[1] for x in mine)
    queries = 2 * half - tokens
    return pl.pallas_call(
        functools.partial(join_kernel, tokens, len(mine)),
        in_specs=[ANY_SPEC] + [VMEM_SPEC] * (2 * len(mine)),
        out_specs=[VMEM_SPEC] * 2,
        out_shape=[shape_of(tokens, width, BF16), shape_of(width, queries, BF16)],
        compiler_params=pltpu.CompilerParams(vmem_limit_bytes=12 * MIB),
        cost_estimate=cost(1024, 1024),
    )(prev, *mine, *other)


def inverse_kernel(chunks, corr_ref, prev_ref, *refs):
    *inv_refs, slot_ref, sems = refs
    slots, block = slot_ref.shape[0], slot_ref.shape[1]
    steps = corr_ref.shape[0] // block

    def fetch(step):
        rows = pl.ds(step * block, block)
        return pltpu.make_async_copy(
            corr_ref.at[rows, :], slot_ref.at[step % slots], sems.at[step % slots]
        )

    for step in range(min(slots, steps)):
        fetch(step).start()
    for step in range(steps):
        fetch(step).wait()
        for (first, width), inv_ref in zip(chunks, inv_refs):
            value = slot_ref[step % slots, :, first : first + width]
            inv_ref[step * block : (step + 1) * block, :] = 1.0 / value
        if step + slots < steps:
            fetch(step + slots).start()


def inverse_part(correction, prev, chunks):
    rows, width = correction.shape
    block = largest_divisor(rows, (128, 64, 8))
    out = pl.pallas_call(
        functools.partial(inverse_kernel, chunks),
        in_specs=[ANY_SPEC, ANY_SPEC],
        out_specs=[VMEM_SPEC] * len(chunks),
        out_shape=[shape_of(rows, width, F32) for _, width in chunks],
        scratch_shapes=[pltpu.VMEM((4, block, width), F32), pltpu.SemaphoreType.DMA((4,))],
        compiler_params=pltpu.CompilerParams(vmem_limit_bytes=16 * MIB),
        cost_estimate=cost(1024, 1024),
    )(in_hbm(correction), prev)
    return list(out)


def at_end():
    me = lax.axis_index("row")
    return (me == 0) | (me == lax.axis_size("row") - 1)


def pay_kernel(has_part, acc_ref, got_ref, *refs):
    total = acc_ref[...] + got_ref[...].astype(F32)
    if has_part:
        total = jnp.where(at_end(), refs[0][...], total)
    refs[-1][...] = total.astype(BF16)


def pay_part(hint, acc, got, part, prev):
    has_part = part is not None
    return pl.pallas_call(
        functools.partial(pay_kernel, has_part),
        in_specs=[VMEM_SPEC, VMEM_SPEC] + [VMEM_SPEC] * has_part + [ANY_SPEC],
        out_specs=VMEM_SPEC,
        out_shape=shape_of(*acc.shape, BF16),
        compiler_params=pltpu.CompilerParams(vmem_limit_bytes=12 * MIB),
        cost_estimate=cost(hint, 1024),
    )(acc, got, *([part] if has_part else []), prev)


def after_kernel(first_ref, second_ref, out_ref):
    out_ref[...] = jnp.zeros_like(out_ref)


def after_part(first, second):
    return pl.pallas_call(
        after_kernel,
        in_specs=[ANY_SPEC] * 2,
        out_specs=VMEM_SPEC,
        out_shape=shape_of(8, LANES, F32),
        compiler_params=pltpu.CompilerParams(vmem_limit_bytes=4 * MIB),
        cost_estimate=cost(10**9, 1024),
    )(first, second)


def score_kernel(
    start, scale, outs, gt_ref, gq_ref, inv_ref, sent_ref, got_ref, prev_ref, order_ref, *refs
):
    out_refs = refs[:outs]
    quot_ref, wide_ref, own_ref, sums_ref = refs[outs:]
    tokens = gt_ref.shape[0]
    queries = gq_ref.shape[1]
    width = inv_ref.shape[1]
    total = jnp.where(at_end(), got_ref[...].astype(F32), sent_ref[...].astype(F32))
    wide_ref[...] = total[:tokens]
    own_ref[...] = total[tokens:]
    owner = lax.broadcasted_iota(jnp.int32, (queries, width), 0) // LQ
    lane = lax.broadcasted_iota(jnp.int32, (tokens, LANES), 1)

    def quotient(q, slot):
        own = jnp.where(owner == q, own_ref[...], 0.0).astype(BF16)
        products = jnp.dot(gq_ref[...], own, preferred_element_type=F32)
        quot_ref[slot] = (products * inv_ref[...]).astype(BF16)

    def add_scores(q, slot):
        mapped = jnp.dot(gt_ref[...], quot_ref[slot], preferred_element_type=F32)
        scaled = mapped * wide_ref[...]
        folded = scaled[:, :LANES]
        for part in range(1, width // LANES):
            folded = folded + scaled[:, part * LANES : (part + 1) * LANES]
        sums_ref[...] += jnp.where(lane == q, jnp.sum(folded, axis=1, keepdims=True), 0.0)

    def pair(i, carry):
        quotient(2 * i + 1, 1)
        add_scores(2 * i, 0)
        quotient(2 * i + 2, 0)
        add_scores(2 * i + 1, 1)
        return carry

    sums_ref[...] = jnp.zeros_like(sums_ref) if start else prev_ref[...]
    quotient(0, 0)
    lax.fori_loop(0, NQ // 2, pair, 0)
    result = sums_ref[...]
    if scale is None:
        out_refs[0][...] = result
        return
    final = (result * scale).T[:NQ]
    if outs == 1:
        out_refs[0][...] = final
        return
    me = lax.axis_index("row")
    cols = final.shape[1] // outs
    for step, out_ref in enumerate(out_refs):
        block = final[:, :cols]
        for other in range(1, outs):
            own = final[:, other * cols : (other + 1) * cols]
            block = jnp.where(jnp.bitwise_xor(me, step) == other, own, block)
        out_ref[...] = block


def score_part(rot_gt, rot_gq_t, inv, sent, got, prev, order, start, scale, halves):
    tokens, outs = rot_gt.shape
    width = inv.shape[1]
    queries = rot_gq_t.shape[1]
    if scale is None:
        out_shape = [shape_of(tokens, LANES, F32)]
    elif halves:
        out_shape = [shape_of(NQ, tokens // halves, F32)] * halves
    else:
        out_shape = [shape_of(NQ, tokens, F32)]
    return pl.pallas_call(
        functools.partial(score_kernel, start, scale, len(out_shape)),
        in_specs=[VMEM_SPEC] * 5 + [ANY_SPEC if start else VMEM_SPEC, ANY_SPEC],
        out_specs=[VMEM_SPEC] * len(out_shape),
        out_shape=out_shape,
        scratch_shapes=[
            pltpu.VMEM((2, outs, width), BF16),
            pltpu.VMEM((tokens, width), F32),
            pltpu.VMEM((queries, width), F32),
            pltpu.VMEM((tokens, LANES), F32),
        ],
        compiler_params=pltpu.CompilerParams(vmem_limit_bytes=16 * MIB),
        cost_estimate=cost(1024, 1024),
    )(rot_gt, rot_gq_t, inv, sent, got, prev, order)


def gather_kernel(*refs):
    total = refs[0][...]
    for ref in refs[1:-1]:
        total = total + ref[...]
    refs[-1][...] = total


def gather_part(arrays):
    return pl.pallas_call(
        gather_kernel,
        in_specs=[VMEM_SPEC] * len(arrays),
        out_specs=VMEM_SPEC,
        out_shape=shape_of(*arrays[0].shape, F32),
        compiler_params=pltpu.CompilerParams(vmem_limit_bytes=4 * MIB),
        cost_estimate=cost(1024, 1024),
    )(*arrays)


def line_sum(partial, axis):
    n = lax.axis_size(axis)
    half = n // 2
    me = lax.axis_index(axis)
    if n % 2:
        return lax.psum(partial, axis).astype(BF16)
    acc = partial
    for s in range(half - 1):
        pairs = [(s, s + 1), (n - 1 - s, n - 2 - s)]
        acc = acc + lax.ppermute(acc.astype(BF16), axis, pairs).astype(F32)
    got = lax.ppermute(acc.astype(BF16), axis, [(half - 1, half), (half, half - 1)])
    total = (acc + got.astype(F32)).astype(BF16)
    for s in range(half - 2, -1, -1):
        pairs = [(s + 1, s), (n - 2 - s, n - 1 - s)]
        got = lax.ppermute(total, axis, pairs)
        total = jnp.where((me == s) | (me == n - 1 - s), got, total)
    return total


def owned_sum(partial, axis):
    n = lax.axis_size(axis)
    me = lax.axis_index(axis)
    total = lax.dynamic_index_in_dim(partial, me, 0, keepdims=False)
    for step in range(1, n):
        block = lax.dynamic_index_in_dim(partial, (me + step) % n, 0, keepdims=False)
        total = total + lax.ppermute(block, axis, [(d, (d + step) % n) for d in range(n)])
    return total


def shared_sum(partial, axis):
    n = lax.axis_size(axis)
    total = partial
    for step in range(1, n):
        total = total + lax.ppermute(partial, axis, [(d, (d + step) % n) for d in range(n)])
    return total


def on_device(act_train, act_query, grad_train, grad_query, basis_in, basis_out, correction):
    norm_scale = (O * I * LQ) ** (-0.5)
    tokens = act_train.shape[0]
    n_row, n_col = lax.axis_size("row"), lax.axis_size("col")
    chunks = chunk_list(basis_in.shape[1])
    count = len(chunks)
    line = n_row == 4
    flip = [(d, d ^ 1) for d in range(n_col)]
    outer = [(0, 1), (1, 0), (2, 3), (3, 2)]
    inner = []
    for c in range(n_col):
        inner += [(n_col + c, 2 * n_col + c), (2 * n_col + c, n_col + c)]
        inner += [(c, c ^ 1), (3 * n_col + c, 3 * n_col + (c ^ 1))]
    sent, got, acc, got_mid = {}, {}, {}, {}

    def swap(j, payload):
        sent[j] = payload
        got[j] = lax.ppermute(payload, "row", outer)

    def meet(j, prev):
        if not line or j >= count:
            return prev
        cast = [parts[2]] if j == 0 else []
        acc[j], thin = add_part(parts[j], [got[j]], prev, 1, cast)
        got_mid[j] = lax.ppermute(thin[0], ("row", "col"), inner)
        if cast:
            swap(2, thin[1])
        return thin[0]

    def pay(j, prev):
        if not line:
            sent[j + LAG] = got[j + LAG] = line_sum(parts[j], "row")
            return prev
        part = parts[j + LAG] if j + LAG < count else None
        payload = pay_part(4 * 10**9 if j == 0 else 1024, acc[j], got_mid[j], part, prev)
        swap(j + LAG, payload)
        return payload

    def score(k, sums, prev):
        return score_part(
            rot_gt, rot_gq_t, invs[k], sent[k + LAG], got[k + LAG], sums[0], prev,
            k == 0, norm_scale if k == count - 1 else None, halves,
        )

    early = min(LAG + 2, count)
    widths = [width for _, width in chunks]
    parts, narrow = in_part(
        act_train, act_query, basis_in, act_query, chunks[:1], [widths[0]]
    )
    if line:
        swap(0, narrow[0])
    more, narrow = in_part(
        act_train, act_query, basis_in, parts[0], chunks[1:early], [widths[1]]
    )
    parts += more
    if line:
        swap(1, narrow[0])
    (half_sum,) = out_part(grad_train, grad_query, basis_out, parts[-1], None)
    prev = meet(0, half_sum)
    keep, *give = out_part(grad_train, grad_query, basis_out, prev, half_sum)
    given = [lax.ppermute(piece, "col", flip) for piece in give]
    prev = meet(1, keep)
    if line:
        prev = after_part(prev, got[2])
    prev = meet(2, pay(0, prev))
    outs = pieces_of(keep.shape[1], 2)
    wide, thin = add_part(keep, given, prev, outs)
    prev, bit = wide, 2
    while bit < n_col:
        other = [lax.ppermute(x, "col", [(d, d ^ bit) for d in range(n_col)]) for x in thin]
        if bit == 2:
            more, _ = in_part(act_train, act_query, basis_in, prev, chunks[early:], [])
            parts += more
            prev = meet(3, pay(1, more[-1]))
            invs = inverse_part(correction, prev, chunks)
            prev = pay(2, invs[0])
        wide, thin = add_part(wide, other, prev, outs)
        prev = wide
        bit *= 2
    other = [lax.ppermute(x, "col", flip) for x in thin]
    prev = meet(5, pay(3, meet(4, prev)))
    rot_gt, rot_gq_t = join_part(thin, other, prev, tokens)
    prev = rot_gt
    halves = n_row if n_row == 4 and n_col == 4 and tokens % (n_row * LANES) == 0 else 0
    sums = score(0, [rot_gt], prev)
    done = 1
    for j in range(6, count + 1):
        prev = meet(j, pay(j - 2, sums[0]))
        sums = score(done, sums, prev)
        done += 1
    if line:
        prev = after_part(sums[0], got[count])
    prev = pay(count - 1, prev)
    for k in range(done, count):
        sums = score(k, sums, prev)
    if not halves:
        blocks = sums[0].reshape(NQ, n_row, tokens // n_row).transpose(1, 0, 2)
        return shared_sum(owned_sum(blocks, "row"), "col")
    moved = [
        lax.ppermute(sums[step], "row", [(d, d ^ step) for d in range(n_row)])
        for step in range(1, n_row)
    ]
    owned = gather_part([sums[0]] + moved)
    moved = [
        lax.ppermute(owned, "col", [(d, d ^ step) for d in range(n_col)]) for step in range(1, n_col)
    ]
    return gather_part([owned] + moved)


def solution(mesh):
    in_specs = (
        P("groups", "row"),
        P("groups", "row"),
        P("groups", "col"),
        P("groups", "col"),
        P(("groups", "row"), "col"),
        P(("groups", "col"), "row"),
        P(("groups", "row"), "col"),
    )
    out_specs = P("groups", "row")
    return jax.shard_map(
        on_device, mesh=mesh, in_specs=in_specs, out_specs=out_specs, check_vma=False
    )
```

```python
import functools

import jax
import jax.numpy as jnp
from jax import lax
from jax.experimental import pallas as pl
from jax.experimental.pallas import tpu as pltpu
from jax.sharding import PartitionSpec as P

I = 8192
O = 4096
NQ = 8
LQ = 16
LANES = 128
CHUNKS = 8
LAG = 3
F32 = jnp.float32
BF16 = jnp.bfloat16
MIB = 1 << 20

VMEM_SPEC = pl.BlockSpec(memory_space=pltpu.VMEM)
SMEM_SPEC = pl.BlockSpec(memory_space=pltpu.SMEM)
ANY_SPEC = pl.BlockSpec(memory_space=pl.ANY)


def shape_of(rows, width, dtype):
    return jax.ShapeDtypeStruct((rows, width), dtype)


def chunk_list(size):
    tiles = size // LANES
    count = min(CHUNKS, tiles)
    chunks, first = [], 0
    for k in range(count):
        width = LANES * (tiles // count + (1 if k < tiles % count else 0))
        chunks.append((first, width))
        first += width
    return chunks


def largest_divisor(size, choices):
    for choice in choices:
        if size % choice == 0:
            return choice
    return size


def pieces_of(width, most):
    return max(p for p in range(1, most + 1) if width % (p * LANES) == 0)


def cost(flops, bytes_accessed):
    return pl.CostEstimate(flops=flops, bytes_accessed=bytes_accessed, transcendentals=0)


def in_hbm(x):
    return pltpu.with_memory_space_constraint(x, pltpu.HBM)


def halves_dot(rows, basis):
    half = rows.shape[0] // 2
    return [jnp.dot(part, basis, preferred_element_type=F32) for part in (rows[:half], rows[half:])]


def in_kernel(chunks, narrow, groups, train_ref, query_ref, basis_ref, prev_ref, *refs):
    count = len(chunks)
    rows_ref, slot_ref, sum_ref, sems = refs[count + narrow :]
    tokens, queries = train_ref.shape[0], query_ref.shape[0]
    start, total = chunks[0][0], slot_ref.shape[2]
    depth = slot_ref.shape[1]
    half = rows_ref.shape[1] // 2

    def copies(g):
        part = pl.ds(pl.multiple_of(g * depth, depth), depth)
        return [
            pltpu.make_async_copy(
                basis_ref.at[part, pl.ds(start, total)], slot_ref.at[g], sems.at[g, 0]
            ),
            pltpu.make_async_copy(
                train_ref.at[:, part], rows_ref.at[g, pl.ds(0, tokens), :], sems.at[g, 1]
            ),
            pltpu.make_async_copy(
                query_ref.at[:, part], rows_ref.at[g, pl.ds(tokens, queries), :], sems.at[g, 2]
            ),
        ]

    for g in range(groups):
        for copy in copies(g):
            copy.start()
    sum_ref[...] = jnp.zeros_like(sum_ref)

    def body(g, carry):
        for copy in copies(g):
            copy.wait()
        for h, value in enumerate(halves_dot(rows_ref[g], slot_ref[g])):
            sum_ref[h * half : (h + 1) * half, :] += value
        return carry

    lax.fori_loop(0, groups, body, 0)
    for j, (first, width) in enumerate(chunks):
        refs[j][...] = sum_ref[:, first - start : first - start + width]
    column = 0
    for narrow_ref in refs[count : count + narrow]:
        width = narrow_ref.shape[1]
        narrow_ref[...] = sum_ref[:, column : column + width].astype(BF16)
        column += width


def in_part(act_train, act_query, basis_in, prev, chunks, narrow):
    tokens, depth = act_train.shape
    rows = tokens + act_query.shape[0]
    total = sum(width for _, width in chunks)
    groups = next(g for g in (4, 2, 1) if depth % (g * LANES) == 0)
    shapes = [shape_of(rows, width, F32) for _, width in chunks]
    shapes += [shape_of(rows, width, BF16) for width in narrow]
    out = pl.pallas_call(
        functools.partial(in_kernel, chunks, len(narrow), groups),
        in_specs=[ANY_SPEC] * 4,
        out_specs=[VMEM_SPEC] * len(shapes),
        out_shape=shapes,
        scratch_shapes=[
            pltpu.VMEM((groups, rows, depth // groups), BF16),
            pltpu.VMEM((groups, depth // groups, total), BF16),
            pltpu.VMEM((rows, total), F32),
            pltpu.SemaphoreType.DMA((groups, 3)),
        ],
        compiler_params=pltpu.CompilerParams(vmem_limit_bytes=24 * MIB),
        cost_estimate=cost(1024, 1024),
    )(in_hbm(act_train), in_hbm(act_query), in_hbm(basis_in), prev)
    return list(out[: len(chunks)]), list(out[len(chunks) :])


def out_kernel(begin, steps, last, train_ref, query_ref, basis_ref, prev_ref, *refs):
    if last:
        start_ref, keep_ref, *give_refs, rows_ref, slot_ref, acc_ref, sems = refs
    else:
        acc_ref, rows_ref, slot_ref, sems = refs
    tokens, queries = train_ref.shape[0], query_ref.shape[0]
    slots, block = slot_ref.shape[0], slot_ref.shape[1]
    half, width = acc_ref.shape[0] // 2, acc_ref.shape[1]
    tile = largest_divisor(width, (256, 128))

    def copies(step):
        slot = lax.rem(step, slots)
        part = pl.ds(pl.multiple_of((begin + step) * block, block), block)
        return [
            pltpu.make_async_copy(basis_ref.at[part, :], slot_ref.at[slot], sems.at[slot, 0]),
            pltpu.make_async_copy(
                train_ref.at[:, part], rows_ref.at[slot, pl.ds(0, tokens), :], sems.at[slot, 1]
            ),
            pltpu.make_async_copy(
                query_ref.at[:, part], rows_ref.at[slot, pl.ds(tokens, queries), :], sems.at[slot, 2]
            ),
        ]

    for step in range(min(slots - 1, steps)):
        for copy in copies(step):
            copy.start()
    acc_ref[...] = start_ref[...] if last else jnp.zeros_like(acc_ref)

    def body(step, carry):
        for copy in copies(step):
            copy.wait()

        @pl.when(step + slots - 1 < steps)
        def _():
            for copy in copies(step + slots - 1):
                copy.start()

        slot = lax.rem(step, slots)
        rows = rows_ref[slot]
        for first in range(0, width, tile):
            span = slice(first, first + tile)
            acc_ref[:, span] += jnp.dot(rows, slot_ref[slot, :, span], preferred_element_type=F32)
        return carry

    lax.fori_loop(0, steps, body, 0)
    if not last:
        return
    odd = lax.rem(lax.axis_index("col"), 2)
    keep_ref[...] = acc_ref[pl.ds(pl.multiple_of(odd * half, 16), half), :]
    cols = give_refs[0].shape[1]
    for c, give_ref in enumerate(give_refs):
        span = slice(c * cols, (c + 1) * cols)
        give_ref[...] = acc_ref[pl.ds(pl.multiple_of((1 - odd) * half, 16), half), span]


def out_part(grad_train, grad_query, basis_out, prev, acc):
    tokens, depth = grad_train.shape
    width = basis_out.shape[1]
    rows = tokens + grad_query.shape[0]
    block = largest_divisor(depth, (512, 256, 128))
    steps = depth // block
    slots = min(6, steps)
    last = acc is not None
    first = steps * 2 // 7
    begin, count = (first, steps - first) if last else (0, first)
    pieces = pieces_of(width, 2)
    if last:
        out_shape = [shape_of(rows // 2, width, F32)]
        out_shape += [shape_of(rows // 2, width // pieces, F32)] * pieces
    else:
        out_shape = [shape_of(rows, width, F32)]
    return pl.pallas_call(
        functools.partial(out_kernel, begin, count, last),
        in_specs=[ANY_SPEC] * 4 + [VMEM_SPEC] * last,
        out_specs=[VMEM_SPEC] * len(out_shape),
        out_shape=out_shape,
        scratch_shapes=[
            pltpu.VMEM((slots, rows, block), BF16),
            pltpu.VMEM((slots, block, width), BF16),
        ]
        + [pltpu.VMEM((rows, width), F32)] * last
        + [pltpu.SemaphoreType.DMA((slots, 3))],
        compiler_params=pltpu.CompilerParams(vmem_limit_bytes=22 * MIB),
        cost_estimate=cost(2 * rows * block * count * width if last else 1024, 1024),
    )(
        in_hbm(grad_train), in_hbm(grad_query), in_hbm(basis_out), prev, *([acc] if last else [])
    )


def by_rows(rows, step):
    block = rows // 5 if rows % 80 == 0 else rows

    def body(i, carry):
        step(pl.ds(pl.multiple_of(i * block, block), block))
        return carry

    lax.fori_loop(0, rows // block, body, 0)


def add_kernel(pieces, outs, cast, keep_ref, *refs):
    wide_ref, narrow_refs = refs[pieces + cast + 1], refs[pieces + cast + 2 :]
    width = keep_ref.shape[1]

    def step(rows):
        total = keep_ref[rows, :]
        got = [refs[c][rows, :].astype(F32) for c in range(pieces)]
        total = total + (jnp.concatenate(got, axis=1) if pieces > 1 else got[0])
        wide_ref[rows, :] = total
        cols = width // outs
        for c in range(outs):
            narrow_refs[c][rows, :] = total[:, c * cols : (c + 1) * cols].astype(BF16)
        if cast:
            narrow_refs[outs][rows, :] = refs[pieces][rows, :].astype(BF16)

    by_rows(keep_ref.shape[0], step)


def add_part(keep, got, prev, outs=1, cast=()):
    rows, width = keep.shape
    out = pl.pallas_call(
        functools.partial(add_kernel, len(got), outs, len(cast)),
        in_specs=[VMEM_SPEC] * (1 + len(got) + len(cast)) + [ANY_SPEC],
        out_specs=[VMEM_SPEC] * (1 + outs + len(cast)),
        out_shape=[shape_of(rows, width, F32)]
        + [shape_of(rows, width // outs, BF16)] * outs
        + [shape_of(*x.shape, BF16) for x in cast],
        compiler_params=pltpu.CompilerParams(vmem_limit_bytes=12 * MIB),
        cost_estimate=cost(1024, 1024),
    )(keep, *got, *cast, prev)
    return out[0], list(out[1:])


def join_kernel(tokens, pieces, prev_ref, *refs):
    mine_refs, other_refs = refs[:pieces], refs[pieces : 2 * pieces]
    gt_ref, gq_ref = refs[2 * pieces :]
    odd = lax.rem(lax.axis_index("col"), 2)
    for c, (mine_ref, other_ref) in enumerate(zip(mine_refs, other_refs)):
        mine, other = mine_ref[...].astype(F32), other_ref[...].astype(F32)
        low = jnp.where(odd == 1, other, mine)
        high = jnp.where(odd == 1, mine, other)
        rows = jnp.concatenate([low, high], axis=0)
        cols = rows.shape[1]
        gt_ref[:, c * cols : (c + 1) * cols] = rows[:tokens].astype(BF16)
        gq_ref[c * cols : (c + 1) * cols, :] = rows[tokens:].T.astype(BF16)


def join_part(mine, other, prev, tokens):
    half = mine[0].shape[0]
    width = sum(x.shape[1] for x in mine)
    queries = 2 * half - tokens
    return pl.pallas_call(
        functools.partial(join_kernel, tokens, len(mine)),
        in_specs=[ANY_SPEC] + [VMEM_SPEC] * (2 * len(mine)),
        out_specs=[VMEM_SPEC] * 2,
        out_shape=[shape_of(tokens, width, BF16), shape_of(width, queries, BF16)],
        compiler_params=pltpu.CompilerParams(vmem_limit_bytes=12 * MIB),
        cost_estimate=cost(1024, 1024),
    )(prev, *mine, *other)


def inverse_kernel(chunks, corr_ref, prev_ref, *refs):
    *inv_refs, slot_ref, sems = refs
    slots, block = slot_ref.shape[0], slot_ref.shape[1]
    steps = corr_ref.shape[0] // block

    def fetch(step):
        slot = lax.rem(step, slots)
        rows = pl.ds(pl.multiple_of(step * block, block), block)
        return pltpu.make_async_copy(corr_ref.at[rows, :], slot_ref.at[slot], sems.at[slot])

    for step in range(min(slots, steps)):
        fetch(step).start()

    def body(step, carry):
        fetch(step).wait()
        rows = pl.ds(pl.multiple_of(step * block, block), block)
        slot = lax.rem(step, slots)
        for (first, width), inv_ref in zip(chunks, inv_refs):
            inv_ref[rows, :] = 1.0 / slot_ref[slot, :, first : first + width]

        @pl.when(step + slots < steps)
        def _():
            fetch(step + slots).start()

        return carry

    lax.fori_loop(0, steps, body, 0)


def inverse_part(correction, prev, chunks):
    rows, width = correction.shape
    block = largest_divisor(rows, (128, 64, 8))
    out = pl.pallas_call(
        functools.partial(inverse_kernel, chunks),
        in_specs=[ANY_SPEC, ANY_SPEC],
        out_specs=[VMEM_SPEC] * len(chunks),
        out_shape=[shape_of(rows, width, F32) for _, width in chunks],
        scratch_shapes=[pltpu.VMEM((4, block, width), F32), pltpu.SemaphoreType.DMA((4,))],
        compiler_params=pltpu.CompilerParams(vmem_limit_bytes=16 * MIB),
        cost_estimate=cost(1024, 1024),
    )(in_hbm(correction), prev)
    return list(out)


def at_end():
    me = lax.axis_index("row")
    return (me == 0) | (me == lax.axis_size("row") - 1)


def pay_kernel(has_part, acc_ref, got_ref, *refs):
    end = at_end()

    def step(rows):
        total = acc_ref[rows, :] + got_ref[rows, :].astype(F32)
        if has_part:
            total = jnp.where(end, refs[0][rows, :], total)
        refs[-1][rows, :] = total.astype(BF16)

    by_rows(acc_ref.shape[0], step)


def pay_part(hint, acc, got, part, prev):
    has_part = part is not None
    return pl.pallas_call(
        functools.partial(pay_kernel, has_part),
        in_specs=[VMEM_SPEC, VMEM_SPEC] + [VMEM_SPEC] * has_part + [ANY_SPEC],
        out_specs=VMEM_SPEC,
        out_shape=shape_of(*acc.shape, BF16),
        compiler_params=pltpu.CompilerParams(vmem_limit_bytes=12 * MIB),
        cost_estimate=cost(hint, 1024),
    )(acc, got, *([part] if has_part else []), prev)


def after_kernel(first_ref, second_ref, out_ref):
    out_ref[...] = jnp.zeros_like(out_ref)


def after_part(first, second):
    return pl.pallas_call(
        after_kernel,
        in_specs=[ANY_SPEC] * 2,
        out_specs=VMEM_SPEC,
        out_shape=shape_of(8, LANES, F32),
        compiler_params=pltpu.CompilerParams(vmem_limit_bytes=4 * MIB),
        cost_estimate=cost(10**9, 1024),
    )(first, second)


def score_kernel(
    start, scale, outs, gt_ref, gq_ref, inv_ref, sent_ref, got_ref, prev_ref, order_ref, *refs
):
    out_refs = refs[:outs]
    quot_ref, wide_ref, own_ref = refs[outs:]
    tokens = gt_ref.shape[0]
    queries = gq_ref.shape[1]
    width = inv_ref.shape[1]
    total = jnp.where(at_end(), got_ref[...].astype(F32), sent_ref[...].astype(F32))
    wide_ref[...] = total[:tokens]
    own_ref[...] = total[tokens:]
    owner = lax.broadcasted_iota(jnp.int32, (queries, width), 0) // LQ
    lane = lax.broadcasted_iota(jnp.int32, (tokens, LANES), 1)

    def quotient(q):
        own = jnp.where(owner == q, own_ref[...], 0.0).astype(BF16)
        products = jnp.dot(gq_ref[...], own, preferred_element_type=F32)
        quot_ref[q % 2] = (products * inv_ref[...]).astype(BF16)

    quotient(0)
    result = jnp.zeros((tokens, LANES), F32) if start else prev_ref[...]
    for q in range(NQ):
        if q + 1 < NQ:
            quotient(q + 1)
        mapped = jnp.dot(gt_ref[...], quot_ref[q % 2], preferred_element_type=F32)
        scaled = mapped * wide_ref[...]
        folded = scaled[:, :LANES]
        for part in range(1, width // LANES):
            folded = folded + scaled[:, part * LANES : (part + 1) * LANES]
        result = result + jnp.where(lane == q, jnp.sum(folded, axis=1, keepdims=True), 0.0)
    if scale is None:
        out_refs[0][...] = result
        return
    final = (result * scale).T[:NQ]
    if outs == 1:
        out_refs[0][...] = final
        return
    me = lax.axis_index("row")
    cols = final.shape[1] // outs
    for step, out_ref in enumerate(out_refs):
        block = final[:, :cols]
        for other in range(1, outs):
            own = final[:, other * cols : (other + 1) * cols]
            block = jnp.where(jnp.bitwise_xor(me, step) == other, own, block)
        out_ref[...] = block


def score_part(rot_gt, rot_gq_t, inv, sent, got, prev, order, start, scale, halves):
    tokens, outs = rot_gt.shape
    width = inv.shape[1]
    queries = rot_gq_t.shape[1]
    if scale is None:
        out_shape = [shape_of(tokens, LANES, F32)]
    elif halves:
        out_shape = [shape_of(NQ, tokens // halves, F32)] * halves
    else:
        out_shape = [shape_of(NQ, tokens, F32)]
    return pl.pallas_call(
        functools.partial(score_kernel, start, scale, len(out_shape)),
        in_specs=[VMEM_SPEC] * 5 + [ANY_SPEC if start else VMEM_SPEC, ANY_SPEC],
        out_specs=[VMEM_SPEC] * len(out_shape),
        out_shape=out_shape,
        scratch_shapes=[
            pltpu.VMEM((2, outs, width), BF16),
            pltpu.VMEM((tokens, width), F32),
            pltpu.VMEM((queries, width), F32),
        ],
        compiler_params=pltpu.CompilerParams(vmem_limit_bytes=16 * MIB),
        cost_estimate=cost(1024, 1024),
    )(rot_gt, rot_gq_t, inv, sent, got, prev, order)


def gather_kernel(*refs):
    total = refs[0][...]
    for ref in refs[1:-1]:
        total = total + ref[...]
    refs[-1][...] = total


def gather_part(arrays):
    return pl.pallas_call(
        gather_kernel,
        in_specs=[VMEM_SPEC] * len(arrays),
        out_specs=VMEM_SPEC,
        out_shape=shape_of(*arrays[0].shape, F32),
        compiler_params=pltpu.CompilerParams(vmem_limit_bytes=4 * MIB),
        cost_estimate=cost(1024, 1024),
    )(*arrays)


def line_sum(partial, axis):
    n = lax.axis_size(axis)
    half = n // 2
    me = lax.axis_index(axis)
    if n % 2:
        return lax.psum(partial, axis).astype(BF16)
    acc = partial
    for s in range(half - 1):
        pairs = [(s, s + 1), (n - 1 - s, n - 2 - s)]
        acc = acc + lax.ppermute(acc.astype(BF16), axis, pairs).astype(F32)
    got = lax.ppermute(acc.astype(BF16), axis, [(half - 1, half), (half, half - 1)])
    total = (acc + got.astype(F32)).astype(BF16)
    for s in range(half - 2, -1, -1):
        pairs = [(s + 1, s), (n - 2 - s, n - 1 - s)]
        got = lax.ppermute(total, axis, pairs)
        total = jnp.where((me == s) | (me == n - 1 - s), got, total)
    return total


def owned_sum(partial, axis):
    n = lax.axis_size(axis)
    me = lax.axis_index(axis)
    total = lax.dynamic_index_in_dim(partial, me, 0, keepdims=False)
    for step in range(1, n):
        block = lax.dynamic_index_in_dim(partial, (me + step) % n, 0, keepdims=False)
        total = total + lax.ppermute(block, axis, [(d, (d + step) % n) for d in range(n)])
    return total


def shared_sum(partial, axis):
    n = lax.axis_size(axis)
    total = partial
    for step in range(1, n):
        total = total + lax.ppermute(partial, axis, [(d, (d + step) % n) for d in range(n)])
    return total


def on_device(act_train, act_query, grad_train, grad_query, basis_in, basis_out, correction):
    norm_scale = (O * I * LQ) ** (-0.5)
    tokens = act_train.shape[0]
    n_row, n_col = lax.axis_size("row"), lax.axis_size("col")
    chunks = chunk_list(basis_in.shape[1])
    count = len(chunks)
    line = n_row == 4
    flip = [(d, d ^ 1) for d in range(n_col)]
    outer = [(0, 1), (1, 0), (2, 3), (3, 2)]
    inner = []
    for c in range(n_col):
        inner += [(n_col + c, 2 * n_col + c), (2 * n_col + c, n_col + c)]
        inner += [(c, c ^ 1), (3 * n_col + c, 3 * n_col + (c ^ 1))]
    sent, got, acc, got_mid = {}, {}, {}, {}

    def swap(j, payload):
        sent[j] = payload
        got[j] = lax.ppermute(payload, "row", outer)

    def meet(j, prev):
        if not line or j >= count:
            return prev
        cast = [parts[2]] if j == 0 else []
        acc[j], thin = add_part(parts[j], [got[j]], prev, 1, cast)
        got_mid[j] = lax.ppermute(thin[0], ("row", "col"), inner)
        if cast:
            swap(2, thin[1])
        return thin[0]

    def pay(j, prev):
        if not line:
            sent[j + LAG] = got[j + LAG] = line_sum(parts[j], "row")
            return prev
        part = parts[j + LAG] if j + LAG < count else None
        payload = pay_part(4 * 10**9 if j == 0 else 1024, acc[j], got_mid[j], part, prev)
        swap(j + LAG, payload)
        return payload

    def score(k, sums, prev):
        return score_part(
            rot_gt, rot_gq_t, invs[k], sent[k + LAG], got[k + LAG], sums[0], prev,
            k == 0, norm_scale if k == count - 1 else None, halves,
        )

    early = min(LAG + 2, count)
    widths = [width for _, width in chunks]
    parts, narrow = in_part(
        act_train, act_query, basis_in, act_query, chunks[:1], [widths[0]]
    )
    if line:
        swap(0, narrow[0])
    more, narrow = in_part(
        act_train, act_query, basis_in, parts[0], chunks[1:early], [widths[1]]
    )
    parts += more
    if line:
        swap(1, narrow[0])
    (half_sum,) = out_part(grad_train, grad_query, basis_out, parts[-1], None)
    prev = meet(0, half_sum)
    keep, *give = out_part(grad_train, grad_query, basis_out, prev, half_sum)
    given = [lax.ppermute(piece, "col", flip) for piece in give]
    prev = meet(1, keep)
    if line:
        prev = after_part(prev, got[2])
    prev = meet(2, pay(0, prev))
    outs = pieces_of(keep.shape[1], 2)
    wide, thin = add_part(keep, given, prev, outs)
    prev, bit = wide, 2
    while bit < n_col:
        other = [lax.ppermute(x, "col", [(d, d ^ bit) for d in range(n_col)]) for x in thin]
        if bit == 2:
            more, _ = in_part(act_train, act_query, basis_in, prev, chunks[early:], [])
            parts += more
            prev = meet(3, pay(1, more[-1]))
            invs = inverse_part(correction, prev, chunks)
            prev = pay(2, invs[0])
        wide, thin = add_part(wide, other, prev, outs)
        prev = wide
        bit *= 2
    other = [lax.ppermute(x, "col", flip) for x in thin]
    prev = meet(5, pay(3, meet(4, prev)))
    rot_gt, rot_gq_t = join_part(thin, other, prev, tokens)
    prev = rot_gt
    halves = n_row if n_row == 4 and n_col == 4 and tokens % (n_row * LANES) == 0 else 0
    sums = score(0, [rot_gt], prev)
    done = 1
    for j in range(6, count + 1):
        prev = meet(j, pay(j - 2, sums[0]))
        sums = score(done, sums, prev)
        done += 1
    if line:
        prev = after_part(sums[0], got[count])
    prev = pay(count - 1, prev)
    for k in range(done, count):
        sums = score(k, sums, prev)
    if not halves:
        blocks = sums[0].reshape(NQ, n_row, tokens // n_row).transpose(1, 0, 2)
        return shared_sum(owned_sum(blocks, "row"), "col")
    moved = [
        lax.ppermute(sums[step], "row", [(d, d ^ step) for d in range(n_row)])
        for step in range(1, n_row)
    ]
    owned = gather_part([sums[0]] + moved)
    moved = [
        lax.ppermute(owned, "col", [(d, d ^ step) for d in range(n_col)]) for step in range(1, n_col)
    ]
    return gather_part([owned] + moved)


def solution(mesh):
    in_specs = (
        P("groups", "row"),
        P("groups", "row"),
        P("groups", "col"),
        P("groups", "col"),
        P(("groups", "row"), "col"),
        P(("groups", "col"), "row"),
        P(("groups", "row"), "col"),
    )
    out_specs = P("groups", "row")
    return jax.shard_map(
        on_device, mesh=mesh, in_specs=in_specs, out_specs=out_specs, check_vma=False
    )
```

```python
import functools

import jax
import jax.numpy as jnp
from jax import lax
from jax.experimental import pallas as pl
from jax.experimental.pallas import tpu as pltpu
from jax.sharding import PartitionSpec as P

I = 8192
O = 4096
NQ = 8
LQ = 16
LANES = 128
CHUNKS = 8
LAG = 3
F32 = jnp.float32
BF16 = jnp.bfloat16
MIB = 1 << 20

VMEM_SPEC = pl.BlockSpec(memory_space=pltpu.VMEM)
SMEM_SPEC = pl.BlockSpec(memory_space=pltpu.SMEM)
ANY_SPEC = pl.BlockSpec(memory_space=pl.ANY)


def shape_of(rows, width, dtype):
    return jax.ShapeDtypeStruct((rows, width), dtype)


def chunk_list(size):
    tiles = size // LANES
    count = min(CHUNKS, tiles)
    chunks, first = [], 0
    for k in range(count):
        width = LANES * (tiles // count + (1 if k < tiles % count else 0))
        chunks.append((first, width))
        first += width
    return chunks


def largest_divisor(size, choices):
    for choice in choices:
        if size % choice == 0:
            return choice
    return size


def pieces_of(width, most):
    return max(p for p in range(1, most + 1) if width % (p * LANES) == 0)


def cost(flops, bytes_accessed):
    return pl.CostEstimate(flops=flops, bytes_accessed=bytes_accessed, transcendentals=0)


def in_hbm(x):
    return pltpu.with_memory_space_constraint(x, pltpu.HBM)


def halves_dot(rows, basis):
    half = rows.shape[0] // 2
    return [jnp.dot(part, basis, preferred_element_type=F32) for part in (rows[:half], rows[half:])]


def in_kernel(chunks, narrow, groups, train_ref, query_ref, basis_ref, prev_ref, *refs):
    count = len(chunks)
    rows_ref, slot_ref, sum_ref, sems = refs[count + narrow :]
    tokens, queries = train_ref.shape[0], query_ref.shape[0]
    start, total = chunks[0][0], slot_ref.shape[2]
    depth = slot_ref.shape[1]
    half = rows_ref.shape[1] // 2

    def copies(g):
        part = pl.ds(pl.multiple_of(g * depth, depth), depth)
        return [
            pltpu.make_async_copy(
                basis_ref.at[part, pl.ds(start, total)], slot_ref.at[g], sems.at[g, 0]
            ),
            pltpu.make_async_copy(
                train_ref.at[:, part], rows_ref.at[g, pl.ds(0, tokens), :], sems.at[g, 1]
            ),
            pltpu.make_async_copy(
                query_ref.at[:, part], rows_ref.at[g, pl.ds(tokens, queries), :], sems.at[g, 2]
            ),
        ]

    for g in range(groups):
        for copy in copies(g):
            copy.start()

    def body(g, carry):
        for copy in copies(g):
            copy.wait()
        for h, value in enumerate(halves_dot(rows_ref[g], slot_ref[g])):
            span = slice(h * half, (h + 1) * half)
            if isinstance(g, int):
                sum_ref[span, :] = value + sum_ref[span, :] if g > 0 else value
            else:
                sum_ref[span, :] = value + jnp.where(g > 0, sum_ref[span, :], 0.0)
        return carry

    if total <= 2 * LANES:
        for g in range(groups):
            body(g, 0)
    else:
        lax.fori_loop(0, groups, body, 0)
    for j, (first, width) in enumerate(chunks):
        refs[j][...] = sum_ref[:, first - start : first - start + width]
    column = 0
    for narrow_ref in refs[count : count + narrow]:
        width = narrow_ref.shape[1]
        narrow_ref[...] = sum_ref[:, column : column + width].astype(BF16)
        column += width


def in_part(act_train, act_query, basis_in, prev, chunks, narrow):
    tokens, depth = act_train.shape
    rows = tokens + act_query.shape[0]
    total = sum(width for _, width in chunks)
    groups = next(g for g in (4, 2, 1) if depth % (g * LANES) == 0)
    shapes = [shape_of(rows, width, F32) for _, width in chunks]
    shapes += [shape_of(rows, width, BF16) for width in narrow]
    out = pl.pallas_call(
        functools.partial(in_kernel, chunks, len(narrow), groups),
        in_specs=[ANY_SPEC] * 4,
        out_specs=[VMEM_SPEC] * len(shapes),
        out_shape=shapes,
        scratch_shapes=[
            pltpu.VMEM((groups, rows, depth // groups), BF16),
            pltpu.VMEM((groups, depth // groups, total), BF16),
            pltpu.VMEM((rows, total), F32),
            pltpu.SemaphoreType.DMA((groups, 3)),
        ],
        compiler_params=pltpu.CompilerParams(vmem_limit_bytes=24 * MIB),
        cost_estimate=cost(1024, 1024),
    )(in_hbm(act_train), in_hbm(act_query), in_hbm(basis_in), prev)
    return list(out[: len(chunks)]), list(out[len(chunks) :])


def out_kernel(begin, steps, last, train_ref, query_ref, basis_ref, prev_ref, *refs):
    if last:
        start_ref, keep_ref, *give_refs, rows_ref, slot_ref, acc_ref, sems = refs
    else:
        acc_ref, rows_ref, slot_ref, sems = refs
    tokens, queries = train_ref.shape[0], query_ref.shape[0]
    slots, block = slot_ref.shape[0], slot_ref.shape[1]
    half, width = acc_ref.shape[0] // 2, acc_ref.shape[1]
    tile = largest_divisor(width, (256, 128))

    def copies(step):
        slot = lax.rem(step, slots)
        part = pl.ds(pl.multiple_of((begin + step) * block, block), block)
        return [
            pltpu.make_async_copy(basis_ref.at[part, :], slot_ref.at[slot], sems.at[slot, 0]),
            pltpu.make_async_copy(
                train_ref.at[:, part], rows_ref.at[slot, pl.ds(0, tokens), :], sems.at[slot, 1]
            ),
            pltpu.make_async_copy(
                query_ref.at[:, part], rows_ref.at[slot, pl.ds(tokens, queries), :], sems.at[slot, 2]
            ),
        ]

    for step in range(min(slots - 1, steps)):
        for copy in copies(step):
            copy.start()
    acc_ref[...] = start_ref[...] if last else jnp.zeros_like(acc_ref)

    def body(step, carry):
        for copy in copies(step):
            copy.wait()

        @pl.when(step + slots - 1 < steps)
        def _():
            for copy in copies(step + slots - 1):
                copy.start()

        slot = lax.rem(step, slots)
        rows = rows_ref[slot]
        for first in range(0, width, tile):
            span = slice(first, first + tile)
            acc_ref[:, span] += jnp.dot(rows, slot_ref[slot, :, span], preferred_element_type=F32)
        return carry

    lax.fori_loop(0, steps, body, 0)
    if not last:
        return
    odd = lax.rem(lax.axis_index("col"), 2)
    keep_ref[...] = acc_ref[pl.ds(pl.multiple_of(odd * half, 16), half), :]
    cols = give_refs[0].shape[1]
    for c, give_ref in enumerate(give_refs):
        span = slice(c * cols, (c + 1) * cols)
        give_ref[...] = acc_ref[pl.ds(pl.multiple_of((1 - odd) * half, 16), half), span]


def out_part(grad_train, grad_query, basis_out, prev, acc):
    tokens, depth = grad_train.shape
    width = basis_out.shape[1]
    rows = tokens + grad_query.shape[0]
    block = largest_divisor(depth, (512, 256, 128))
    steps = depth // block
    slots = min(6, steps)
    last = acc is not None
    first = steps * 2 // 7
    begin, count = (first, steps - first) if last else (0, first)
    pieces = pieces_of(width, 2)
    if last:
        out_shape = [shape_of(rows // 2, width, F32)]
        out_shape += [shape_of(rows // 2, width // pieces, F32)] * pieces
    else:
        out_shape = [shape_of(rows, width, F32)]
    return pl.pallas_call(
        functools.partial(out_kernel, begin, count, last),
        in_specs=[ANY_SPEC] * 4 + [VMEM_SPEC] * last,
        out_specs=[VMEM_SPEC] * len(out_shape),
        out_shape=out_shape,
        scratch_shapes=[
            pltpu.VMEM((slots, rows, block), BF16),
            pltpu.VMEM((slots, block, width), BF16),
        ]
        + [pltpu.VMEM((rows, width), F32)] * last
        + [pltpu.SemaphoreType.DMA((slots, 3))],
        compiler_params=pltpu.CompilerParams(vmem_limit_bytes=22 * MIB),
        cost_estimate=cost(2 * rows * block * count * width if last else 1024, 1024),
    )(
        in_hbm(grad_train), in_hbm(grad_query), in_hbm(basis_out), prev, *([acc] if last else [])
    )


def by_rows(rows, step):
    block = rows // 5 if rows % 80 == 0 else rows

    def body(i, carry):
        step(pl.ds(pl.multiple_of(i * block, block), block))
        return carry

    lax.fori_loop(0, rows // block, body, 0)


def add_kernel(pieces, outs, cast, keep_ref, *refs):
    wide_ref, narrow_refs = refs[pieces + cast + 1], refs[pieces + cast + 2 :]
    width = keep_ref.shape[1]

    def step(rows):
        total = keep_ref[rows, :]
        got = [refs[c][rows, :].astype(F32) for c in range(pieces)]
        total = total + (jnp.concatenate(got, axis=1) if pieces > 1 else got[0])
        wide_ref[rows, :] = total
        cols = width // outs
        for c in range(outs):
            narrow_refs[c][rows, :] = total[:, c * cols : (c + 1) * cols].astype(BF16)
        if cast:
            narrow_refs[outs][rows, :] = refs[pieces][rows, :].astype(BF16)

    by_rows(keep_ref.shape[0], step)


def add_part(keep, got, prev, outs=1, cast=()):
    rows, width = keep.shape
    out = pl.pallas_call(
        functools.partial(add_kernel, len(got), outs, len(cast)),
        in_specs=[VMEM_SPEC] * (1 + len(got) + len(cast)) + [ANY_SPEC],
        out_specs=[VMEM_SPEC] * (1 + outs + len(cast)),
        out_shape=[shape_of(rows, width, F32)]
        + [shape_of(rows, width // outs, BF16)] * outs
        + [shape_of(*x.shape, BF16) for x in cast],
        compiler_params=pltpu.CompilerParams(vmem_limit_bytes=12 * MIB),
        cost_estimate=cost(1024, 1024),
    )(keep, *got, *cast, prev)
    return out[0], list(out[1:])


def join_kernel(tokens, pieces, prev_ref, *refs):
    mine_refs, other_refs = refs[:pieces], refs[pieces : 2 * pieces]
    gt_ref, gq_ref = refs[2 * pieces :]
    odd = lax.rem(lax.axis_index("col"), 2)
    for c, (mine_ref, other_ref) in enumerate(zip(mine_refs, other_refs)):
        mine, other = mine_ref[...].astype(F32), other_ref[...].astype(F32)
        low = jnp.where(odd == 1, other, mine)
        high = jnp.where(odd == 1, mine, other)
        rows = jnp.concatenate([low, high], axis=0)
        cols = rows.shape[1]
        gt_ref[:, c * cols : (c + 1) * cols] = rows[:tokens].astype(BF16)
        gq_ref[c * cols : (c + 1) * cols, :] = rows[tokens:].T.astype(BF16)


def join_part(mine, other, prev, tokens):
    half = mine[0].shape[0]
    width = sum(x.shape[1] for x in mine)
    queries = 2 * half - tokens
    return pl.pallas_call(
        functools.partial(join_kernel, tokens, len(mine)),
        in_specs=[ANY_SPEC] + [VMEM_SPEC] * (2 * len(mine)),
        out_specs=[VMEM_SPEC] * 2,
        out_shape=[shape_of(tokens, width, BF16), shape_of(width, queries, BF16)],
        compiler_params=pltpu.CompilerParams(vmem_limit_bytes=12 * MIB),
        cost_estimate=cost(1024, 1024),
    )(prev, *mine, *other)


def inverse_kernel(chunks, corr_ref, prev_ref, *refs):
    *inv_refs, slot_ref, sems = refs
    slots, block = slot_ref.shape[0], slot_ref.shape[1]
    steps = corr_ref.shape[0] // block

    def fetch(step):
        slot = lax.rem(step, slots)
        rows = pl.ds(pl.multiple_of(step * block, block), block)
        return pltpu.make_async_copy(corr_ref.at[rows, :], slot_ref.at[slot], sems.at[slot])

    for step in range(min(slots, steps)):
        fetch(step).start()

    def body(step, carry):
        fetch(step).wait()
        rows = pl.ds(pl.multiple_of(step * block, block), block)
        slot = lax.rem(step, slots)
        for (first, width), inv_ref in zip(chunks, inv_refs):
            inv_ref[rows, :] = 1.0 / slot_ref[slot, :, first : first + width]

        @pl.when(step + slots < steps)
        def _():
            fetch(step + slots).start()

        return carry

    lax.fori_loop(0, steps, body, 0)


def inverse_part(correction, prev, chunks):
    rows, width = correction.shape
    block = largest_divisor(rows, (128, 64, 8))
    out = pl.pallas_call(
        functools.partial(inverse_kernel, chunks),
        in_specs=[ANY_SPEC, ANY_SPEC],
        out_specs=[VMEM_SPEC] * len(chunks),
        out_shape=[shape_of(rows, width, F32) for _, width in chunks],
        scratch_shapes=[pltpu.VMEM((4, block, width), F32), pltpu.SemaphoreType.DMA((4,))],
        compiler_params=pltpu.CompilerParams(vmem_limit_bytes=16 * MIB),
        cost_estimate=cost(1024, 1024),
    )(in_hbm(correction), prev)
    return list(out)


def at_end():
    me = lax.axis_index("row")
    return (me == 0) | (me == lax.axis_size("row") - 1)


def pay_kernel(has_part, acc_ref, got_ref, *refs):
    end = at_end()

    def step(rows):
        total = acc_ref[rows, :] + got_ref[rows, :].astype(F32)
        if has_part:
            total = jnp.where(end, refs[0][rows, :], total)
        refs[-1][rows, :] = total.astype(BF16)

    by_rows(acc_ref.shape[0], step)


def pay_part(hint, acc, got, part, prev):
    has_part = part is not None
    return pl.pallas_call(
        functools.partial(pay_kernel, has_part),
        in_specs=[VMEM_SPEC, VMEM_SPEC] + [VMEM_SPEC] * has_part + [ANY_SPEC],
        out_specs=VMEM_SPEC,
        out_shape=shape_of(*acc.shape, BF16),
        compiler_params=pltpu.CompilerParams(vmem_limit_bytes=12 * MIB),
        cost_estimate=cost(hint, 1024),
    )(acc, got, *([part] if has_part else []), prev)


def after_kernel(first_ref, second_ref, out_ref):
    out_ref[...] = jnp.zeros_like(out_ref)


def after_part(first, second):
    return pl.pallas_call(
        after_kernel,
        in_specs=[ANY_SPEC] * 2,
        out_specs=VMEM_SPEC,
        out_shape=shape_of(8, LANES, F32),
        compiler_params=pltpu.CompilerParams(vmem_limit_bytes=4 * MIB),
        cost_estimate=cost(10**9, 1024),
    )(first, second)


def score_kernel(
    start, scale, outs, gt_ref, gq_ref, inv_ref, sent_ref, got_ref, prev_ref, order_ref, *refs
):
    out_refs = refs[:outs]
    quot_ref, wide_ref, own_ref = refs[outs:]
    tokens = gt_ref.shape[0]
    queries = gq_ref.shape[1]
    width = inv_ref.shape[1]
    total = jnp.where(at_end(), got_ref[...].astype(F32), sent_ref[...].astype(F32))
    wide_ref[...] = total[:tokens]
    own_ref[...] = total[tokens:]
    owner = lax.broadcasted_iota(jnp.int32, (queries, width), 0) // LQ
    lane = lax.broadcasted_iota(jnp.int32, (tokens, LANES), 1)

    def quotient(q):
        own = jnp.where(owner == q, own_ref[...], 0.0).astype(BF16)
        products = jnp.dot(gq_ref[...], own, preferred_element_type=F32)
        quot_ref[q % 2] = (products * inv_ref[...]).astype(BF16)

    quotient(0)
    result = jnp.zeros((tokens, LANES), F32) if start else prev_ref[...]
    for q in range(NQ):
        if q + 1 < NQ:
            quotient(q + 1)
        mapped = jnp.dot(gt_ref[...], quot_ref[q % 2], preferred_element_type=F32)
        scaled = mapped * wide_ref[...]
        folded = scaled[:, :LANES]
        for part in range(1, width // LANES):
            folded = folded + scaled[:, part * LANES : (part + 1) * LANES]
        result = result + jnp.where(lane == q, jnp.sum(folded, axis=1, keepdims=True), 0.0)
    if scale is None:
        out_refs[0][...] = result
        return
    final = (result * scale).T[:NQ]
    if outs == 1:
        out_refs[0][...] = final
        return
    me = lax.axis_index("row")
    cols = final.shape[1] // outs
    for step, out_ref in enumerate(out_refs):
        block = final[:, :cols]
        for other in range(1, outs):
            own = final[:, other * cols : (other + 1) * cols]
            block = jnp.where(jnp.bitwise_xor(me, step) == other, own, block)
        out_ref[...] = block


def score_part(rot_gt, rot_gq_t, inv, sent, got, prev, order, start, scale, halves):
    tokens, outs = rot_gt.shape
    width = inv.shape[1]
    queries = rot_gq_t.shape[1]
    if scale is None:
        out_shape = [shape_of(tokens, LANES, F32)]
    elif halves:
        out_shape = [shape_of(NQ, tokens // halves, F32)] * halves
    else:
        out_shape = [shape_of(NQ, tokens, F32)]
    return pl.pallas_call(
        functools.partial(score_kernel, start, scale, len(out_shape)),
        in_specs=[VMEM_SPEC] * 5 + [ANY_SPEC if start else VMEM_SPEC, ANY_SPEC],
        out_specs=[VMEM_SPEC] * len(out_shape),
        out_shape=out_shape,
        scratch_shapes=[
            pltpu.VMEM((2, outs, width), BF16),
            pltpu.VMEM((tokens, width), F32),
            pltpu.VMEM((queries, width), F32),
        ],
        compiler_params=pltpu.CompilerParams(vmem_limit_bytes=16 * MIB),
        cost_estimate=cost(1024, 1024),
    )(rot_gt, rot_gq_t, inv, sent, got, prev, order)


def gather_kernel(*refs):
    total = refs[0][...]
    for ref in refs[1:-1]:
        total = total + ref[...]
    refs[-1][...] = total


def gather_part(arrays):
    return pl.pallas_call(
        gather_kernel,
        in_specs=[VMEM_SPEC] * len(arrays),
        out_specs=VMEM_SPEC,
        out_shape=shape_of(*arrays[0].shape, F32),
        compiler_params=pltpu.CompilerParams(vmem_limit_bytes=4 * MIB),
        cost_estimate=cost(1024, 1024),
    )(*arrays)


def line_sum(partial, axis):
    n = lax.axis_size(axis)
    half = n // 2
    me = lax.axis_index(axis)
    if n % 2:
        return lax.psum(partial, axis).astype(BF16)
    acc = partial
    for s in range(half - 1):
        pairs = [(s, s + 1), (n - 1 - s, n - 2 - s)]
        acc = acc + lax.ppermute(acc.astype(BF16), axis, pairs).astype(F32)
    got = lax.ppermute(acc.astype(BF16), axis, [(half - 1, half), (half, half - 1)])
    total = (acc + got.astype(F32)).astype(BF16)
    for s in range(half - 2, -1, -1):
        pairs = [(s + 1, s), (n - 2 - s, n - 1 - s)]
        got = lax.ppermute(total, axis, pairs)
        total = jnp.where((me == s) | (me == n - 1 - s), got, total)
    return total


def owned_sum(partial, axis):
    n = lax.axis_size(axis)
    me = lax.axis_index(axis)
    total = lax.dynamic_index_in_dim(partial, me, 0, keepdims=False)
    for step in range(1, n):
        block = lax.dynamic_index_in_dim(partial, (me + step) % n, 0, keepdims=False)
        total = total + lax.ppermute(block, axis, [(d, (d + step) % n) for d in range(n)])
    return total


def shared_sum(partial, axis):
    n = lax.axis_size(axis)
    total = partial
    for step in range(1, n):
        total = total + lax.ppermute(partial, axis, [(d, (d + step) % n) for d in range(n)])
    return total


def on_device(act_train, act_query, grad_train, grad_query, basis_in, basis_out, correction):
    norm_scale = (O * I * LQ) ** (-0.5)
    tokens = act_train.shape[0]
    n_row, n_col = lax.axis_size("row"), lax.axis_size("col")
    chunks = chunk_list(basis_in.shape[1])
    count = len(chunks)
    line = n_row == 4
    flip = [(d, d ^ 1) for d in range(n_col)]
    outer = [(0, 1), (1, 0), (2, 3), (3, 2)]
    inner = []
    for c in range(n_col):
        inner += [(n_col + c, 2 * n_col + c), (2 * n_col + c, n_col + c)]
        inner += [(c, c ^ 1), (3 * n_col + c, 3 * n_col + (c ^ 1))]
    sent, got, acc, got_mid = {}, {}, {}, {}

    def swap(j, payload):
        sent[j] = payload
        got[j] = lax.ppermute(payload, "row", outer)

    def meet(j, prev):
        if not line or j >= count:
            return prev
        cast = [parts[2]] if j == 0 else []
        acc[j], thin = add_part(parts[j], [got[j]], prev, 1, cast)
        got_mid[j] = lax.ppermute(thin[0], ("row", "col"), inner)
        if cast:
            swap(2, thin[1])
        return thin[0]

    def pay(j, prev):
        if not line:
            sent[j + LAG] = got[j + LAG] = line_sum(parts[j], "row")
            return prev
        part = parts[j + LAG] if j + LAG < count else None
        payload = pay_part(4 * 10**9 if j == 0 else 1024, acc[j], got_mid[j], part, prev)
        swap(j + LAG, payload)
        return payload

    def score(k, sums, prev):
        return score_part(
            rot_gt, rot_gq_t, invs[k], sent[k + LAG], got[k + LAG], sums[0], prev,
            k == 0, norm_scale if k == count - 1 else None, halves,
        )

    early = min(LAG + 2, count)
    widths = [width for _, width in chunks]
    parts, narrow = in_part(
        act_train, act_query, basis_in, act_query, chunks[:1], [widths[0]]
    )
    if line:
        swap(0, narrow[0])
    more, narrow = in_part(
        act_train, act_query, basis_in, parts[0], chunks[1:early], [widths[1]]
    )
    parts += more
    if line:
        swap(1, narrow[0])
    (half_sum,) = out_part(grad_train, grad_query, basis_out, parts[-1], None)
    prev = meet(0, half_sum)
    keep, *give = out_part(grad_train, grad_query, basis_out, prev, half_sum)
    given = [lax.ppermute(piece, "col", flip) for piece in give]
    prev = meet(1, keep)
    if line:
        prev = after_part(prev, got[2])
    prev = meet(2, pay(0, prev))
    outs = pieces_of(keep.shape[1], 2)
    wide, thin = add_part(keep, given, prev, outs)
    prev, bit = wide, 2
    while bit < n_col:
        other = [lax.ppermute(x, "col", [(d, d ^ bit) for d in range(n_col)]) for x in thin]
        if bit == 2:
            more, _ = in_part(act_train, act_query, basis_in, prev, chunks[early:], [])
            parts += more
            prev = meet(3, pay(1, more[-1]))
            invs = inverse_part(correction, prev, chunks)
            prev = pay(2, invs[0])
        wide, thin = add_part(wide, other, prev, outs)
        prev = wide
        bit *= 2
    other = [lax.ppermute(x, "col", flip) for x in thin]
    prev = meet(5, pay(3, meet(4, prev)))
    rot_gt, rot_gq_t = join_part(thin, other, prev, tokens)
    prev = rot_gt
    halves = n_row if n_row == 4 and n_col == 4 and tokens % (n_row * LANES) == 0 else 0
    sums = score(0, [rot_gt], prev)
    done = 1
    for j in range(6, count + 1):
        prev = meet(j, pay(j - 2, sums[0]))
        sums = score(done, sums, prev)
        done += 1
    if line:
        prev = after_part(sums[0], got[count])
    prev = pay(count - 1, prev)
    for k in range(done, count):
        sums = score(k, sums, prev)
    if not halves:
        blocks = sums[0].reshape(NQ, n_row, tokens // n_row).transpose(1, 0, 2)
        return shared_sum(owned_sum(blocks, "row"), "col")
    moved = [
        lax.ppermute(sums[step], "row", [(d, d ^ step) for d in range(n_row)])
        for step in range(1, n_row)
    ]
    owned = gather_part([sums[0]] + moved)
    moved = [
        lax.ppermute(owned, "col", [(d, d ^ step) for d in range(n_col)]) for step in range(1, n_col)
    ]
    return gather_part([owned] + moved)


def solution(mesh):
    in_specs = (
        P("groups", "row"),
        P("groups", "row"),
        P("groups", "col"),
        P("groups", "col"),
        P(("groups", "row"), "col"),
        P(("groups", "col"), "row"),
        P(("groups", "row"), "col"),
    )
    out_specs = P("groups", "row")
    return jax.shard_map(
        on_device, mesh=mesh, in_specs=in_specs, out_specs=out_specs, check_vma=False
    )
```

```python
import functools

import jax
import jax.numpy as jnp
from jax import lax
from jax.experimental import pallas as pl
from jax.experimental.pallas import tpu as pltpu
from jax.sharding import PartitionSpec as P

I = 8192
O = 4096
NQ = 8
LQ = 16
LANES = 128
CHUNKS = 8
LAG = 3
F32 = jnp.float32
BF16 = jnp.bfloat16
MIB = 1 << 20

VMEM_SPEC = pl.BlockSpec(memory_space=pltpu.VMEM)
SMEM_SPEC = pl.BlockSpec(memory_space=pltpu.SMEM)
ANY_SPEC = pl.BlockSpec(memory_space=pl.ANY)


def shape_of(rows, width, dtype):
    return jax.ShapeDtypeStruct((rows, width), dtype)


def chunk_list(size):
    tiles = size // LANES
    count = min(CHUNKS, tiles)
    chunks, first = [], 0
    for k in range(count):
        width = LANES * (tiles // count + (1 if k < tiles % count else 0))
        chunks.append((first, width))
        first += width
    return chunks


def largest_divisor(size, choices):
    for choice in choices:
        if size % choice == 0:
            return choice
    return size


def pieces_of(width, most):
    return max(p for p in range(1, most + 1) if width % (p * LANES) == 0)


def cost(flops, bytes_accessed):
    return pl.CostEstimate(flops=flops, bytes_accessed=bytes_accessed, transcendentals=0)


def in_hbm(x):
    return pltpu.with_memory_space_constraint(x, pltpu.HBM)


def halves_dot(rows, basis):
    half = rows.shape[0] // 2
    return [jnp.dot(part, basis, preferred_element_type=F32) for part in (rows[:half], rows[half:])]


def in_kernel(chunks, narrow, groups, train_ref, query_ref, basis_ref, prev_ref, *refs):
    count = len(chunks)
    rows_ref, slot_ref, sum_ref, sems = refs[count + narrow :]
    tokens, queries = train_ref.shape[0], query_ref.shape[0]
    start, total = chunks[0][0], slot_ref.shape[2]
    depth = slot_ref.shape[1]
    half = rows_ref.shape[1] // 2

    def copies(g):
        part = pl.ds(pl.multiple_of(g * depth, depth), depth)
        return [
            pltpu.make_async_copy(
                basis_ref.at[part, pl.ds(start, total)], slot_ref.at[g], sems.at[g, 0]
            ),
            pltpu.make_async_copy(
                train_ref.at[:, part], rows_ref.at[g, pl.ds(0, tokens), :], sems.at[g, 1]
            ),
            pltpu.make_async_copy(
                query_ref.at[:, part], rows_ref.at[g, pl.ds(tokens, queries), :], sems.at[g, 2]
            ),
        ]

    for g in range(groups):
        for copy in copies(g):
            copy.start()

    def body(g, carry):
        for copy in copies(g):
            copy.wait()
        for h, value in enumerate(halves_dot(rows_ref[g], slot_ref[g])):
            span = slice(h * half, (h + 1) * half)
            if isinstance(g, int):
                sum_ref[span, :] = value + sum_ref[span, :] if g > 0 else value
            else:
                sum_ref[span, :] = value + jnp.where(g > 0, sum_ref[span, :], 0.0)
        return carry

    if total <= 2 * LANES:
        for g in range(groups):
            body(g, 0)
    else:
        lax.fori_loop(0, groups, body, 0)
    for j, (first, width) in enumerate(chunks):
        refs[j][...] = sum_ref[:, first - start : first - start + width]
    column = 0
    for narrow_ref in refs[count : count + narrow]:
        width = narrow_ref.shape[1]
        narrow_ref[...] = sum_ref[:, column : column + width].astype(BF16)
        column += width


def in_part(act_train, act_query, basis_in, prev, chunks, narrow):
    tokens, depth = act_train.shape
    rows = tokens + act_query.shape[0]
    total = sum(width for _, width in chunks)
    groups = next(g for g in (4, 2, 1) if depth % (g * LANES) == 0)
    shapes = [shape_of(rows, width, F32) for _, width in chunks]
    shapes += [shape_of(rows, width, BF16) for width in narrow]
    out = pl.pallas_call(
        functools.partial(in_kernel, chunks, len(narrow), groups),
        in_specs=[ANY_SPEC] * 4,
        out_specs=[VMEM_SPEC] * len(shapes),
        out_shape=shapes,
        scratch_shapes=[
            pltpu.VMEM((groups, rows, depth // groups), BF16),
            pltpu.VMEM((groups, depth // groups, total), BF16),
            pltpu.VMEM((rows, total), F32),
            pltpu.SemaphoreType.DMA((groups, 3)),
        ],
        compiler_params=pltpu.CompilerParams(vmem_limit_bytes=24 * MIB),
        cost_estimate=cost(1024, 1024),
    )(in_hbm(act_train), in_hbm(act_query), in_hbm(basis_in), prev)
    return list(out[: len(chunks)]), list(out[len(chunks) :])


def out_kernel(begin, steps, last, train_ref, query_ref, basis_ref, prev_ref, *refs):
    if last:
        start_ref, keep_ref, *give_refs, rows_ref, slot_ref, acc_ref, sems = refs
    else:
        acc_ref, rows_ref, slot_ref, sems = refs
    tokens, queries = train_ref.shape[0], query_ref.shape[0]
    slots, block = slot_ref.shape[0], slot_ref.shape[1]
    half, width = acc_ref.shape[0] // 2, acc_ref.shape[1]
    tile = largest_divisor(width, (256, 128))

    def copies(step):
        slot = lax.rem(step, slots)
        part = pl.ds(pl.multiple_of((begin + step) * block, block), block)
        return [
            pltpu.make_async_copy(basis_ref.at[part, :], slot_ref.at[slot], sems.at[slot, 0]),
            pltpu.make_async_copy(
                train_ref.at[:, part], rows_ref.at[slot, pl.ds(0, tokens), :], sems.at[slot, 1]
            ),
            pltpu.make_async_copy(
                query_ref.at[:, part], rows_ref.at[slot, pl.ds(tokens, queries), :], sems.at[slot, 2]
            ),
        ]

    for step in range(min(slots - 1, steps)):
        for copy in copies(step):
            copy.start()
    acc_ref[...] = start_ref[...] if last else jnp.zeros_like(acc_ref)

    def body(step, carry):
        for copy in copies(step):
            copy.wait()

        @pl.when(step + slots - 1 < steps)
        def _():
            for copy in copies(step + slots - 1):
                copy.start()

        slot = lax.rem(step, slots)
        rows = rows_ref[slot]
        for first in range(0, width, tile):
            span = slice(first, first + tile)
            acc_ref[:, span] += jnp.dot(rows, slot_ref[slot, :, span], preferred_element_type=F32)
        return carry

    lax.fori_loop(0, steps, body, 0)
    if not last:
        return
    odd = lax.rem(lax.axis_index("col"), 2)
    keep_ref[...] = acc_ref[pl.ds(pl.multiple_of(odd * half, 16), half), :]
    cols = give_refs[0].shape[1]
    for c, give_ref in enumerate(give_refs):
        span = slice(c * cols, (c + 1) * cols)
        give_ref[...] = acc_ref[pl.ds(pl.multiple_of((1 - odd) * half, 16), half), span]


def out_part(grad_train, grad_query, basis_out, prev, acc):
    tokens, depth = grad_train.shape
    width = basis_out.shape[1]
    rows = tokens + grad_query.shape[0]
    block = largest_divisor(depth, (512, 256, 128))
    steps = depth // block
    slots = min(6, steps)
    last = acc is not None
    first = steps * 2 // 7
    begin, count = (first, steps - first) if last else (0, first)
    pieces = pieces_of(width, 2)
    if last:
        out_shape = [shape_of(rows // 2, width, F32)]
        out_shape += [shape_of(rows // 2, width // pieces, F32)] * pieces
    else:
        out_shape = [shape_of(rows, width, F32)]
    return pl.pallas_call(
        functools.partial(out_kernel, begin, count, last),
        in_specs=[ANY_SPEC] * 4 + [VMEM_SPEC] * last,
        out_specs=[VMEM_SPEC] * len(out_shape),
        out_shape=out_shape,
        scratch_shapes=[
            pltpu.VMEM((slots, rows, block), BF16),
            pltpu.VMEM((slots, block, width), BF16),
        ]
        + [pltpu.VMEM((rows, width), F32)] * last
        + [pltpu.SemaphoreType.DMA((slots, 3))],
        compiler_params=pltpu.CompilerParams(vmem_limit_bytes=22 * MIB),
        cost_estimate=cost(2 * rows * block * count * width if last else 1024, 1024),
    )(
        in_hbm(grad_train), in_hbm(grad_query), in_hbm(basis_out), prev, *([acc] if last else [])
    )


def by_rows(rows, step):
    block = rows // 5 if rows % 80 == 0 else rows

    def body(i, carry):
        step(pl.ds(pl.multiple_of(i * block, block), block))
        return carry

    lax.fori_loop(0, rows // block, body, 0)


def add_kernel(pieces, outs, cast, keep_ref, *refs):
    wide_ref, narrow_refs = refs[pieces + cast + 1], refs[pieces + cast + 2 :]
    width = keep_ref.shape[1]

    def step(rows):
        total = keep_ref[rows, :]
        got = [refs[c][rows, :].astype(F32) for c in range(pieces)]
        total = total + (jnp.concatenate(got, axis=1) if pieces > 1 else got[0])
        wide_ref[rows, :] = total
        cols = width // outs
        for c in range(outs):
            narrow_refs[c][rows, :] = total[:, c * cols : (c + 1) * cols].astype(BF16)
        if cast:
            narrow_refs[outs][rows, :] = refs[pieces][rows, :].astype(BF16)

    by_rows(keep_ref.shape[0], step)


def add_part(keep, got, prev, outs=1, cast=()):
    rows, width = keep.shape
    out = pl.pallas_call(
        functools.partial(add_kernel, len(got), outs, len(cast)),
        in_specs=[VMEM_SPEC] * (1 + len(got) + len(cast)) + [ANY_SPEC],
        out_specs=[VMEM_SPEC] * (1 + outs + len(cast)),
        out_shape=[shape_of(rows, width, F32)]
        + [shape_of(rows, width // outs, BF16)] * outs
        + [shape_of(*x.shape, BF16) for x in cast],
        compiler_params=pltpu.CompilerParams(vmem_limit_bytes=12 * MIB),
        cost_estimate=cost(1024, 1024),
    )(keep, *got, *cast, prev)
    return out[0], list(out[1:])


def join_kernel(tokens, pieces, prev_ref, *refs):
    mine_refs, other_refs = refs[:pieces], refs[pieces : 2 * pieces]
    gt_ref, gq_ref = refs[2 * pieces :]
    odd = lax.rem(lax.axis_index("col"), 2)
    for c, (mine_ref, other_ref) in enumerate(zip(mine_refs, other_refs)):
        mine, other = mine_ref[...].astype(F32), other_ref[...].astype(F32)
        low = jnp.where(odd == 1, other, mine)
        high = jnp.where(odd == 1, mine, other)
        rows = jnp.concatenate([low, high], axis=0)
        cols = rows.shape[1]
        gt_ref[:, c * cols : (c + 1) * cols] = rows[:tokens].astype(BF16)
        gq_ref[c * cols : (c + 1) * cols, :] = rows[tokens:].T.astype(BF16)


def join_part(mine, other, prev, tokens):
    half = mine[0].shape[0]
    width = sum(x.shape[1] for x in mine)
    queries = 2 * half - tokens
    return pl.pallas_call(
        functools.partial(join_kernel, tokens, len(mine)),
        in_specs=[ANY_SPEC] + [VMEM_SPEC] * (2 * len(mine)),
        out_specs=[VMEM_SPEC] * 2,
        out_shape=[shape_of(tokens, width, BF16), shape_of(width, queries, BF16)],
        compiler_params=pltpu.CompilerParams(vmem_limit_bytes=12 * MIB),
        cost_estimate=cost(1024, 1024),
    )(prev, *mine, *other)


def inverse_kernel(chunks, corr_ref, prev_ref, *refs):
    *inv_refs, slot_ref, sems = refs
    slots, block = slot_ref.shape[0], slot_ref.shape[1]
    steps = corr_ref.shape[0] // block

    def fetch(step):
        slot = lax.rem(step, slots)
        rows = pl.ds(pl.multiple_of(step * block, block), block)
        return pltpu.make_async_copy(corr_ref.at[rows, :], slot_ref.at[slot], sems.at[slot])

    for step in range(min(slots, steps)):
        fetch(step).start()

    def body(step, carry):
        fetch(step).wait()
        rows = pl.ds(pl.multiple_of(step * block, block), block)
        slot = lax.rem(step, slots)
        for (first, width), inv_ref in zip(chunks, inv_refs):
            inv_ref[rows, :] = 1.0 / slot_ref[slot, :, first : first + width]

        @pl.when(step + slots < steps)
        def _():
            fetch(step + slots).start()

        return carry

    lax.fori_loop(0, steps, body, 0)


def inverse_part(correction, prev, chunks):
    rows, width = correction.shape
    block = largest_divisor(rows, (128, 64, 8))
    out = pl.pallas_call(
        functools.partial(inverse_kernel, chunks),
        in_specs=[ANY_SPEC, ANY_SPEC],
        out_specs=[VMEM_SPEC] * len(chunks),
        out_shape=[shape_of(rows, width, F32) for _, width in chunks],
        scratch_shapes=[pltpu.VMEM((4, block, width), F32), pltpu.SemaphoreType.DMA((4,))],
        compiler_params=pltpu.CompilerParams(vmem_limit_bytes=16 * MIB),
        cost_estimate=cost(1024, 1024),
    )(in_hbm(correction), prev)
    return list(out)


def at_end():
    me = lax.axis_index("row")
    return (me == 0) | (me == lax.axis_size("row") - 1)


def pay_kernel(has_part, acc_ref, got_ref, *refs):
    end = at_end()

    def step(rows):
        total = acc_ref[rows, :] + got_ref[rows, :].astype(F32)
        if has_part:
            total = jnp.where(end, refs[0][rows, :], total)
        refs[-1][rows, :] = total.astype(BF16)

    by_rows(acc_ref.shape[0], step)


def pay_part(hint, acc, got, part, prev):
    has_part = part is not None
    return pl.pallas_call(
        functools.partial(pay_kernel, has_part),
        in_specs=[VMEM_SPEC, VMEM_SPEC] + [VMEM_SPEC] * has_part + [ANY_SPEC],
        out_specs=VMEM_SPEC,
        out_shape=shape_of(*acc.shape, BF16),
        compiler_params=pltpu.CompilerParams(vmem_limit_bytes=12 * MIB),
        cost_estimate=cost(hint, 1024),
    )(acc, got, *([part] if has_part else []), prev)


def after_kernel(first_ref, second_ref, out_ref):
    out_ref[...] = jnp.zeros_like(out_ref)


def after_part(first, second):
    return pl.pallas_call(
        after_kernel,
        in_specs=[ANY_SPEC] * 2,
        out_specs=VMEM_SPEC,
        out_shape=shape_of(8, LANES, F32),
        compiler_params=pltpu.CompilerParams(vmem_limit_bytes=4 * MIB),
        cost_estimate=cost(10**9, 1024),
    )(first, second)


def score_kernel(
    start, scale, outs, gt_ref, gq_ref, inv_ref, sent_ref, got_ref, prev_ref, order_ref, *refs
):
    out_refs = refs[:outs]
    quot_ref, wide_ref, own_ref = refs[outs:]
    tokens = gt_ref.shape[0]
    queries = gq_ref.shape[1]
    width = inv_ref.shape[1]
    total = jnp.where(at_end(), got_ref[...].astype(F32), sent_ref[...].astype(F32))
    wide_ref[...] = total[:tokens]
    own_ref[...] = total[tokens:]
    owner = lax.broadcasted_iota(jnp.int32, (queries, width), 0) // LQ
    lane = lax.broadcasted_iota(jnp.int32, (tokens, LANES), 1)

    def quotient(q):
        own = jnp.where(owner == q, own_ref[...], 0.0).astype(BF16)
        products = jnp.dot(gq_ref[...], own, preferred_element_type=F32)
        quot_ref[q % 2] = (products * inv_ref[...]).astype(BF16)

    quotient(0)
    result = jnp.zeros((tokens, LANES), F32) if start else prev_ref[...]
    for q in range(NQ):
        if q + 1 < NQ:
            quotient(q + 1)
        mapped = jnp.dot(gt_ref[...], quot_ref[q % 2], preferred_element_type=F32)
        scaled = mapped * wide_ref[...]
        folded = scaled[:, :LANES]
        for part in range(1, width // LANES):
            folded = folded + scaled[:, part * LANES : (part + 1) * LANES]
        result = result + jnp.where(lane == q, jnp.sum(folded, axis=1, keepdims=True), 0.0)
    if scale is None:
        out_refs[0][...] = result
        return
    final = (result * scale).T[:NQ]
    if outs == 1:
        out_refs[0][...] = final
        return
    me = lax.axis_index("row")
    cols = final.shape[1] // outs
    for step, out_ref in enumerate(out_refs):
        block = final[:, :cols]
        for other in range(1, outs):
            own = final[:, other * cols : (other + 1) * cols]
            block = jnp.where(jnp.bitwise_xor(me, step) == other, own, block)
        out_ref[...] = block


def score_part(rot_gt, rot_gq_t, inv, sent, got, prev, order, start, scale, halves):
    tokens, outs = rot_gt.shape
    width = inv.shape[1]
    queries = rot_gq_t.shape[1]
    if scale is None:
        out_shape = [shape_of(tokens, LANES, F32)]
    elif halves:
        out_shape = [shape_of(NQ, tokens // halves, F32)] * halves
    else:
        out_shape = [shape_of(NQ, tokens, F32)]
    return pl.pallas_call(
        functools.partial(score_kernel, start, scale, len(out_shape)),
        in_specs=[VMEM_SPEC] * 5 + [ANY_SPEC if start else VMEM_SPEC, ANY_SPEC],
        out_specs=[VMEM_SPEC] * len(out_shape),
        out_shape=out_shape,
        scratch_shapes=[
            pltpu.VMEM((2, outs, width), BF16),
            pltpu.VMEM((tokens, width), F32),
            pltpu.VMEM((queries, width), F32),
        ],
        compiler_params=pltpu.CompilerParams(vmem_limit_bytes=16 * MIB),
        cost_estimate=cost(1024, 1024),
    )(rot_gt, rot_gq_t, inv, sent, got, prev, order)


def gather_kernel(*refs):
    total = refs[0][...]
    for ref in refs[1:-1]:
        total = total + ref[...]
    refs[-1][...] = total


def gather_part(arrays):
    return pl.pallas_call(
        gather_kernel,
        in_specs=[VMEM_SPEC] * len(arrays),
        out_specs=VMEM_SPEC,
        out_shape=shape_of(*arrays[0].shape, F32),
        compiler_params=pltpu.CompilerParams(vmem_limit_bytes=4 * MIB),
        cost_estimate=cost(1024, 1024),
    )(*arrays)


def line_sum(partial, axis):
    n = lax.axis_size(axis)
    half = n // 2
    me = lax.axis_index(axis)
    if n % 2:
        return lax.psum(partial, axis).astype(BF16)
    acc = partial
    for s in range(half - 1):
        pairs = [(s, s + 1), (n - 1 - s, n - 2 - s)]
        acc = acc + lax.ppermute(acc.astype(BF16), axis, pairs).astype(F32)
    got = lax.ppermute(acc.astype(BF16), axis, [(half - 1, half), (half, half - 1)])
    total = (acc + got.astype(F32)).astype(BF16)
    for s in range(half - 2, -1, -1):
        pairs = [(s + 1, s), (n - 2 - s, n - 1 - s)]
        got = lax.ppermute(total, axis, pairs)
        total = jnp.where((me == s) | (me == n - 1 - s), got, total)
    return total


def owned_sum(partial, axis):
    n = lax.axis_size(axis)
    me = lax.axis_index(axis)
    total = lax.dynamic_index_in_dim(partial, me, 0, keepdims=False)
    for step in range(1, n):
        block = lax.dynamic_index_in_dim(partial, (me + step) % n, 0, keepdims=False)
        total = total + lax.ppermute(block, axis, [(d, (d + step) % n) for d in range(n)])
    return total


def shared_sum(partial, axis):
    n = lax.axis_size(axis)
    total = partial
    for step in range(1, n):
        total = total + lax.ppermute(partial, axis, [(d, (d + step) % n) for d in range(n)])
    return total


def on_device(act_train, act_query, grad_train, grad_query, basis_in, basis_out, correction):
    norm_scale = (O * I * LQ) ** (-0.5)
    tokens = act_train.shape[0]
    n_row, n_col = lax.axis_size("row"), lax.axis_size("col")
    chunks = chunk_list(basis_in.shape[1])
    count = len(chunks)
    line = n_row == 4
    flip = [(d, d ^ 1) for d in range(n_col)]
    outer = [(0, 1), (1, 0), (2, 3), (3, 2)]
    inner = []
    for c in range(n_col):
        inner += [(n_col + c, 2 * n_col + c), (2 * n_col + c, n_col + c)]
        inner += [(c, c ^ 1), (3 * n_col + c, 3 * n_col + (c ^ 1))]
    sent, got, acc, got_mid = {}, {}, {}, {}

    def swap(j, payload):
        sent[j] = payload
        got[j] = lax.ppermute(payload, "row", outer)

    def meet(j, prev):
        if not line or j >= count:
            return prev
        cast = [parts[2]] if j == 0 else []
        acc[j], thin = add_part(parts[j], [got[j]], prev, 1, cast)
        got_mid[j] = lax.ppermute(thin[0], ("row", "col"), inner)
        if cast:
            swap(2, thin[1])
        return thin[0]

    def pay(j, prev):
        if not line:
            sent[j + LAG] = got[j + LAG] = line_sum(parts[j], "row")
            return prev
        part = parts[j + LAG] if j + LAG < count else None
        payload = pay_part(4 * 10**9 if j == 0 else 1024, acc[j], got_mid[j], part, prev)
        swap(j + LAG, payload)
        return payload

    def score(k, sums, prev):
        return score_part(
            rot_gt, rot_gq_t, invs[k], sent[k + LAG], got[k + LAG], sums[0], prev,
            k == 0, norm_scale if k == count - 1 else None, halves,
        )

    early = min(LAG + 1, count)
    widths = [width for _, width in chunks]
    parts, narrow = in_part(
        act_train, act_query, basis_in, act_query, chunks[:1], [widths[0]]
    )
    if line:
        swap(0, narrow[0])
    more, narrow = in_part(
        act_train, act_query, basis_in, parts[0], chunks[1:early], [widths[1]]
    )
    parts += more
    if line:
        swap(1, narrow[0])
    (half_sum,) = out_part(grad_train, grad_query, basis_out, parts[-1], None)
    prev = meet(0, half_sum)
    keep, *give = out_part(grad_train, grad_query, basis_out, prev, half_sum)
    given = [lax.ppermute(piece, "col", flip) for piece in give]
    prev = meet(1, keep)
    if line:
        prev = after_part(prev, got[2])
    prev = meet(2, pay(0, prev))
    outs = pieces_of(keep.shape[1], 2)
    wide, thin = add_part(keep, given, prev, outs)
    prev, bit = wide, 2
    while bit < n_col:
        other = [lax.ppermute(x, "col", [(d, d ^ bit) for d in range(n_col)]) for x in thin]
        if bit == 2:
            more, _ = in_part(act_train, act_query, basis_in, prev, chunks[early:], [])
            parts += more
            prev = meet(3, pay(1, more[-1]))
            invs = inverse_part(correction, prev, chunks)
            prev = pay(2, invs[0])
        wide, thin = add_part(wide, other, prev, outs)
        prev = wide
        bit *= 2
    other = [lax.ppermute(x, "col", flip) for x in thin]
    prev = meet(5, pay(3, meet(4, prev)))
    rot_gt, rot_gq_t = join_part(thin, other, prev, tokens)
    prev = rot_gt
    halves = n_row if n_row == 4 and n_col == 4 and tokens % (n_row * LANES) == 0 else 0
    sums = score(0, [rot_gt], prev)
    done = 1
    for j in range(6, count + 1):
        prev = meet(j, pay(j - 2, sums[0]))
        sums = score(done, sums, prev)
        done += 1
    if line:
        prev = after_part(sums[0], got[count])
    prev = pay(count - 1, prev)
    for k in range(done, count):
        sums = score(k, sums, prev)
    if not halves:
        blocks = sums[0].reshape(NQ, n_row, tokens // n_row).transpose(1, 0, 2)
        return shared_sum(owned_sum(blocks, "row"), "col")
    moved = [
        lax.ppermute(sums[step], "row", [(d, d ^ step) for d in range(n_row)])
        for step in range(1, n_row)
    ]
    owned = gather_part([sums[0]] + moved)
    moved = [
        lax.ppermute(owned, "col", [(d, d ^ step) for d in range(n_col)]) for step in range(1, n_col)
    ]
    return gather_part([owned] + moved)


def solution(mesh):
    in_specs = (
        P("groups", "row"),
        P("groups", "row"),
        P("groups", "col"),
        P("groups", "col"),
        P(("groups", "row"), "col"),
        P(("groups", "col"), "row"),
        P(("groups", "row"), "col"),
    )
    out_specs = P("groups", "row")
    return jax.shard_map(
        on_device, mesh=mesh, in_specs=in_specs, out_specs=out_specs, check_vma=False
    )
```
